32 devices in a mesh: dp: 8 (over z, y), tensor: 4 (over x, core).
Axes of the slice: x: 2, y: 2, z: 4, core: 2. Of those that a mesh axis runs over, the one named last changes fastest.
Arguments:
- tokens: bfloat16 [16384, 768], P(('dp', 'tensor')), may hold values from -6 to 6
- doc_lengths: int32 [8, 2], P('dp'), may hold values from 0 to 2048, as said below
- w_qkv: bfloat16 [768, 2304], P(None, 'tensor'), may hold values from -0.21875 to 0.21875
- b_qkv: bfloat16 [2304], P('tensor'), may hold values from -1.5 to 1.5
- w_out: bfloat16 [768, 768], P('tensor'), may hold values from -3.5 to 3.5
- w_up: bfloat16 [768, 3072], P(None, 'tensor'), may hold values from -0.21875 to 0.21875
- b_up: bfloat16 [3072], P('tensor'), may hold values from -1.5 to 1.5
- w_down: bfloat16 [3072, 768], P('tensor'), may hold values from -0.109375 to 0.109375
- out_bias: bfloat16 [768], replicated, may hold values from -1.5 to 1.5
- norm1_gain: bfloat16 [768], replicated, may hold values from 0.5 to 1.5
- norm1_shift: bfloat16 [768], replicated, may hold values from -1.5 to 1.5
- norm2_gain: bfloat16 [768], replicated, may hold values from 0.5 to 1.5
- norm2_shift: bfloat16 [768], replicated, may hold values from -1.5 to 1.5
- cotangent: bfloat16 [16384, 768], P(('dp', 'tensor')), may hold values from -6 to 6
Outputs:
- block_out: bfloat16 [16384, 768], P(('dp', 'tensor'))
- grad_input: float32 [16384, 768], P(('dp', 'tensor'))
- grad_qkv: float32 [768, 2304], P(None, 'tensor')
- grad_qkv_bias: float32 [2304], P('tensor')
- grad_out: float32 [768, 768], P('tensor')
- grad_up: float32 [768, 3072], P(None, 'tensor')
- grad_up_bias: float32 [3072], P('tensor')
- grad_down: float32 [3072, 768], P('tensor')
- grad_vectors: float32 [5, 768], P(None, 'tensor')
The draws below stay inside these ranges and needn't reach their ends.
Inputs may be any that keep to these rules, and one draw needn't show every extreme that they name: `doc_lengths`: row g holds the lengths of the sequences of group g, laid one after another from the group's first row, each starting at a multiple of 128 rows. The first length of a row is 1024 or more; a zero marks an empty slot and is followed only by zeros; each length rounded up to a multiple of 128 and summed over a row gives at most 2048. In every draw some sequence has exactly 2048 tokens.
All inputs are finite; a program needn't handle non-finite values.
Results may differ from the reference program's by a relative error of at most 0.012.
Values may be sent and summed in bfloat16 or wider, within the bound.
No kernel may reach another device: no remote copies, remote signals or barrier semaphores. Data moves between devices by JAX's collectives and lax.ppermute only.
A program may use at most 192 MiB of HBM per device.

```python
import jax
import jax.numpy as jnp
from jax import lax

HEADS = 12
HDIM = 64
D = 768
FF = 3072
ROT = 16
TOK_DEV = 512
TOKENS = 16384
MAX_LEN = 2048
PADB = 128
QBLK = 256
N_DP = 8
N_TENSOR = 4


def draw_doc_lengths(key, part):
    key = jax.random.fold_in(key, 7)
    group_tok = TOK_DEV * N_TENSOR
    slot_count = 2 * group_tok // MAX_LEN
    keys = jax.random.split(key, 3)
    firsts = jax.random.randint(keys[0], (N_DP,), MAX_LEN // 2, MAX_LEN + 1)
    chosen = jax.random.randint(keys[1], (), 0, N_DP)
    firsts = jnp.where(jnp.arange(N_DP) == chosen, MAX_LEN, firsts)
    others = jax.random.randint(keys[2], (N_DP, slot_count), 1, MAX_LEN + 1)
    used = (firsts + PADB - 1) // PADB * PADB
    columns = [firsts]
    for slot in range(1, slot_count):
        room = group_tok - used
        length = jnp.minimum(others[:, slot], room)
        columns.append(length)
        used = used + (length + PADB - 1) // PADB * PADB
    return jnp.stack(columns, axis=1).astype(jnp.int32)


def levels(key, dims, cuts, low, top_value):
    def one(axis_at, parts):
        heights = jax.random.uniform(jax.random.fold_in(jax.random.fold_in(key, 6), axis_at), (parts,), jnp.float32, low / len(cuts), top_value / len(cuts))
        return jnp.repeat(jnp.exp(heights), dims[axis_at] // parts).reshape((-1,) + (1,) * (len(dims) - axis_at - 1))

    level = one(*cuts[0])
    for cut in cuts[1:]:
        level = level * one(*cut)
    return level


def noise(key, dims, scale, reach, cuts=(), kind=jnp.bfloat16):
    entries = jax.random.normal(key, dims, jnp.float32) * scale
    if len(cuts) > 0:
        entries = levels(key, dims, cuts, -0.22, 0.18) * entries
    return jnp.clip(entries, min=-reach, max=reach).astype(kind)


def setup_inputs(seed: int = 0) -> dict:
    seeds = jax.random.split(jax.random.key(seed), 15)
    return {
        "tokens": noise(seeds[0], (TOKENS, D), 1.0, 6.0, ((0, 32),)),
        "doc_lengths": draw_doc_lengths(jax.random.fold_in(seeds[14], 71), 0),
        "w_qkv": noise(seeds[2], (D, 3 * D), D ** -0.5, 0.21875, ((1, 4),)),
        "b_qkv": noise(seeds[3], (3 * D,), 0.3, 1.5, ((0, 4),)),
        "w_out": noise(seeds[4], (D, D), (max(D // 256, 2)) ** -0.5, 3.5, ((0, 4),)),
        "w_up": noise(seeds[5], (D, FF), D ** -0.5, 0.21875, ((1, 4),)),
        "b_up": noise(seeds[6], (FF,), 0.3, 1.5, ((0, 4),)),
        "w_down": noise(seeds[7], (FF, D), FF ** -0.5, 0.109375, ((0, 4),)),
        "out_bias": noise(seeds[8], (D,), 0.3, 1.5),
        "norm1_gain": jnp.clip(1.0 + 0.1 * jax.random.normal(seeds[9], (D,), jnp.float32), 0.5, 1.5).astype(jnp.bfloat16),
        "norm1_shift": noise(seeds[10], (D,), 0.3, 1.5),
        "norm2_gain": jnp.clip(1.0 + 0.1 * jax.random.normal(seeds[11], (D,), jnp.float32), 0.5, 1.5).astype(jnp.bfloat16),
        "norm2_shift": noise(seeds[12], (D,), 0.3, 1.5),
        "cotangent": noise(seeds[13], (TOKENS, D), 1.0, 6.0, ((0, 32),)),
    }


norm_eps = 1e-05
masked_fill = -1e+30
rotary_base = 10000.0
HIGHEST = lax.Precision.HIGHEST

@jax.custom_vjp
def low(v):
    return lax.optimization_barrier(v.astype(jnp.bfloat16)).astype(jnp.float32)

@jax.custom_vjp
def low_back(v):
    return v

def low_keep(v):
    return (low(v), None)

def low_pass(kept, grad):
    return (grad,)

def back_keep(v):
    return (v, None)

def back_low(kept, grad):
    return (low(grad),)
low.defvjp(low_keep, low_pass)
low_back.defvjp(back_keep, back_low)

def layer_norm(values, gain, shift):
    center = lax.optimization_barrier(jnp.mean(values, axis=-1, keepdims=True))
    offsets = values - center
    spread = lax.optimization_barrier(jnp.mean(offsets * offsets, axis=-1, keepdims=True))
    return offsets * lax.rsqrt(spread + norm_eps) * gain + shift

def rotary_tables(positions):
    half_dims = ROT // 2
    inverse = rotary_base ** (-(jnp.arange(half_dims, dtype=jnp.float32) * 2.0 / ROT))
    angles = positions.astype(jnp.float32)[:, None] * inverse[None, :]
    return (jnp.cos(angles), jnp.sin(angles))

def rotate(heads_in, cosine, sine):
    half_dims = cosine.shape[-1]
    first_half = heads_in[..., :half_dims]
    second_half = heads_in[..., half_dims:2 * half_dims]
    remainder = heads_in[..., 2 * half_dims:]
    cos_rows = cosine[:, None, :]
    sin_rows = sine[:, None, :]
    return jnp.concatenate([first_half * cos_rows - second_half * sin_rows, second_half * cos_rows + first_half * sin_rows, remainder], axis=-1)

def token_layout(lengths, total):
    padded = (lengths + PADB - 1) // PADB * PADB
    starts = (jnp.cumsum(padded) - padded).astype(jnp.int32)
    row_ids = jnp.arange(total, dtype=jnp.int32)
    inside = (row_ids[None, :] >= starts[:, None]) & (row_ids[None, :] < (starts + lengths)[:, None])
    slot_ids = jnp.arange(lengths.shape[0], dtype=jnp.int32)
    documents = lax.optimization_barrier(jnp.sum(jnp.where(inside, slot_ids[:, None] + 1, 0), axis=0)).astype(jnp.int32) - 1
    offsets = lax.optimization_barrier(jnp.sum(jnp.where(inside, starts[:, None], 0), axis=0)).astype(jnp.int32)
    return (documents, row_ids - offsets)

def group_forward(params, inputs, documents, positions):
    w_qkv, b_qkv, w_out, w_up, b_up, w_down, out_bias, gain_one, shift_one, gain_two, shift_two = params
    total = inputs.shape[0]
    scale = HDIM ** (-0.5)
    normed_attn = low(layer_norm(inputs, gain_one, shift_one))
    normed_mlp = low(layer_norm(inputs, gain_two, shift_two))
    qkv = low_back(jnp.dot(normed_attn, w_qkv, precision=HIGHEST)) + b_qkv
    qkv = qkv.reshape(total, HEADS, 3, HDIM)
    cosine, sine = rotary_tables(positions)
    query = low(rotate(qkv[:, :, 0], cosine, sine))
    keys_all = low(rotate(qkv[:, :, 1], cosine, sine))
    values_all = low(qkv[:, :, 2])
    key_ids = jnp.arange(total, dtype=jnp.int32)
    block_count = total // QBLK

    def attend(items):
        query_block, doc_block, opening = items
        row_ids = opening + jnp.arange(QBLK, dtype=jnp.int32)
        scores = jnp.einsum('qhd,khd->hqk', query_block, keys_all, precision=HIGHEST) * scale
        scores = low_back(scores)
        allowed = (doc_block[:, None] == documents[None, :]) & (key_ids[None, :] <= row_ids[:, None])
        masked = jnp.where(allowed[None], scores, masked_fill)
        row_peak = lax.optimization_barrier(jnp.max(masked, axis=-1, keepdims=True))
        expo = jnp.exp(masked - row_peak)
        probs = low(expo / lax.optimization_barrier(jnp.sum(expo, axis=-1, keepdims=True)))
        return jnp.einsum('hqk,khd->qhd', probs, values_all, precision=HIGHEST)
    block_starts = jnp.arange(block_count, dtype=jnp.int32) * QBLK
    contexts = lax.map(jax.checkpoint(attend), (query.reshape(block_count, QBLK, HEADS, HDIM), documents.reshape(block_count, QBLK), block_starts))
    context = low(low_back(contexts.reshape(total, HEADS * HDIM)))
    attn_part = jnp.dot(context, w_out, precision=HIGHEST)
    hidden = low_back(jnp.dot(normed_mlp, w_up, precision=HIGHEST)) + b_up
    act = low(jax.nn.gelu(hidden, approximate=False))
    mlp_part = jnp.dot(act, w_down, precision=HIGHEST)
    return inputs + out_bias + attn_part + mlp_part

def reference(tokens, doc_lengths, w_qkv, b_qkv, w_out, w_up, b_up, w_down, out_bias, norm1_gain, norm1_shift, norm2_gain, norm2_shift, cotangent):
    params = tuple((item.astype(jnp.float32) for item in (w_qkv, b_qkv, w_out, w_up, b_up, w_down, out_bias, norm1_gain, norm1_shift, norm2_gain, norm2_shift)))
    group_tok = tokens.shape[0] // N_DP
    width = tokens.shape[1]
    rows_all = tokens.astype(jnp.float32).reshape(N_DP, group_tok, width)
    grads_all = cotangent.astype(jnp.float32).reshape(N_DP, group_tok, width)

    def one_group(carry, items):
        inputs, grad_rows, lengths = items
        documents, positions = token_layout(lengths, group_tok)
        grad_rows = grad_rows * (documents >= 0).astype(jnp.float32)[:, None]
        output, pullback = jax.vjp(lambda weights, rows: group_forward(weights, rows, documents, positions), params, inputs)
        grad_params, grad_inputs = pullback(grad_rows)
        carry = jax.tree.map(jnp.add, carry, grad_params)
        return (carry, (output.astype(jnp.bfloat16), grad_inputs))
    zeros = jax.tree.map(jnp.zeros_like, params)
    totals, (outputs, grad_inputs) = lax.scan(one_group, zeros, (rows_all, grads_all, doc_lengths))
    grad_vectors = jnp.stack([totals[6], totals[7], totals[8], totals[9], totals[10]])
    return (outputs.reshape(tokens.shape), grad_inputs.reshape(tokens.shape), totals[0], totals[1], totals[2], totals[3], totals[4], totals[5], grad_vectors)
```

```python
import functools

import jax
import jax.numpy as jnp
from jax import lax
from jax.experimental import pallas as pl
from jax.experimental.pallas import tpu as pltpu
from jax.sharding import PartitionSpec as P

HDIM = 64
ROT = 16
PADB = 128
LANES = 128
QB = 256

norm_eps = 1e-05
masked_fill = -1e30
rotary_base = 10000.0
f32 = jnp.float32
bf16 = jnp.bfloat16


def swap(values, axis, bit):
    n = lax.axis_size(axis)
    return lax.ppermute(values, axis, [(i, i ^ bit) for i in range(n)])


def gather_rows(values, axis):
    n = lax.axis_size(axis)
    me = lax.axis_index(axis)
    rows = values.shape[0]
    blocks = {0: values}
    bit = n // 2
    while bit:
        for at in list(blocks):
            blocks[at | bit] = swap(blocks[at], axis, bit)
        bit //= 2
    out = jnp.zeros((n * rows,) + values.shape[1:], values.dtype)
    for at in sorted(blocks):
        out = lax.dynamic_update_slice_in_dim(out, blocks[at], (me ^ at) * rows, 0)
    return out


def halves(values, axis, bit):
    side = (lax.axis_index(axis) // bit) % 2
    keep = lax.dynamic_index_in_dim(values, side, 0, keepdims=False)
    give = lax.dynamic_index_in_dim(values, 1 - side, 0, keepdims=False)
    return keep, give


def scatter_sum_rows(values, axis):
    n = lax.axis_size(axis)
    rows = values.shape[0] // n
    tail = values.shape[1:]
    out = values.reshape((n, rows) + tail)
    bit = 1
    while bit < n:
        left = out.shape[0] // 2
        out = out.reshape((left, 2, rows) + tail).swapaxes(0, 1)
        keep, give = halves(out, axis, bit)
        got = swap(give.astype(bf16), axis, bit)
        out = keep.astype(f32) + got.astype(f32)
        bit *= 2
    return out.reshape((rows,) + tail)


def all_sum_rows(values, axis):
    n = lax.axis_size(axis)
    out = values.astype(bf16)
    bit = 1
    while bit < n:
        out = out.reshape((2, out.shape[0] // 2) + out.shape[1:])
        keep, give = halves(out, axis, bit)
        got = swap(give, axis, bit)
        out = (keep.astype(f32) + got.astype(f32)).astype(bf16)
        bit *= 2
    while bit > 1:
        bit //= 2
        got = swap(out, axis, bit)
        side = (lax.axis_index(axis) // bit) % 2
        low = jnp.where(side == 0, out, got)
        high = jnp.where(side == 0, got, out)
        out = jnp.concatenate([low, high], axis=0)
    return out


def all_sum_small(values, axis):
    n = lax.axis_size(axis)
    bit = 1
    while bit < n:
        values = values + swap(values, axis, bit)
        bit *= 2
    return values


def token_layout(lengths, total, pad_block):
    padded = (lengths + pad_block - 1) // pad_block * pad_block
    starts = jnp.cumsum(padded) - padded
    row_ids = jnp.arange(total, dtype=jnp.int32)
    inside = (row_ids[None, :] >= starts[:, None]) & (
        row_ids[None, :] < (starts + lengths)[:, None]
    )
    slot_ids = jnp.arange(lengths.shape[0], dtype=jnp.int32)
    documents = jnp.sum(jnp.where(inside, slot_ids[:, None] + 1, 0), axis=0) - 1
    offsets = jnp.sum(jnp.where(inside, starts[:, None], 0), axis=0)
    return (documents, row_ids - offsets)


def rotary_lanes(positions):
    half = ROT // 2
    lane = jnp.arange(LANES, dtype=jnp.int32)
    inverse = rotary_base ** (-((lane % half).astype(f32) * 2.0 / ROT))
    angles = positions.astype(f32)[:, None] * inverse[None, :]
    cosine = jnp.where(lane < ROT, jnp.cos(angles), 1.0)
    sine = jnp.sin(angles)
    sine_up = jnp.where(lane < half, sine, 0.0)
    sine_down = jnp.where((lane >= half) & (lane < ROT), sine, 0.0)
    return cosine, sine_up, sine_down


def doc_lanes(documents, slots):
    lane = jnp.arange(LANES, dtype=jnp.int32) - HDIM
    used = (lane >= 0) & (lane <= slots)
    hit = (documents[:, None] + 1) == lane[None, :]
    key_side = jnp.where(used & hit, 1.0, 0.0).astype(bf16)
    query_side = jnp.where(used & ~hit, masked_fill, 0.0).astype(bf16)
    return query_side, key_side


def dot(left, right):
    return lax.dot_general(left, right, (((1,), (0,)), ((), ())), preferred_element_type=f32)


def front_kernel(
    heads, x_ref, w_ref, b_ref, vec_ref, cos_ref, up_ref, down_ref, eq_ref, ek_ref,
    na_ref, nb_ref, qkv_ref,
):
    x = x_ref[...].astype(f32)
    center = jnp.mean(x, axis=-1, keepdims=True)
    off = x - center
    xhat = off * lax.rsqrt(jnp.mean(off * off, axis=-1, keepdims=True) + norm_eps)
    normed = (xhat * vec_ref[0:1, :] + vec_ref[1:2, :]).astype(bf16)
    na_ref[...] = normed
    nb_ref[...] = (xhat * vec_ref[2:3, :] + vec_ref[3:4, :]).astype(bf16)
    half = ROT // 2
    for h in range(heads):
        cols = pl.ds(h * 3 * LANES, 3 * LANES)
        proj = dot(normed, w_ref[:, cols]) + b_ref[:, cols]
        for part in range(2):
            a = proj[:, part * LANES : (part + 1) * LANES]
            a = (
                a * cos_ref[...]
                - pltpu.roll(a, LANES - half, 1) * up_ref[...]
                + pltpu.roll(a, half, 1) * down_ref[...]
            )
            if part == 0:
                a = (a * HDIM**-0.5).astype(bf16) + eq_ref[...]
            else:
                a = a.astype(bf16) + ek_ref[...]
            qkv_ref[:, pl.ds((h * 3 + part) * LANES, LANES)] = a
        qkv_ref[:, pl.ds((h * 3 + 2) * LANES, LANES)] = proj[:, 2 * LANES :].astype(bf16)


def front(x, w_ext, b_ext, vectors, tables, heads):
    rows, width = x.shape
    tile = 512
    wide = w_ext.shape[1]
    row_block = lambda w: pl.BlockSpec((tile, w), lambda r: (r, 0))
    whole = lambda a: pl.BlockSpec(a.shape, lambda r: (0, 0))
    return pl.pallas_call(
        functools.partial(front_kernel, heads),
        grid=(rows // tile,),
        in_specs=[row_block(width), whole(w_ext), whole(b_ext), whole(vectors)]
        + [row_block(LANES)] * 5,
        out_specs=[row_block(width), row_block(width), row_block(wide)],
        out_shape=[
            jax.ShapeDtypeStruct((rows, width), bf16),
            jax.ShapeDtypeStruct((rows, width), bf16),
            jax.ShapeDtypeStruct((rows, wide), bf16),
        ],
        compiler_params=pltpu.CompilerParams(vmem_limit_bytes=48 * 2**20),
        cost_estimate=pl.CostEstimate(
            flops=2 * rows * width * wide, bytes_accessed=rows * 8000, transcendentals=0
        ),
        name="front",
    )(x, w_ext, b_ext, vectors, *tables)


def attention_kernel(
    q_ref, k_ref, v_ref, g_ref, cos_ref, up_ref, down_ref,
    ctx_ref, proj_ref, bias_ref,
    kt_ref, vt_ref, s_ref, e_ref, d_ref, dk_ref, dv_ref,
):
    total = q_ref.shape[0]
    half = ROT // 2
    kt_ref[...] = k_ref[...].T
    vt_ref[...] = v_ref[...].T
    row_at = lax.broadcasted_iota(jnp.int32, (QB, QB), 0)
    col_at = lax.broadcasted_iota(jnp.int32, (QB, QB), 1)
    causal = row_at <= col_at
    feature = lax.broadcasted_iota(jnp.int32, (LANES, QB), 0)
    lane = lax.broadcasted_iota(jnp.int32, (QB, LANES), 1)
    bias_q = jnp.zeros((1, LANES), f32)

    def unrotate(a, at):
        return (
            a * cos_ref[at, :]
            + pltpu.roll(a, LANES - half, 1) * up_ref[at, :]
            - pltpu.roll(a, half, 1) * down_ref[at, :]
        )

    for i in range(total // QB):
        here = pl.ds(i * QB, QB)
        reach = (i + 1) * QB
        qt = q_ref[here, :].T
        gt = g_ref[here, :].T.astype(f32)
        top = None
        for j in range(i + 1):
            at = pl.ds(j * QB, QB)
            s = dot(k_ref[at, :], qt)
            if j == i:
                s = jnp.where(causal, s, masked_fill)
            s_ref[at, :] = s
            part = jnp.max(s.reshape(QB // 8, 8, QB), axis=0)
            top = part if top is None else jnp.maximum(top, part)
        top = jnp.max(top, axis=0, keepdims=True)
        for j in range(i + 1):
            at = pl.ds(j * QB, QB)
            e_ref[at, :] = jnp.exp(s_ref[at, :] - top).astype(bf16)
        ct = dot(vt_ref[:, :reach], e_ref[:reach, :])
        inv = 1.0 / ct[HDIM : HDIM + 1, :]
        ct = jnp.where(feature < HDIM, ct * inv, 0.0)
        ctx_ref[here, :] = ct.T.astype(bf16)
        less = -jnp.sum(gt * ct, axis=0, keepdims=True)
        less_hi = less.astype(bf16).astype(f32)
        ge = jnp.where(feature == HDIM, less_hi, gt)
        ge = jnp.where(feature == HDIM + 1, less - less_hi, ge).astype(bf16)
        gl = (gt * inv).T.astype(bf16)
        ql = jnp.where(feature < HDIM, qt.astype(f32) * inv, 0.0).T.astype(bf16)
        for j in range(i + 1):
            at = pl.ds(j * QB, QB)
            e = e_ref[at, :]
            d = (e.astype(f32) * dot(v_ref[at, :], ge)).astype(bf16)
            d_ref[at, :] = d
            dv = dot(e, gl)
            dk = dot(d, ql)
            if j == i:
                dv_ref[at, :] = dv
                dk_ref[at, :] = dk
            else:
                dv_ref[at, :] += dv
                dk_ref[at, :] += dk
        dqt = dot(kt_ref[:, :reach], d_ref[:reach, :]) * (inv * HDIM**-0.5)
        dq = unrotate(jnp.where(feature < HDIM, dqt, 0.0).T, here)
        bias_q += jnp.sum(dq, axis=0, keepdims=True)
        proj_ref[here, :HDIM] = dq[:, :HDIM].astype(bf16)
    bias_k = jnp.zeros((1, LANES), f32)
    bias_v = jnp.zeros((1, LANES), f32)
    for i in range(total // QB):
        here = pl.ds(i * QB, QB)
        dk = unrotate(dk_ref[here, :], here)
        dv = dv_ref[here, :]
        bias_k += jnp.sum(dk, axis=0, keepdims=True)
        bias_v += jnp.sum(dv, axis=0, keepdims=True)
        proj_ref[here, HDIM : 2 * HDIM] = dk[:, :HDIM].astype(bf16)
        proj_ref[here, 2 * HDIM :] = dv[:, :HDIM].astype(bf16)
    bias_ref[...] = jnp.concatenate([bias_q, bias_k, bias_v], axis=1)


def attention(qkv, grad_ctx, tables, head):
    total = qkv.shape[0]
    pick = lambda c: pl.BlockSpec((total, LANES), lambda r, c=c: (0, c))
    whole = lambda r, w: pl.BlockSpec((r, w), lambda r: (0, 0))
    pairs = (total // QB) * (total // QB + 1) // 2
    return pl.pallas_call(
        attention_kernel,
        grid=(1,),
        in_specs=[pick(head * 3), pick(head * 3 + 1), pick(head * 3 + 2), pick(head)]
        + [whole(total, LANES)] * 3,
        out_specs=[whole(total, LANES), whole(total, 3 * HDIM), whole(1, 3 * LANES)],
        out_shape=[
            jax.ShapeDtypeStruct((total, LANES), bf16),
            jax.ShapeDtypeStruct((total, 3 * HDIM), bf16),
            jax.ShapeDtypeStruct((1, 3 * LANES), f32),
        ],
        scratch_shapes=[
            pltpu.VMEM((LANES, total), bf16),
            pltpu.VMEM((LANES, total), bf16),
            pltpu.VMEM((total, QB), f32),
            pltpu.VMEM((total, QB), bf16),
            pltpu.VMEM((total, QB), bf16),
            pltpu.VMEM((total, LANES), f32),
            pltpu.VMEM((total, LANES), f32),
        ],
        compiler_params=pltpu.CompilerParams(vmem_limit_bytes=48 * 2**20),
        cost_estimate=pl.CostEstimate(
            flops=pairs * 6 * 2 * QB**3, bytes_accessed=total * 5000, transcendentals=0
        ),
        name="attention",
    )(qkv, qkv, qkv, grad_ctx, *tables)


def times_trans(left, right):
    return lax.dot_general(
        left, right, (((1,), (1,)), ((), ())), preferred_element_type=f32
    )


def trans_times(left, right):
    return lax.dot_general(
        left, right, (((0,), (0,)), ((), ())), preferred_element_type=f32
    )


def exact_gelu(values):
    return jax.nn.gelu(values, approximate=False)


def body(
    tokens,
    doc_lengths,
    w_qkv,
    b_qkv,
    w_out,
    w_up,
    b_up,
    w_down,
    out_bias,
    norm1_gain,
    norm1_shift,
    norm2_gain,
    norm2_shift,
    cotangent,
):
    row_count, width = tokens.shape
    n_tensor = lax.axis_size("tensor")
    group_tok = row_count * n_tensor
    first_row = lax.axis_index("tensor") * row_count
    heads = w_out.shape[0] // HDIM
    documents, positions = token_layout(doc_lengths[0], group_tok, PADB)
    local_docs = lax.dynamic_slice_in_dim(documents, first_row, row_count)
    grad_send = jnp.where(local_docs[:, None] >= 0, cotangent, 0)

    x_all = gather_rows(tokens, "tensor")
    piece = gather_rows(grad_send, "tensor")

    rotary = rotary_lanes(positions)
    docs = doc_lanes(documents, doc_lengths.shape[1])
    w_ext = jnp.pad(
        w_qkv.reshape(width, heads * 3, HDIM), ((0, 0), (0, 0), (0, LANES - HDIM))
    ).reshape(width, heads * 3 * LANES)
    ones = (jnp.arange(LANES - HDIM) < 2).astype(f32)
    b_ext = jnp.concatenate(
        [
            b_qkv.astype(f32).reshape(heads, 3, HDIM),
            jnp.stack([0 * ones, 0 * ones, ones])[None].repeat(heads, 0),
        ],
        axis=2,
    ).reshape(1, heads * 3 * LANES)
    w_out_ext = jnp.pad(
        w_out.reshape(heads, HDIM, width), ((0, 0), (0, LANES - HDIM), (0, 0))
    ).reshape(heads * LANES, width)
    vectors = jnp.stack([norm1_gain, norm1_shift, norm2_gain, norm2_shift]).astype(f32)

    normed_a, normed_b, qkv = front(x_all, w_ext, b_ext, vectors, rotary + docs, heads)

    hidden = jnp.dot(normed_b, w_up, preferred_element_type=f32) + b_up.astype(f32)
    act_f, gelu_pull = jax.vjp(exact_gelu, hidden)
    act = act_f.astype(bf16)
    grad_hidden = gelu_pull(times_trans(piece, w_down))[0]
    grad_up_bias = jnp.sum(grad_hidden, axis=0)
    grad_hidden = grad_hidden.astype(bf16)
    grad_down = trans_times(act, piece)
    grad_up = trans_times(normed_b, grad_hidden)
    mlp_sum = all_sum_rows(
        jnp.concatenate([grad_up.astype(bf16), grad_down.astype(bf16)], axis=0), "dp"
    )
    grad_ctx = times_trans(piece, w_out_ext).astype(bf16)
    back_mlp = times_trans(grad_hidden, w_up)

    done = [attention(qkv, grad_ctx, rotary, h) for h in range(heads)]
    context = jnp.concatenate([d[0] for d in done], axis=1)
    proj = jnp.concatenate([d[1] for d in done], axis=1)
    grad_qkv_bias = jnp.concatenate(
        [d[2].reshape(3, LANES)[:, :HDIM].reshape(-1) for d in done]
    )

    summed = scatter_sum_rows(
        (jnp.dot(context, w_out_ext, preferred_element_type=f32)
        + jnp.dot(act, w_down, preferred_element_type=f32)),
        "tensor",
    )
    inputs = tokens.astype(f32)
    block_out = (inputs + out_bias.astype(f32) + summed).astype(bf16)
    grad_out = trans_times(context, piece)
    grad_out = grad_out.reshape(heads, LANES, width)[:, :HDIM].reshape(heads * HDIM, width)
    grad_qkv = trans_times(normed_a, proj)
    back_attn = times_trans(proj, w_qkv)

    x_f = x_all.astype(f32)
    off = x_f - jnp.mean(x_f, axis=-1, keepdims=True)
    xhat_all = off * lax.rsqrt(jnp.mean(off * off, axis=-1, keepdims=True) + norm_eps)
    part = jnp.stack(
        [
            jnp.sum(back_attn * xhat_all, axis=0),
            jnp.sum(back_attn, axis=0),
            jnp.sum(back_mlp * xhat_all, axis=0),
            jnp.sum(back_mlp, axis=0),
        ]
    )
    grad_rows = grad_send.astype(f32)
    vec = jnp.concatenate([jnp.sum(grad_rows, axis=0)[None], part], axis=0)
    vec = all_sum_small(vec, "tensor")
    share = width // n_tensor
    vec = lax.dynamic_slice_in_dim(vec, lax.axis_index("tensor") * share, share, 1)

    dx = scatter_sum_rows(back_attn * vectors[0:1] + back_mlp * vectors[2:3], "tensor")
    off = inputs - jnp.mean(inputs, axis=-1, keepdims=True)
    inv = lax.rsqrt(jnp.mean(off * off, axis=-1, keepdims=True) + norm_eps)
    xhat = off * inv
    grad_input = grad_rows + inv * (
        dx
        - jnp.mean(dx, axis=-1, keepdims=True)
        - xhat * jnp.mean(dx * xhat, axis=-1, keepdims=True)
    )

    tail_sum = all_sum_rows(grad_qkv, "dp")
    out_sum = all_sum_rows(grad_out, "dp")
    small = all_sum_small(
        jnp.concatenate([grad_qkv_bias, grad_up_bias, vec.reshape(-1)]), "dp"
    )
    nq, nu = grad_qkv_bias.shape[0], grad_up_bias.shape[0]
    return (
        block_out,
        grad_input,
        tail_sum.astype(f32),
        small[:nq],
        out_sum.astype(f32),
        mlp_sum[:width].astype(f32),
        small[nq : nq + nu],
        mlp_sum[width:].astype(f32),
        small[nq + nu :].reshape(5, share),
    )


def solution(mesh):
    placed = (
        P(("dp", "tensor"), None),
        P("dp", None),
        P(None, "tensor"),
        P("tensor"),
        P("tensor", None),
        P(None, "tensor"),
        P("tensor"),
        P("tensor", None),
        P(),
        P(),
        P(),
        P(),
        P(),
        P(("dp", "tensor"), None),
    )
    return jax.shard_map(
        body,
        mesh=mesh,
        in_specs=placed,
        out_specs=(
            P(("dp", "tensor"), None),
            P(("dp", "tensor"), None),
            P(None, "tensor"),
            P("tensor"),
            P("tensor", None),
            P(None, "tensor"),
            P("tensor"),
            P("tensor", None),
            P(None, "tensor"),
        ),
        check_vma=False,
    )
```

```python
import functools

import jax
import jax.numpy as jnp
from jax import lax
from jax.experimental import pallas as pl
from jax.experimental.pallas import tpu as pltpu
from jax.sharding import PartitionSpec as P

HDIM = 64
ROT = 16
PADB = 128
LANES = 128
QB = 256

norm_eps = 1e-05
masked_fill = -1e30
rotary_base = 10000.0
f32 = jnp.float32
bf16 = jnp.bfloat16


def swap(values, axis, bit):
    n = lax.axis_size(axis)
    return lax.ppermute(values, axis, [(i, i ^ bit) for i in range(n)])


def gather_blocks(values, axis):
    blocks = {0: values}
    bit = lax.axis_size(axis) // 2
    while bit:
        for at in list(blocks):
            blocks[at | bit] = swap(blocks[at], axis, bit)
        bit //= 2
    return [blocks[j] for j in range(lax.axis_size(axis))]


def scatter_sum_blocks(blocks, axis):
    blocks = dict(enumerate(blocks))
    n = lax.axis_size(axis)
    bit = 1
    while bit < n:
        got = {j ^ bit: swap(blocks[j].astype(bf16), axis, bit) for j in blocks if j & bit}
        blocks = {j: blocks[j].astype(f32) + got[j].astype(f32) for j in got}
        bit *= 2
    return blocks[0]


def axis_bits(axis, first):
    n = lax.axis_size(axis)
    bits = [1 << k for k in range(n.bit_length() - 1)]
    return bits[first:] + bits[:first]


def all_sum_rows(values, axis, first):
    out = values.astype(bf16)
    bits = axis_bits(axis, first)
    me = lax.axis_index(axis)
    for bit in bits:
        out = out.reshape((2, out.shape[0] // 2) + out.shape[1:])
        side = (me // bit) % 2
        keep = lax.dynamic_index_in_dim(out, side, 0, keepdims=False)
        give = lax.dynamic_index_in_dim(out, 1 - side, 0, keepdims=False)
        got = swap(give, axis, bit)
        out = (keep.astype(f32) + got.astype(f32)).astype(bf16)
    for bit in reversed(bits):
        got = swap(out, axis, bit)
        side = (me // bit) % 2
        low = jnp.where(side == 0, out, got)
        high = jnp.where(side == 0, got, out)
        out = jnp.concatenate([low, high], axis=0)
    return out


def all_sum_small(values, axis):
    for bit in axis_bits(axis, 0):
        values = values + swap(values, axis, bit)
    return values


def token_layout(lengths, total, pad_block):
    padded = (lengths + pad_block - 1) // pad_block * pad_block
    starts = jnp.cumsum(padded) - padded
    row_ids = jnp.arange(total, dtype=jnp.int32)
    inside = (row_ids[None, :] >= starts[:, None]) & (
        row_ids[None, :] < (starts + lengths)[:, None]
    )
    slot_ids = jnp.arange(lengths.shape[0], dtype=jnp.int32)
    documents = jnp.sum(jnp.where(inside, slot_ids[:, None] + 1, 0), axis=0) - 1
    offsets = jnp.sum(jnp.where(inside, starts[:, None], 0), axis=0)
    return (documents, row_ids - offsets)


def aux_rows(documents, positions):
    half = ROT // 2
    inverse = rotary_base ** (-(jnp.arange(half, dtype=f32) * 2.0 / ROT))
    angles = inverse[:, None] * positions.astype(f32)[None, :]
    docs = (documents + 1).astype(f32)[None, :]
    return jnp.concatenate(
        [jnp.cos(angles), jnp.sin(angles), docs, jnp.zeros((7, docs.shape[1]), f32)], axis=0
    )


def dot(left, right):
    return lax.dot_general(left, right, (((1,), (0,)), ((), ())), preferred_element_type=f32)


def dot_nt(left, right):
    return lax.dot_general(left, right, (((1,), (1,)), ((), ())), preferred_element_type=f32)


def normalize(x):
    center = jnp.mean(x, axis=-1, keepdims=True)
    off = x - center
    inv = lax.rsqrt(jnp.mean(off * off, axis=-1, keepdims=True) + norm_eps)
    return off * inv, inv


def lane_tables(aux):
    rows = aux.shape[1]
    half = ROT // 2
    t = jnp.concatenate([aux, jnp.zeros((LANES - aux.shape[0], rows), f32)], axis=0).T
    lane = lax.broadcasted_iota(jnp.int32, (rows, LANES), 1)
    cosine = jnp.where(lane < half, t, jnp.where(lane < ROT, pltpu.roll(t, half, 1), 1.0))
    up = jnp.where(lane < half, pltpu.roll(t, LANES - half, 1), 0.0)
    down = jnp.where((lane >= half) & (lane < ROT), t, 0.0)
    return cosine, up, down, t[:, ROT : ROT + 1], lane


def front_kernel(heads, slots, me_ref, x_ref, w_ref, b_ref, vec_ref, aux_ref, *rest):
    qkv_ref = rest[-1]
    half = ROT // 2
    xhat, _ = normalize(x_ref[...].astype(f32))
    normed = (xhat * vec_ref[0:1, :] + vec_ref[1:2, :]).astype(bf16)
    cosine, up, down, doc, lane = lane_tables(aux_ref[...])
    used = (lane >= HDIM) & (lane <= HDIM + slots)
    hit = (lane - HDIM).astype(f32) == doc
    key_side = jnp.where(used & hit, 1.0, 0.0)
    query_side = jnp.where(used & ~hit, masked_fill, 0.0)
    for h in range(heads):
        cols = pl.ds(h * 3 * LANES, 3 * LANES)
        proj = dot(normed, w_ref[:, cols]) + b_ref[:, cols]
        for part in range(2):
            a = proj[:, part * LANES : (part + 1) * LANES]
            a = a * cosine - pltpu.roll(a, LANES - half, 1) * up + pltpu.roll(a, half, 1) * down
            a = a * HDIM**-0.5 + query_side if part == 0 else a + key_side
            qkv_ref[:, pl.ds((h * 3 + part) * LANES, LANES)] = a.astype(bf16)
        qkv_ref[:, pl.ds((h * 3 + 2) * LANES, LANES)] = proj[:, 2 * LANES :].astype(bf16)


def front(me, offset, x, w_ext, b_ext, vectors, aux, slots, heads, kept):
    rows, width = x.shape
    tile = aux.shape[1] // lax.axis_size("tensor")
    wide = w_ext.shape[1]
    whole = lambda a: pl.BlockSpec(a.shape, lambda r, me: (0, 0))
    args = [x, w_ext, b_ext, vectors, aux]
    specs = [
        pl.BlockSpec((tile, width), lambda r, me: (r, 0)),
        whole(w_ext), whole(b_ext), whole(vectors),
        pl.BlockSpec((aux.shape[0], tile), lambda r, me: (0, (r + offset) ^ me[0])),
    ]
    alias = {}
    if kept is not None:
        args.append(kept)
        specs.append(pl.BlockSpec(memory_space=pl.ANY))
        alias = {len(args): 0}
    return pl.pallas_call(
        functools.partial(front_kernel, heads, slots),
        grid_spec=pltpu.PrefetchScalarGridSpec(
            num_scalar_prefetch=1,
            grid=(rows // tile,),
            in_specs=specs,
            out_specs=pl.BlockSpec((tile, wide), lambda r, me: ((r + offset) ^ me[0], 0)),
        ),
        out_shape=jax.ShapeDtypeStruct((aux.shape[1], wide), bf16),
        input_output_aliases=alias,
        compiler_params=pltpu.CompilerParams(vmem_limit_bytes=40 * 2**20),
        cost_estimate=pl.CostEstimate(
            flops=2 * rows * width * wide, bytes_accessed=rows * 4000, transcendentals=0
        ),
        name="front",
    )(me, *args)


def mlp_kernel(
    first, me_ref, x_ref, c_ref, wu_ref, wd_ref, wo_ref, vec_ref, bu_ref, *rest
):
    y_ref, dx_ref, g_ref, gu_ref, gd_ref, sums_ref, up_acc, down_acc = rest[-8:]
    step = pl.program_id(0)

    @pl.when(step == 0)
    def _():
        if first:
            up_acc[...] = jnp.zeros_like(up_acc)
            down_acc[...] = jnp.zeros_like(down_acc)
            sums_ref[...] = jnp.zeros_like(sums_ref)
        else:
            up_acc[...] = rest[1][...]
            down_acc[...] = rest[2][...]
            sums_ref[...] = rest[3][...]

    xhat, _ = normalize(x_ref[...].astype(f32))
    normed = (xhat * vec_ref[2:3, :] + vec_ref[3:4, :]).astype(bf16)
    normed_t = normed.T
    c = c_ref[...]
    g_ref[...] = dot_nt(c, wo_ref[...]).astype(bf16)
    y = None
    hidden_width = wu_ref.shape[1]
    for at in range(0, hidden_width, QB):
        cols = pl.ds(at, QB)
        h = dot(normed, wu_ref[:, cols]) + bu_ref[:, cols]
        cdf = 0.5 + 0.5 * lax.erf(h * 0.5**0.5)
        pdf = jnp.exp(-0.5 * h * h) * (2.0 * jnp.pi) ** -0.5
        act = (h * cdf).astype(bf16)
        gh = dot_nt(c, wd_ref[cols, :]) * (cdf + h * pdf)
        sums_ref[0:1, cols] += jnp.sum(gh, axis=0, keepdims=True)
        gh = gh.astype(bf16)
        y_part = dot(act, wd_ref[cols, :])
        dn_part = dot_nt(gh, wu_ref[:, cols])
        y = y_part if y is None else y + y_part
        dn = dn_part if at == 0 else dn + dn_part
        down_acc[cols, :] += dot(act.T, c)
        up_acc[:, cols] += dot(normed_t, gh)
    y_ref[...] = y.astype(bf16)
    dx_ref[...] = (dn * vec_ref[2:3, :]).astype(bf16)
    sums_ref[1:2, :] += jnp.sum(dn * xhat, axis=0, keepdims=True)
    sums_ref[2:3, :] += jnp.sum(dn, axis=0, keepdims=True)

    @pl.when(step == pl.num_programs(0) - 1)
    def _():
        gu_ref[...] = up_acc[...].astype(gu_ref.dtype)
        gd_ref[...] = down_acc[...].astype(gd_ref.dtype)


def mlp(me, offset, total, x, c, w_up, w_down, w_out_ext, vectors, b_up, kept):
    rows, width = x.shape
    tile = total // lax.axis_size("tensor")
    units = w_up.shape[1]
    wide = w_out_ext.shape[0]
    whole = lambda a: pl.BlockSpec(a.shape, lambda r, me: (0, 0))
    shaped = lambda *s: pl.BlockSpec(s, lambda r, me: (0, 0))
    row_block = pl.BlockSpec((tile, width), lambda r, me: (r, 0))
    args = [x, c, w_up, w_down, w_out_ext, vectors, b_up]
    specs = [row_block, row_block] + [whole(a) for a in args[2:]]
    alias = {}
    first = kept is None
    if not first:
        args += kept
        specs += [pl.BlockSpec(memory_space=pl.ANY)] + [whole(a) for a in kept[1:]]
        alias = {8: 2}
    kind = f32 if first else bf16
    return pl.pallas_call(
        functools.partial(mlp_kernel, first),
        grid_spec=pltpu.PrefetchScalarGridSpec(
            num_scalar_prefetch=1,
            grid=(rows // tile,),
            in_specs=specs,
            out_specs=[
                row_block, row_block,
                pl.BlockSpec((tile, wide), lambda r, me: ((r + offset) ^ me[0], 0)),
                shaped(width, units), shaped(units, width), shaped(8, width),
            ],
            scratch_shapes=[pltpu.VMEM((width, units), f32), pltpu.VMEM((units, width), f32)],
        ),
        out_shape=[
            jax.ShapeDtypeStruct((rows, width), bf16),
            jax.ShapeDtypeStruct((rows, width), bf16),
            jax.ShapeDtypeStruct((total, wide), bf16),
            jax.ShapeDtypeStruct((width, units), kind),
            jax.ShapeDtypeStruct((units, width), kind),
            jax.ShapeDtypeStruct((8, width), f32),
        ],
        input_output_aliases=alias,
        compiler_params=pltpu.CompilerParams(vmem_limit_bytes=48 * 2**20),
        cost_estimate=pl.CostEstimate(
            flops=14 * rows * width * units, bytes_accessed=rows * 8000, transcendentals=0
        ),
        name="mlp",
    )(me, *args)


def block_rows_of(i):
    return i * (i + 1) // 2 * QB


def attend_kernel(q_ref, k_ref, v_ref, ctx_ref, ct_ref, e_ref, inv_ref, vt_ref, s_ref):
    total = q_ref.shape[0]
    vt_ref[...] = v_ref[...].T
    row_at = lax.broadcasted_iota(jnp.int32, (QB, QB), 0)
    col_at = lax.broadcasted_iota(jnp.int32, (QB, QB), 1)
    causal = row_at <= col_at
    feature = lax.broadcasted_iota(jnp.int32, (LANES, QB), 0)
    for i in range(total // QB):
        here = pl.ds(i * QB, QB)
        reach = (i + 1) * QB
        base = block_rows_of(i)
        qt = q_ref[here, :].T
        top = None
        for j in range(i + 1):
            at = pl.ds(j * QB, QB)
            s = dot(k_ref[at, :], qt)
            if j == i:
                s = jnp.where(causal, s, masked_fill)
            s_ref[at, :] = s
            part = jnp.max(s.reshape(QB // 8, 8, QB), axis=0)
            top = part if top is None else jnp.maximum(top, part)
        top = jnp.max(top, axis=0, keepdims=True)
        for j in range(i + 1):
            e_ref[0, pl.ds(base + j * QB, QB), :] = jnp.exp(
                s_ref[pl.ds(j * QB, QB), :] - top
            ).astype(bf16)
        ct = dot(vt_ref[:, :reach], e_ref[0, base : base + reach, :])
        inv = 1.0 / ct[HDIM : HDIM + 1, :]
        ct = jnp.where(feature < HDIM, ct * inv, 0.0)
        ctx_ref[here, :] = ct.T.astype(bf16)
        ct_ref[0, :, here] = ct[:HDIM, :]
        inv_ref[0, i : i + 1, :] = inv


def attend(qkv, heads):
    total = qkv.shape[0]
    pick = lambda p: pl.BlockSpec((total, LANES), lambda h: (0, h * 3 + p))
    deep = lambda *s: pl.BlockSpec((1,) + s, lambda h: (h, 0, 0))
    blocks = total // QB
    kept = block_rows_of(blocks)
    return pl.pallas_call(
        attend_kernel,
        grid=(heads,),
        in_specs=[pick(0), pick(1), pick(2)],
        out_specs=[
            pl.BlockSpec((total, LANES), lambda h: (0, h)),
            deep(HDIM, total), deep(kept, QB), deep(blocks, QB),
        ],
        out_shape=[
            jax.ShapeDtypeStruct((total, heads * LANES), bf16),
            jax.ShapeDtypeStruct((heads, HDIM, total), f32),
            jax.ShapeDtypeStruct((heads, kept, QB), bf16),
            jax.ShapeDtypeStruct((heads, blocks, QB), f32),
        ],
        scratch_shapes=[pltpu.VMEM((LANES, total), bf16), pltpu.VMEM((total, QB), f32)],
        compiler_params=pltpu.CompilerParams(vmem_limit_bytes=48 * 2**20),
        cost_estimate=pl.CostEstimate(
            flops=heads * kept * 3 * 2 * QB**2, bytes_accessed=heads * kept * 600, transcendentals=0
        ),
        name="attend",
    )(qkv, qkv, qkv)


def attend_back_kernel(
    q_ref, k_ref, v_ref, g_ref, ct_ref, e_ref, inv_ref, aux_ref,
    proj_ref, bias_ref,
    kt_ref, d_ref, dk_ref, dv_ref,
):
    total = q_ref.shape[0]
    half = ROT // 2
    kt_ref[...] = k_ref[...].T
    feature = lax.broadcasted_iota(jnp.int32, (LANES, QB), 0)
    bias_q = jnp.zeros((1, LANES), f32)
    for i in range(total // QB):
        here = pl.ds(i * QB, QB)
        reach = (i + 1) * QB
        base = block_rows_of(i)
        qt = q_ref[here, :].T.astype(f32)
        gt = g_ref[here, :].T.astype(f32)
        inv = inv_ref[0, i : i + 1, :]
        less = -jnp.sum(gt[:HDIM, :] * ct_ref[0, :, here], axis=0, keepdims=True)
        less_hi = less.astype(bf16).astype(f32)
        ge = jnp.where(feature == HDIM, less_hi, gt)
        ge = jnp.where(feature == HDIM + 1, less - less_hi, ge).astype(bf16)
        gl = (gt * inv).T.astype(bf16)
        ql = jnp.where(feature < HDIM, qt * inv, 0.0).T.astype(bf16)
        for j in range(i + 1):
            at = pl.ds(j * QB, QB)
            e = e_ref[0, pl.ds(base + j * QB, QB), :]
            d = (e.astype(f32) * dot(v_ref[at, :], ge)).astype(bf16)
            d_ref[at, :] = d
            dv = dot(e, gl)
            dk = dot(d, ql)
            if j == i:
                dv_ref[at, :] = dv
                dk_ref[at, :] = dk
            else:
                dv_ref[at, :] += dv
                dk_ref[at, :] += dk
        dqt = dot(kt_ref[:, :reach], d_ref[:reach, :]) * (inv * HDIM**-0.5)
        c, s = aux_ref[:half, here], aux_ref[half:ROT, here]
        low, high = dqt[:half, :], dqt[half:ROT, :]
        dqt = jnp.concatenate(
            [low * c + high * s, high * c - low * s, dqt[ROT:HDIM, :],
             jnp.zeros((LANES - HDIM, QB), f32)], axis=0
        )
        dq = dqt.T
        bias_q += jnp.sum(dq, axis=0, keepdims=True)
        proj_ref[0, here, :HDIM] = dq[:, :HDIM].astype(bf16)
    bias_k = jnp.zeros((1, LANES), f32)
    bias_v = jnp.zeros((1, LANES), f32)
    for i in range(total // QB):
        here = pl.ds(i * QB, QB)
        cosine, up, down, _, _ = lane_tables(aux_ref[:, here])
        dk = dk_ref[here, :]
        dk = dk * cosine + pltpu.roll(dk, LANES - half, 1) * up - pltpu.roll(dk, half, 1) * down
        dv = dv_ref[here, :]
        bias_k += jnp.sum(dk, axis=0, keepdims=True)
        bias_v += jnp.sum(dv, axis=0, keepdims=True)
        proj_ref[0, here, HDIM : 2 * HDIM] = dk[:, :HDIM].astype(bf16)
        proj_ref[0, here, 2 * HDIM :] = dv[:, :HDIM].astype(bf16)
    bias_ref[0] = jnp.concatenate([bias_q, bias_k, bias_v], axis=1)


def attend_back(qkv, grad_ctx, kept, aux, start, count):
    ct, e, inv = kept
    total = qkv.shape[0]
    pick = lambda p: pl.BlockSpec((total, LANES), lambda h: (0, (h + start) * 3 + p))
    deep = lambda a: pl.BlockSpec((1,) + a.shape[1:], lambda h: (h + start, 0, 0))
    out = lambda *s: pl.BlockSpec((1,) + s, lambda h: (h, 0, 0))
    return pl.pallas_call(
        attend_back_kernel,
        grid=(count,),
        in_specs=[
            pick(0), pick(1), pick(2),
            pl.BlockSpec((total, LANES), lambda h: (0, h + start)),
            deep(ct), deep(e), deep(inv),
            pl.BlockSpec(aux.shape, lambda h: (0, 0)),
        ],
        out_specs=[out(total, 3 * HDIM), out(1, 3 * LANES)],
        out_shape=[
            jax.ShapeDtypeStruct((count, total, 3 * HDIM), bf16),
            jax.ShapeDtypeStruct((count, 1, 3 * LANES), f32),
        ],
        scratch_shapes=[
            pltpu.VMEM((LANES, total), bf16),
            pltpu.VMEM((total, QB), bf16),
            pltpu.VMEM((total, LANES), f32),
            pltpu.VMEM((total, LANES), f32),
        ],
        compiler_params=pltpu.CompilerParams(vmem_limit_bytes=48 * 2**20),
        cost_estimate=pl.CostEstimate(
            flops=count * e.shape[1] * 6 * 2 * QB**2,
            bytes_accessed=count * e.shape[1] * 600,
            transcendentals=0,
        ),
        name="attend_back",
    )(qkv, qkv, qkv, grad_ctx, ct, e, inv, aux)


def pick_half(step, ref_a, ref_b):
    return jnp.where(step < 2, ref_a[...], ref_b[...])


def mid_kernel(n, me_ref, ctx_ref, c0_ref, c1_ref, y0_ref, y1_ref, wo_ref, *rest):
    outs, go_ref, acc = rest[:n], rest[n], rest[n + 1]
    step = pl.program_id(0)
    near = step < n // 2
    c = jnp.where(near, c0_ref[...], c1_ref[...])
    y = jnp.where(near, y0_ref[...], y1_ref[...]).astype(f32)
    ctx = ctx_ref[...]
    y = (y + dot(ctx, wo_ref[...])).astype(bf16)
    go = dot(ctx.T, c)
    for j in range(n):
        @pl.when(step == j)
        def _(j=j):
            outs[j][...] = y

    @pl.when(step == 0)
    def _():
        acc[...] = go

    @pl.when(step > 0)
    def _():
        acc[...] += go

    @pl.when(step == n - 1)
    def _():
        go_ref[...] = acc[...].astype(bf16)


def near_far(n, tile, width):
    half = n // 2
    return [
        pl.BlockSpec((tile, width), lambda r, me: (jnp.minimum(r, half - 1), 0)),
        pl.BlockSpec((tile, width), lambda r, me: (jnp.maximum(r - half, 0), 0)),
    ]


def mid(me, ctx, c_halves, y_halves, w_out_ext):
    n = lax.axis_size("tensor")
    total, wide = ctx.shape
    tile = total // n
    width = w_out_ext.shape[1]
    fixed = lambda *s: pl.BlockSpec(s, lambda r, me: (0, 0))
    out = pl.pallas_call(
        functools.partial(mid_kernel, n),
        grid_spec=pltpu.PrefetchScalarGridSpec(
            num_scalar_prefetch=1,
            grid=(n,),
            in_specs=[pl.BlockSpec((tile, wide), lambda r, me: (r ^ me[0], 0))]
            + near_far(n, tile, width) * 2
            + [fixed(wide, width)],
            out_specs=[fixed(tile, width)] * n + [fixed(wide, width)],
            scratch_shapes=[pltpu.VMEM((wide, width), f32)],
        ),
        out_shape=[jax.ShapeDtypeStruct((tile, width), bf16)] * n
        + [jax.ShapeDtypeStruct((wide, width), bf16)],
        compiler_params=pltpu.CompilerParams(vmem_limit_bytes=40 * 2**20),
        cost_estimate=pl.CostEstimate(
            flops=4 * total * wide * width, bytes_accessed=total * 8000, transcendentals=0
        ),
        name="mid",
    )(me, ctx, *c_halves, *y_halves, w_out_ext)
    return out[:n], out[n]


def back_kernel(n, heads, me_ref, proj_ref, x0_ref, x1_ref, d0_ref, d1_ref, w_ref, vec_ref, *rest):
    outs, gq_ref, sums_ref, acc = rest[:n], rest[n], rest[n + 1], rest[n + 2]
    step = pl.program_id(0)
    near = step < n // 2
    xhat, _ = normalize(jnp.where(near, x0_ref[...], x1_ref[...]).astype(f32))
    dx = jnp.where(near, d0_ref[...], d1_ref[...]).astype(f32)
    normed_t = (xhat * vec_ref[0:1, :] + vec_ref[1:2, :]).astype(bf16).T

    @pl.when(step == 0)
    def _():
        acc[...] = jnp.zeros_like(acc)
        sums_ref[...] = jnp.zeros_like(sums_ref)

    dn = None
    for h in range(heads):
        p = proj_ref[h]
        part = dot(p, w_ref[h])
        dn = part if dn is None else dn + part
        acc[h] += dot(normed_t, p)
    dx = (dx + dn * vec_ref[0:1, :]).astype(bf16)
    sums_ref[1:2, :] += jnp.sum(dn * xhat, axis=0, keepdims=True)
    sums_ref[2:3, :] += jnp.sum(dn, axis=0, keepdims=True)
    for j in range(n):
        @pl.when(step == j)
        def _(j=j):
            outs[j][...] = dx

    @pl.when(step == n - 1)
    def _():
        gq_ref[...] = acc[...].astype(bf16)


def back(me, proj, x_halves, d_halves, w_heads, vectors):
    n = lax.axis_size("tensor")
    heads, total, wide = proj.shape
    tile = total // n
    width = w_heads.shape[2]
    fixed = lambda *s: pl.BlockSpec(s, lambda r, me: (0,) * len(s))
    out = pl.pallas_call(
        functools.partial(back_kernel, n, heads),
        grid_spec=pltpu.PrefetchScalarGridSpec(
            num_scalar_prefetch=1,
            grid=(n,),
            in_specs=[pl.BlockSpec((heads, tile, wide), lambda r, me: (0, r ^ me[0], 0))]
            + near_far(n, tile, width) * 2
            + [fixed(*w_heads.shape), fixed(*vectors.shape)],
            out_specs=[fixed(tile, width)] * n + [fixed(heads, width, wide), fixed(8, width)],
            scratch_shapes=[pltpu.VMEM((heads, width, wide), f32)],
        ),
        out_shape=[jax.ShapeDtypeStruct((tile, width), bf16)] * n
        + [
            jax.ShapeDtypeStruct((heads, width, wide), bf16),
            jax.ShapeDtypeStruct((8, width), f32),
        ],
        compiler_params=pltpu.CompilerParams(vmem_limit_bytes=40 * 2**20),
        cost_estimate=pl.CostEstimate(
            flops=4 * total * heads * wide * width, bytes_accessed=total * 8000, transcendentals=0
        ),
        name="back",
    )(me, proj, *x_halves, *d_halves, w_heads, vectors)
    return out[:n], out[n], out[n + 1]


def body(
    tokens,
    doc_lengths,
    w_qkv,
    b_qkv,
    w_out,
    w_up,
    b_up,
    w_down,
    out_bias,
    norm1_gain,
    norm1_shift,
    norm2_gain,
    norm2_shift,
    cotangent,
):
    row_count, width = tokens.shape
    n_tensor = lax.axis_size("tensor")
    total = row_count * n_tensor
    index = lax.axis_index("tensor")
    me = index.astype(jnp.int32).reshape(1)
    heads = w_out.shape[0] // HDIM
    slots = doc_lengths.shape[1]
    x_blocks = gather_blocks(tokens, "tensor")
    documents, positions = token_layout(doc_lengths[0], total, PADB)
    local_docs = lax.dynamic_slice_in_dim(documents, index * row_count, row_count)
    grad_send = jnp.where(local_docs[:, None] >= 0, cotangent, 0)
    c_blocks = gather_blocks(grad_send, "tensor")
    half = n_tensor // 2
    cat = lambda blocks: jnp.concatenate(blocks, axis=0)
    x_halves = [cat(x_blocks[:half]), cat(x_blocks[half:])]
    c_halves = [cat(c_blocks[:half]), cat(c_blocks[half:])]

    aux = aux_rows(documents, positions)
    w_ext = jnp.pad(
        w_qkv.reshape(width, heads * 3, HDIM), ((0, 0), (0, 0), (0, LANES - HDIM))
    ).reshape(width, heads * 3 * LANES)
    ones = (jnp.arange(LANES - HDIM) < 2).astype(f32)
    b_ext = jnp.concatenate(
        [
            b_qkv.astype(f32).reshape(heads, 3, HDIM),
            jnp.stack([0 * ones, 0 * ones, ones])[None].repeat(heads, 0),
        ],
        axis=2,
    ).reshape(1, heads * 3 * LANES)
    w_out_ext = jnp.pad(
        w_out.reshape(heads, HDIM, width), ((0, 0), (0, LANES - HDIM), (0, 0))
    ).reshape(heads * LANES, width)
    w_heads = w_qkv.T.reshape(heads, 3 * HDIM, width)
    vectors = jnp.stack([norm1_gain, norm1_shift, norm2_gain, norm2_shift]).astype(f32)
    b_up_row = b_up.astype(f32)[None]

    mlp_args = (w_up, w_down, w_out_ext, vectors, b_up_row)
    front_args = (w_ext, b_ext, vectors, aux, slots, heads)
    y0, d0, g, gu, gd, sums = mlp(me, 0, total, x_halves[0], c_halves[0], *mlp_args, None)
    qkv = front(me, 0, x_halves[0], *front_args, None)
    qkv = front(me, half, x_halves[1], *front_args, qkv)
    ctx, *kept = attend(qkv, heads)
    y1, d1, g, gu, gd, sums = mlp(
        me, half, total, x_halves[1], c_halves[1], *mlp_args, [g, gu, gd, sums]
    )
    up_sum = all_sum_rows(gu, "dp", 0)
    down_sum = all_sum_rows(gd, "dp", 1)
    y_blocks, grad_out = mid(me, ctx, c_halves, [y0, y1], w_out_ext)
    proj, bias = attend_back(qkv, g, kept, aux, 0, heads)
    summed = scatter_sum_blocks(y_blocks, "tensor")
    grad_out = grad_out.reshape(heads, LANES, width)[:, :HDIM].reshape(heads * HDIM, width)
    out_sum = all_sum_rows(grad_out, "dp", 0)
    dx_blocks, grad_qkv, back_sums = back(me, proj, x_halves, [d0, d1], w_heads, vectors)
    qkv_sum = all_sum_rows(grad_qkv.reshape(heads * width, 3 * HDIM), "dp", 0)
    dx = scatter_sum_blocks(dx_blocks, "tensor")

    inputs = tokens.astype(f32)
    block_out = (inputs + out_bias.astype(f32) + summed).astype(bf16)
    grad_rows = grad_send.astype(f32)
    xhat, inv = normalize(inputs)
    grad_input = grad_rows + inv * (
        dx
        - jnp.mean(dx, axis=-1, keepdims=True)
        - xhat * jnp.mean(dx * xhat, axis=-1, keepdims=True)
    )
    grad_qkv_bias = bias.reshape(heads, 3, LANES)[:, :, :HDIM].reshape(-1)
    vec = jnp.concatenate(
        [jnp.sum(grad_rows, axis=0)[None], back_sums[1:3], sums[1:3]], axis=0
    )
    vec = all_sum_small(vec, "tensor")
    share = width // n_tensor
    vec = lax.dynamic_slice_in_dim(vec, index * share, share, 1)
    small = all_sum_small(jnp.concatenate([grad_qkv_bias, sums[0], vec.reshape(-1)]), "dp")
    nq, nu = grad_qkv_bias.shape[0], b_up.shape[0]
    qkv_sum = qkv_sum.reshape(heads, width, 3 * HDIM).swapaxes(0, 1).reshape(w_qkv.shape)
    return (
        block_out,
        grad_input,
        qkv_sum.astype(f32),
        small[:nq],
        out_sum.astype(f32),
        up_sum.astype(f32),
        small[nq : nq + nu],
        down_sum.astype(f32),
        small[nq + nu :].reshape(5, share),
    )


def solution(mesh):
    placed = (
        P(("dp", "tensor"), None),
        P("dp", None),
        P(None, "tensor"),
        P("tensor"),
        P("tensor", None),
        P(None, "tensor"),
        P("tensor"),
        P("tensor", None),
        P(),
        P(),
        P(),
        P(),
        P(),
        P(("dp", "tensor"), None),
    )
    return jax.shard_map(
        body,
        mesh=mesh,
        in_specs=placed,
        out_specs=(
            P(("dp", "tensor"), None),
            P(("dp", "tensor"), None),
            P(None, "tensor"),
            P("tensor"),
            P("tensor", None),
            P(None, "tensor"),
            P("tensor"),
            P("tensor", None),
            P(None, "tensor"),
        ),
        check_vma=False,
    )
```

```python
import functools

import jax
import jax.numpy as jnp
from jax import lax
from jax.experimental import pallas as pl
from jax.experimental.pallas import tpu as pltpu
from jax.sharding import PartitionSpec as P

HDIM = 64
ROT = 16
PADB = 128
LANES = 128
QB = 256

norm_eps = 1e-05
masked_fill = -1e30
rotary_base = 10000.0
f32 = jnp.float32
bf16 = jnp.bfloat16


def swap(values, axis, bit):
    n = lax.axis_size(axis)
    return lax.ppermute(values, axis, [(i, i ^ bit) for i in range(n)])


def gather_far(values, axis):
    return swap(values, axis, lax.axis_size(axis) // 2)


def gather_near(values, axis):
    blocks = {0: values}
    bit = lax.axis_size(axis) // 4
    while bit:
        for at in list(blocks):
            blocks[at | bit] = swap(blocks[at], axis, bit)
        bit //= 2
    return [blocks[j] for j in range(len(blocks))]


class ScatterSum:
    def __init__(self, blocks, axis):
        self.blocks, self.axis, self.bit, self.got = dict(enumerate(blocks)), axis, 1, None

    def send(self):
        bit = self.bit
        self.got = {
            j ^ bit: swap(b.astype(bf16), self.axis, bit)
            for j, b in self.blocks.items()
            if j & bit
        }

    def finish(self):
        while self.bit < lax.axis_size(self.axis):
            self.send()
            self.take()

    def take(self):
        got = self.got
        self.blocks = {j: self.blocks[j].astype(f32) + got[j].astype(f32) for j in got}
        self.bit *= 2

    @property
    def out(self):
        return self.blocks[0]


def axis_bits(axis, first):
    n = lax.axis_size(axis)
    bits = [1 << k for k in range(n.bit_length() - 1)]
    return bits[first:] + bits[:first]


def tie(first, *others):
    return lax.optimization_barrier((first,) + others)


def take_before(value, *sums):
    value, got = lax.optimization_barrier((value, [a.got for a in sums]))
    for a, g in zip(sums, got):
        a.got = g
        a.take()
    return value


class StagedSum:
    def __init__(self, values, axis, first):
        self.held, self.axis, self.got = [values.astype(bf16)], axis, None
        bits = axis_bits(axis, first)
        self.steps = [(b, True) for b in bits] + [(b, False) for b in reversed(bits)]

    def part(self, side):
        def cut(a):
            a = a.reshape((2, a.shape[0] // 2) + a.shape[1:])
            return lax.dynamic_index_in_dim(a, side, 0, keepdims=False)

        parts = self.held if side is None else [cut(a) for a in self.held]
        if len(parts) == 1:
            return parts[0]
        return (parts[0].astype(f32) + parts[1].astype(f32)).astype(bf16)

    def send(self):
        bit, halving = self.steps[0]
        side = (lax.axis_index(self.axis) // bit) % 2
        self.got = swap(self.part(1 - side if halving else None), self.axis, bit)

    def take(self):
        bit, halving = self.steps.pop(0)
        side = (lax.axis_index(self.axis) // bit) % 2
        if halving:
            self.held = [self.part(side), self.got]
        else:
            mine = self.part(None)
            low = jnp.where(side == 0, mine, self.got)
            high = jnp.where(side == 0, self.got, mine)
            self.held = [jnp.concatenate([low, high], axis=0)]

    def finish(self):
        while self.steps:
            self.send()
            self.take()

    @property
    def out(self):
        return self.part(None)

class SmallSum:
    def __init__(self, values, axis):
        self.out, self.axis, self.bits, self.got = values, axis, axis_bits(axis, 0), None

    def send(self):
        self.got = swap(self.out, self.axis, self.bits.pop(0))

    def take(self):
        self.out = self.out + self.got

    def finish(self):
        while self.bits:
            self.send()
            self.take()


def token_layout(lengths, total, pad_block):
    padded = (lengths + pad_block - 1) // pad_block * pad_block
    starts = jnp.cumsum(padded) - padded
    row_ids = jnp.arange(total, dtype=jnp.int32)
    inside = (row_ids[None, :] >= starts[:, None]) & (
        row_ids[None, :] < (starts + lengths)[:, None]
    )
    slot_ids = jnp.arange(lengths.shape[0], dtype=jnp.int32)
    documents = jnp.sum(jnp.where(inside, slot_ids[:, None] + 1, 0), axis=0) - 1
    offsets = jnp.sum(jnp.where(inside, starts[:, None], 0), axis=0)
    return (documents, row_ids - offsets)


def aux_rows(documents, positions):
    half = ROT // 2
    inverse = rotary_base ** (-(jnp.arange(half, dtype=f32) * 2.0 / ROT))
    angles = inverse[:, None] * positions.astype(f32)[None, :]
    docs = (documents + 1).astype(f32)[None, :]
    return jnp.concatenate(
        [jnp.cos(angles), jnp.sin(angles), docs, jnp.zeros((7, docs.shape[1]), f32)], axis=0
    )


def dot(left, right):
    return lax.dot_general(left, right, (((1,), (0,)), ((), ())), preferred_element_type=f32)


def dot_nt(left, right):
    return lax.dot_general(left, right, (((1,), (1,)), ((), ())), preferred_element_type=f32)


def normalize(x):
    center = jnp.mean(x, axis=-1, keepdims=True)
    off = x - center
    inv = lax.rsqrt(jnp.mean(off * off, axis=-1, keepdims=True) + norm_eps)
    return off * inv, inv


def pick_block(refs, step):
    out = refs[0][...]
    for j in range(1, len(refs)):
        out = jnp.where(step == j, refs[j][...], out)
    return out


def head_window(a, at):
    if at % LANES == 0:
        return a[:, at : at + LANES]
    return pltpu.roll(a[:, at - HDIM : at + HDIM], HDIM, 1)


def pad_lanes(a):
    extra = -a.shape[1] % LANES
    if extra == 0:
        return a
    return jnp.concatenate([a, jnp.zeros((a.shape[0], extra), a.dtype)], axis=1)


def lane_tables(aux):
    rows = aux.shape[1]
    half = ROT // 2
    t = jnp.concatenate([aux, jnp.zeros((LANES - aux.shape[0], rows), f32)], axis=0).T
    lane = lax.broadcasted_iota(jnp.int32, (rows, LANES), 1)
    cosine = jnp.where(lane < half, t, jnp.where(lane < ROT, pltpu.roll(t, half, 1), 1.0))
    up = jnp.where(lane < half, pltpu.roll(t, LANES - half, 1), 0.0)
    down = jnp.where((lane >= half) & (lane < ROT), t, 0.0)
    return cosine, up, down, t[:, ROT : ROT + 1], lane


def front_kernel(heads, slots, count, me_ref, *refs):
    w_ref, b_ref, vec_ref, aux_ref = refs[count : count + 4]
    qkv_ref, normed_ref = refs[-2:]
    half = ROT // 2
    x = pick_block(refs[:count], pl.program_id(0))
    xhat, _ = normalize(x.astype(f32))
    normed = (xhat * vec_ref[0:1, :] + vec_ref[1:2, :]).astype(bf16)
    normed_ref[...] = normed
    cosine, up, down, doc, lane = lane_tables(aux_ref[...])
    used = (lane >= HDIM) & (lane <= HDIM + slots)
    hit = (lane - HDIM).astype(f32) == doc
    key_side = jnp.where(used & hit, 1.0, 0.0)
    query_side = jnp.where(used & ~hit, masked_fill, 0.0)
    value_side = jnp.where((lane >= HDIM) & (lane < HDIM + 2), 1.0, 0.0)
    own = lane < HDIM
    proj = pad_lanes(dot(normed, w_ref[...]) + b_ref[...])
    for h in range(heads):
        for part in range(3):
            a = head_window(proj, (h * 3 + part) * HDIM)
            if part < 2:
                a = a * cosine - pltpu.roll(a, LANES - half, 1) * up + pltpu.roll(a, half, 1) * down
            if part == 0:
                a = jnp.where(own, a * HDIM**-0.5, query_side)
            else:
                a = jnp.where(own, a, key_side if part == 1 else value_side)
            qkv_ref[:, pl.ds((h * 3 + part) * LANES, LANES)] = a.astype(bf16)


def front(me, offset, blocks, w_qkv, b_qkv, vectors, aux, slots, heads, kept):
    tile, width = blocks[0].shape
    wide = heads * 3 * LANES
    whole = lambda a: pl.BlockSpec(a.shape, lambda r, me: (0, 0))
    args = blocks + [w_qkv, b_qkv, vectors, aux]
    specs = [whole(a) for a in args[:-1]]
    specs.append(pl.BlockSpec((aux.shape[0], tile), lambda r, me: (0, (r + offset) ^ me[0])))
    alias = {}
    if kept is not None:
        args += kept
        specs += [pl.BlockSpec(memory_space=pl.ANY)] * 2
        alias = {len(args) - 1: 0, len(args): 1}
    return pl.pallas_call(
        functools.partial(front_kernel, heads, slots, len(blocks)),
        grid_spec=pltpu.PrefetchScalarGridSpec(
            num_scalar_prefetch=1,
            grid=(len(blocks),),
            in_specs=specs,
            out_specs=[
                pl.BlockSpec((tile, wide), lambda r, me: ((r + offset) ^ me[0], 0)),
                pl.BlockSpec((tile, width), lambda r, me: ((r + offset) ^ me[0], 0)),
            ],
        ),
        out_shape=[
            jax.ShapeDtypeStruct((aux.shape[1], wide), bf16),
            jax.ShapeDtypeStruct((aux.shape[1], width), bf16),
        ],
        input_output_aliases=alias,
        compiler_params=pltpu.CompilerParams(vmem_limit_bytes=28 * 2**20),
        cost_estimate=pl.CostEstimate(
            flops=4 * len(blocks) * tile * width * wide,
            bytes_accessed=len(blocks) * tile * 4000,
            transcendentals=0,
        ),
        name="front",
    )(me, *args)


def mlp_kernel(
    first, count, me_ref, *refs
):
    wu_ref, wd_ref, wo_ref, vec_ref, bu_ref = refs[2 * count : 2 * count + 5]
    rest = refs[2 * count + 5 :]
    y_ref, dx_ref, g_ref, gu_ref, gd_ref, sums_ref, up_acc, down_acc = rest[-8:]
    step = pl.program_id(0)

    @pl.when(step == 0)
    def _():
        if first:
            up_acc[...] = jnp.zeros_like(up_acc)
            down_acc[...] = jnp.zeros_like(down_acc)
            sums_ref[...] = jnp.zeros_like(sums_ref)
        else:
            up_acc[...] = rest[1][...]
            down_acc[...] = rest[2][...]
            sums_ref[...] = rest[3][...]

    xhat, _ = normalize(pick_block(refs[:count], step).astype(f32))
    normed = (xhat * vec_ref[2:3, :] + vec_ref[3:4, :]).astype(bf16)
    normed_t = normed.T
    c = pick_block(refs[count : 2 * count], step)
    g = pad_lanes(dot_nt(c, wo_ref[...]))
    own = lax.broadcasted_iota(jnp.int32, (c.shape[0], LANES), 1) < HDIM
    for h in range(g_ref.shape[1] // LANES):
        part = jnp.where(own, head_window(g, h * HDIM), 0.0)
        g_ref[:, pl.ds(h * LANES, LANES)] = part.astype(bf16)
    y = None
    hidden_width = wu_ref.shape[1]
    for at in range(0, hidden_width, QB):
        cols = pl.ds(at, QB)
        h = dot(normed, wu_ref[:, cols]) + bu_ref[:, cols]
        cdf = 0.5 + 0.5 * lax.erf(h * 0.5**0.5)
        pdf = jnp.exp(-0.5 * h * h) * (2.0 * jnp.pi) ** -0.5
        act = (h * cdf).astype(bf16)
        gh = dot_nt(c, wd_ref[cols, :]) * (cdf + h * pdf)
        sums_ref[0:1, cols] += jnp.sum(gh, axis=0, keepdims=True)
        gh = gh.astype(bf16)
        y_part = dot(act, wd_ref[cols, :])
        dn_part = dot_nt(gh, wu_ref[:, cols])
        y = y_part if y is None else y + y_part
        dn = dn_part if at == 0 else dn + dn_part
        down_acc[cols, :] += dot(act.T, c)
        up_acc[:, cols] += dot(normed_t, gh)
    y_ref[...] = y.astype(bf16)
    dx_ref[...] = (dn * vec_ref[2:3, :]).astype(bf16)
    sums_ref[1:2, :] += jnp.sum(dn * xhat, axis=0, keepdims=True)
    sums_ref[2:3, :] += jnp.sum(dn, axis=0, keepdims=True)

    @pl.when(step == pl.num_programs(0) - 1)
    def _():
        gu_ref[...] = up_acc[...].astype(gu_ref.dtype)
        gd_ref[...] = down_acc[...].astype(gd_ref.dtype)


def mlp(me, offset, total, x, c, w_up, w_down, w_out, vectors, b_up, kept):
    count = len(x)
    tile, width = x[0].shape
    rows = count * tile
    units = w_up.shape[1]
    wide = w_out.shape[0] // HDIM * LANES
    whole = lambda a: pl.BlockSpec(a.shape, lambda r, me: (0, 0))
    shaped = lambda *s: pl.BlockSpec(s, lambda r, me: (0, 0))
    row_block = pl.BlockSpec((tile, width), lambda r, me: (r, 0))
    args = x + c + [w_up, w_down, w_out, vectors, b_up]
    specs = [whole(a) for a in args]
    alias = {}
    first = kept is None
    if not first:
        args += kept
        specs += [pl.BlockSpec(memory_space=pl.ANY)] + [whole(a) for a in kept[1:]]
        alias = {2 * count + 6: 2}
    kind = f32 if first else bf16
    return pl.pallas_call(
        functools.partial(mlp_kernel, first, count),
        grid_spec=pltpu.PrefetchScalarGridSpec(
            num_scalar_prefetch=1,
            grid=(count,),
            in_specs=specs,
            out_specs=[
                row_block, row_block,
                pl.BlockSpec((tile, wide), lambda r, me: ((r + offset) ^ me[0], 0)),
                shaped(width, units), shaped(units, width), shaped(8, width),
            ],
            scratch_shapes=[pltpu.VMEM((width, units), f32), pltpu.VMEM((units, width), f32)],
        ),
        out_shape=[
            jax.ShapeDtypeStruct((rows, width), bf16),
            jax.ShapeDtypeStruct((rows, width), bf16),
            jax.ShapeDtypeStruct((total, wide), bf16),
            jax.ShapeDtypeStruct((width, units), kind),
            jax.ShapeDtypeStruct((units, width), kind),
            jax.ShapeDtypeStruct((8, width), f32),
        ],
        input_output_aliases=alias,
        compiler_params=pltpu.CompilerParams(vmem_limit_bytes=40 * 2**20),
        cost_estimate=pl.CostEstimate(
            flops=14 * rows * width * units, bytes_accessed=rows * 8000, transcendentals=0
        ),
        name="mlp",
    )(me, *args)


def block_rows_of(i):
    return i * (i + 1) // 2 * QB


def attend_kernel(q_ref, k_ref, v_ref, ct_ref, e_ref, inv_ref, vt_ref, s_ref):
    total = q_ref.shape[0]
    vt_ref[...] = v_ref[...].T
    row_at = lax.broadcasted_iota(jnp.int32, (QB, QB), 0)
    col_at = lax.broadcasted_iota(jnp.int32, (QB, QB), 1)
    causal = row_at <= col_at
    for i in range(total // QB):
        here = pl.ds(i * QB, QB)
        reach = (i + 1) * QB
        base = block_rows_of(i)
        qt = q_ref[here, :].T
        top = None
        for j in range(i + 1):
            at = pl.ds(j * QB, QB)
            s = dot(k_ref[at, :], qt)
            if j == i:
                s = jnp.where(causal, s, masked_fill)
            s_ref[at, :] = s
            part = jnp.max(s.reshape(QB // 8, 8, QB), axis=0)
            top = part if top is None else jnp.maximum(top, part)
        top = jnp.max(top, axis=0, keepdims=True)
        for j in range(i + 1):
            e_ref[0, pl.ds(base + j * QB, QB), :] = jnp.exp(
                s_ref[pl.ds(j * QB, QB), :] - top
            ).astype(bf16)
        ct = dot(vt_ref[:, :reach], e_ref[0, base : base + reach, :])
        inv = 1.0 / ct[HDIM : HDIM + 1, :]
        ct_ref[0, :, here] = ct[:HDIM, :] * inv
        inv_ref[0, i : i + 1, :] = inv


def attend(qkv, start, heads):
    total = qkv.shape[0]
    pick = lambda p: pl.BlockSpec((total, LANES), lambda h: (0, (h + start) * 3 + p))
    deep = lambda *s: pl.BlockSpec((1,) + s, lambda h: (h, 0, 0))
    blocks = total // QB
    kept = block_rows_of(blocks)
    return pl.pallas_call(
        attend_kernel,
        grid=(heads,),
        in_specs=[pick(0), pick(1), pick(2)],
        out_specs=[
            deep(HDIM, total), deep(kept, QB), deep(blocks, QB),
        ],
        out_shape=[
            jax.ShapeDtypeStruct((heads, HDIM, total), f32),
            jax.ShapeDtypeStruct((heads, kept, QB), bf16),
            jax.ShapeDtypeStruct((heads, blocks, QB), f32),
        ],
        scratch_shapes=[pltpu.VMEM((LANES, total), bf16), pltpu.VMEM((total, QB), f32)],
        compiler_params=pltpu.CompilerParams(vmem_limit_bytes=28 * 2**20),
        cost_estimate=pl.CostEstimate(
            flops=heads * kept * 3 * 2 * QB**2, bytes_accessed=heads * kept * 600, transcendentals=0
        ),
        name="attend",
    )(qkv, qkv, qkv)


def attend_back_kernel(
    q_ref, k_ref, v_ref, g_ref, ct_ref, inv_ref, aux_ref, e_any, normed_any,
    proj_ref, bias_ref, grad_ref,
    kt_ref, d_ref, dk_ref, dv_ref, e_ref, normed_ref, sems, head,
):
    total = q_ref.shape[0]
    half = ROT // 2
    blocks = total // QB
    copies = []
    for i in range(blocks):
        rows = pl.ds(block_rows_of(i), (i + 1) * QB)
        copies.append(
            pltpu.make_async_copy(e_any.at[head, rows, :], e_ref.at[rows, :], sems.at[i])
        )
    copies.append(pltpu.make_async_copy(normed_any, normed_ref, sems.at[blocks]))
    for copy in copies:
        copy.start()
    kt_ref[...] = k_ref[...].T
    feature = lax.broadcasted_iota(jnp.int32, (LANES, QB), 0)
    bias_q = jnp.zeros((1, LANES), f32)
    for i in range(total // QB):
        here = pl.ds(i * QB, QB)
        reach = (i + 1) * QB
        base = block_rows_of(i)
        if i == 0:
            for copy in copies[:2]:
                copy.wait()
        if i == 2:
            for copy in copies[2:blocks]:
                copy.wait()
        qt = q_ref[here, :].T.astype(f32)
        gt = g_ref[here, :].T.astype(f32)
        inv = inv_ref[0, i : i + 1, :]
        less = -jnp.sum(gt[:HDIM, :] * ct_ref[0, :, here], axis=0, keepdims=True)
        less_hi = less.astype(bf16).astype(f32)
        ge = jnp.where(feature == HDIM, less_hi, gt)
        ge = jnp.where(feature == HDIM + 1, less - less_hi, ge).astype(bf16)
        gl = (gt * inv).T.astype(bf16)
        ql = jnp.where(feature < HDIM, qt * inv, 0.0).T.astype(bf16)
        for j in range(i + 1):
            at = pl.ds(j * QB, QB)
            e = e_ref[pl.ds(base + j * QB, QB), :]
            d = (e.astype(f32) * dot(v_ref[at, :], ge)).astype(bf16)
            d_ref[at, :] = d
            dv = dot(e, gl)
            dk = dot(d, ql)
            if j == i:
                dv_ref[at, :] = dv
                dk_ref[at, :] = dk
            else:
                dv_ref[at, :] += dv
                dk_ref[at, :] += dk
        dqt = dot(kt_ref[:, :reach], d_ref[:reach, :]) * (inv * HDIM**-0.5)
        c, s = aux_ref[:half, here], aux_ref[half:ROT, here]
        low, high = dqt[:half, :], dqt[half:ROT, :]
        dqt = jnp.concatenate(
            [low * c + high * s, high * c - low * s, dqt[ROT:HDIM, :],
             jnp.zeros((LANES - HDIM, QB), f32)], axis=0
        )
        dq = dqt.T
        bias_q += jnp.sum(dq, axis=0, keepdims=True)
        proj_ref[here, :HDIM] = dq[:, :HDIM].astype(bf16)
    bias_k = jnp.zeros((1, LANES), f32)
    bias_v = jnp.zeros((1, LANES), f32)
    for i in range(total // QB):
        here = pl.ds(i * QB, QB)
        cosine, up, down, _, _ = lane_tables(aux_ref[:, here])
        dk = dk_ref[here, :]
        dk = dk * cosine + pltpu.roll(dk, LANES - half, 1) * up - pltpu.roll(dk, half, 1) * down
        dv = dv_ref[here, :]
        bias_k += jnp.sum(dk, axis=0, keepdims=True)
        bias_v += jnp.sum(dv, axis=0, keepdims=True)
        proj_ref[here, HDIM : 2 * HDIM] = dk[:, :HDIM].astype(bf16)
        proj_ref[here, 2 * HDIM :] = dv[:, :HDIM].astype(bf16)
    bias_ref[...] = jnp.concatenate([bias_q, bias_k, bias_v], axis=1)
    copies[blocks].wait()
    grad_ref[...] = lax.dot_general(
        proj_ref[...], normed_ref[...], (((0,), (0,)), ((), ())), preferred_element_type=f32
    ).astype(bf16)


def attend_back(qkv, grad_ctx, kept, aux, normed, head, at):
    ct, e, inv = kept
    total, width = normed.shape
    blocks = total // QB
    pick = lambda p: pl.BlockSpec((total, LANES), lambda r: (0, head * 3 + p))
    deep = lambda a: pl.BlockSpec((1,) + a.shape[1:], lambda r: (at, 0, 0))
    out = lambda *s: pl.BlockSpec(s, lambda r: (0, 0))
    return pl.pallas_call(
        functools.partial(attend_back_kernel, head=at),
        grid=(1,),
        in_specs=[
            pick(0), pick(1), pick(2),
            pl.BlockSpec((total, LANES), lambda r: (0, head)),
            deep(ct), deep(inv),
            pl.BlockSpec(aux.shape, lambda r: (0, 0)),
            pl.BlockSpec(memory_space=pl.ANY),
            pl.BlockSpec(memory_space=pl.ANY),
        ],
        out_specs=[out(total, 3 * HDIM), out(1, 3 * LANES), out(3 * HDIM, width)],
        out_shape=[
            jax.ShapeDtypeStruct((total, 3 * HDIM), bf16),
            jax.ShapeDtypeStruct((1, 3 * LANES), f32),
            jax.ShapeDtypeStruct((3 * HDIM, width), bf16),
        ],
        scratch_shapes=[
            pltpu.VMEM((LANES, total), bf16),
            pltpu.VMEM((total, QB), bf16),
            pltpu.VMEM((total, LANES), f32),
            pltpu.VMEM((total, LANES), f32),
            pltpu.VMEM(e.shape[1:], bf16),
            pltpu.VMEM((total, width), bf16),
            pltpu.SemaphoreType.DMA((blocks + 1,)),
        ],
        compiler_params=pltpu.CompilerParams(vmem_limit_bytes=32 * 2**20),
        cost_estimate=pl.CostEstimate(
            flops=e.shape[1] * 6 * 2 * QB**2, bytes_accessed=e.shape[1] * 600, transcendentals=0
        ),
        name="attend_back",
    )(qkv, qkv, qkv, grad_ctx, ct, inv, aux, e, normed)


def mid_kernel(n, me_ref, cta_ref, ctb_ref, y0_ref, y1_ref, wo_ref, *refs):
    c_refs, rest = refs[:n], refs[n:]
    outs, go_ref, acc = rest[:n], rest[n], rest[n + 1]
    step = pl.program_id(0)
    near = step < n // 2
    c = pick_block(c_refs, step)
    y = jnp.where(near, y0_ref[...], y1_ref[...]).astype(f32)
    ct = jnp.concatenate([cta_ref[...], ctb_ref[...]], axis=0)
    ct = ct.reshape(wo_ref.shape[0], c.shape[0]).astype(bf16)
    y = (y + dot(ct.T, wo_ref[...])).astype(bf16)
    go = dot(ct, c)
    for j in range(n):
        @pl.when(step == j)
        def _(j=j):
            outs[j][...] = y

    @pl.when(step == 0)
    def _():
        acc[...] = go

    @pl.when(step > 0)
    def _():
        acc[...] += go

    @pl.when(step == n - 1)
    def _():
        go_ref[...] = acc[...].astype(bf16)


def near_far(n, tile, width):
    half = n // 2
    return [
        pl.BlockSpec((tile, width), lambda r, me: (jnp.minimum(r, half - 1), 0)),
        pl.BlockSpec((tile, width), lambda r, me: (jnp.maximum(r - half, 0), 0)),
    ]


def mid(me, cta, ctb, c_blocks, y_halves, w_out):
    n = lax.axis_size("tensor")
    total = cta.shape[2]
    tile = total // n
    wide, width = w_out.shape
    fixed = lambda *s: pl.BlockSpec(s, lambda r, me: (0, 0))
    out = pl.pallas_call(
        functools.partial(mid_kernel, n),
        grid_spec=pltpu.PrefetchScalarGridSpec(
            num_scalar_prefetch=1,
            grid=(n,),
            in_specs=[
                pl.BlockSpec((a.shape[0], HDIM, tile), lambda r, me: (0, 0, r ^ me[0]))
                for a in (cta, ctb)
            ]
            + near_far(n, tile, width)
            + [fixed(wide, width)]
            + [fixed(tile, width)] * n,
            out_specs=[fixed(tile, width)] * n + [fixed(wide, width)],
            scratch_shapes=[pltpu.VMEM((wide, width), f32)],
        ),
        out_shape=[jax.ShapeDtypeStruct((tile, width), bf16)] * n
        + [jax.ShapeDtypeStruct((wide, width), bf16)],
        compiler_params=pltpu.CompilerParams(vmem_limit_bytes=24 * 2**20),
        cost_estimate=pl.CostEstimate(
            flops=4 * total * wide * width, bytes_accessed=total * 8000, transcendentals=0
        ),
        name="mid",
    )(me, cta, ctb, *y_halves, w_out, *c_blocks)
    return out[:n], out[n]


def back_kernel(n, heads, me_ref, *refs):
    projs, (d0_ref, d1_ref, w_ref, vec_ref) = refs[:heads], refs[heads : heads + 4]
    x_refs, outs, sums_ref = refs[heads + 4 : heads + 4 + n], refs[heads + 4 + n : -1], refs[-1]
    step = pl.program_id(0)
    near = step < n // 2
    xhat, _ = normalize(pick_block(x_refs, step).astype(f32))
    dx = jnp.where(near, d0_ref[...], d1_ref[...]).astype(f32)

    @pl.when(step == 0)
    def _():
        sums_ref[...] = jnp.zeros_like(sums_ref)

    dn = dot_nt(jnp.concatenate([p[...] for p in projs], axis=1), w_ref[...])
    dx = (dx + dn * vec_ref[0:1, :]).astype(bf16)
    sums_ref[1:2, :] += jnp.sum(dn * xhat, axis=0, keepdims=True)
    sums_ref[2:3, :] += jnp.sum(dn, axis=0, keepdims=True)
    for j in range(n):
        @pl.when(step == j)
        def _(j=j):
            outs[j][...] = dx


def back(me, projs, x_blocks, d_halves, w_qkv, vectors):
    n = lax.axis_size("tensor")
    heads = len(projs)
    total, wide = projs[0].shape
    tile = total // n
    width = w_qkv.shape[0]
    fixed = lambda *s: pl.BlockSpec(s, lambda r, me: (0,) * len(s))
    out = pl.pallas_call(
        functools.partial(back_kernel, n, heads),
        grid_spec=pltpu.PrefetchScalarGridSpec(
            num_scalar_prefetch=1,
            grid=(n,),
            in_specs=[pl.BlockSpec((tile, wide), lambda r, me: (r ^ me[0], 0))] * heads
            + near_far(n, tile, width)
            + [fixed(*w_qkv.shape), fixed(*vectors.shape)]
            + [fixed(tile, width)] * n,
            out_specs=[fixed(tile, width)] * n + [fixed(8, width)],
        ),
        out_shape=[jax.ShapeDtypeStruct((tile, width), bf16)] * n
        + [jax.ShapeDtypeStruct((8, width), f32)],
        compiler_params=pltpu.CompilerParams(vmem_limit_bytes=28 * 2**20),
        cost_estimate=pl.CostEstimate(
            flops=2 * total * heads * wide * width, bytes_accessed=total * 8000, transcendentals=0
        ),
        name="back",
    )(me, *projs, *d_halves, w_qkv, vectors, *x_blocks)
    return out[:n], out[n]


def body(
    tokens,
    doc_lengths,
    w_qkv,
    b_qkv,
    w_out,
    w_up,
    b_up,
    w_down,
    out_bias,
    norm1_gain,
    norm1_shift,
    norm2_gain,
    norm2_shift,
    cotangent,
):
    row_count, width = tokens.shape
    n_tensor = lax.axis_size("tensor")
    total = row_count * n_tensor
    index = lax.axis_index("tensor")
    me = index.astype(jnp.int32).reshape(1)
    heads = w_out.shape[0] // HDIM
    slots = doc_lengths.shape[1]
    x_far = gather_far(tokens, "tensor")
    x_near = gather_near(tokens, "tensor")
    documents, positions = token_layout(doc_lengths[0], total, PADB)
    local_docs = lax.dynamic_slice_in_dim(documents, index * row_count, row_count)
    grad_send = jnp.where(local_docs[:, None] >= 0, cotangent, 0)
    c_near = gather_near(grad_send, "tensor")
    half = n_tensor // 2

    aux = aux_rows(documents, positions)
    gains = [norm1_gain, norm1_shift, norm2_gain, norm2_shift]
    vectors = jnp.stack(gains).astype(f32)
    b_up_row = b_up.astype(f32)[None]
    b_qkv_row = b_qkv.astype(f32)[None]

    mlp_args = (w_up, w_down, w_out, vectors, b_up_row)
    front_args = (w_qkv, b_qkv_row, vectors, aux, slots, heads)
    qkv, normed = front(me, 0, x_near, *front_args, None)
    c_near, qkv = tie(c_near, qkv)
    y0, d0, g, gu, gd, sums = mlp(me, 0, total, x_near, c_near, *mlp_args, None)
    x_far, grad_far, gu = tie(x_far, grad_send, gu)
    c_far = gather_far(grad_far, "tensor")
    x_far = gather_near(x_far, "tensor")
    qkv, normed = front(me, half, x_far, *front_args, [qkv, normed])
    kept_a = attend(qkv, 0, 1)
    c_far, e_a = tie(c_far, kept_a[1])
    kept_a = (kept_a[0], e_a, kept_a[2])
    c_far = gather_near(c_far, "tensor")
    y1, d1, g, gu, gd, sums = mlp(
        me, half, total, x_far, c_far, *mlp_args, [g, gu, gd, sums]
    )
    up_sum, down_sum = StagedSum(gu, "dp", 0), StagedSum(gd, "dp", 1)
    up_sum.send()
    down_sum.send()
    qkv, y1 = tie(qkv, y1)
    kept_b = attend(qkv, 1, heads - 1)
    ct_b = take_before(kept_b[0], up_sum, down_sum)
    up_sum.send()
    down_sum.send()
    y_blocks, grad_out = mid(me, kept_a[0], ct_b, c_near + c_far, [y0, y1], w_out)
    y_rows = ScatterSum(y_blocks, "tensor")
    y_rows.send()
    qkv, grad_out = tie(qkv, grad_out)
    p1, b1, q1 = attend_back(qkv, g, kept_b, aux, normed, 1, 0)
    qkv, p1 = take_before((qkv, p1), up_sum, down_sum, y_rows)
    up_sum.send()
    down_sum.send()
    y_rows.send()
    p2, b2, q2 = attend_back(qkv, g, kept_b, aux, normed, 2, 1)
    qkv, p2 = take_before((qkv, p2), up_sum, down_sum)
    up_sum.send()
    down_sum.send()
    early = StagedSum(jnp.concatenate([grad_out, q1, q2], axis=0), "dp", 0)
    early.send()
    p0, b0, q0 = attend_back(qkv, g, kept_a, aux, normed, 0, 0)
    p0, q0 = take_before((p0, q0), up_sum, down_sum, early, y_rows)
    late = StagedSum(q0, "dp", 0)
    late.send()
    early.send()
    up_sum.send()
    down_sum.send()
    dx_blocks, back_sums = back(me, [p0, p1, p2], x_near + x_far, [d0, d1], w_qkv, vectors)
    dx_rows = ScatterSum(dx_blocks, "tensor")
    dx_rows.send()
    grad_rows = grad_send.astype(f32)
    vec = jnp.concatenate(
        [jnp.sum(grad_rows, axis=0)[None], back_sums[1:3], sums[1:3]], axis=0
    )
    bias = jnp.stack([b0, b1, b2]).reshape(heads, 3, LANES)[:, :, :HDIM].reshape(-1)
    vec = SmallSum(vec, "tensor")
    vec.send()
    tok = back_sums[0]
    tok = take_before(tok, dx_rows, vec)
    dx_rows.send()
    vec.send()
    tok = take_before(tok, late, early)
    late.send()
    early.send()
    tok = take_before(tok, vec)
    vec.finish()
    share = width // n_tensor
    vec = lax.dynamic_slice_in_dim(vec.out, index * share, share, 1)
    small = SmallSum(jnp.concatenate([bias, sums[0], vec.reshape(-1)]), "dp")
    small.send()
    tok = take_before(tok, late, early, small)
    late.send()
    early.send()
    small.send()
    tok = take_before(tok, late, small)
    late.send()
    small.send()
    tok = take_before(tok, up_sum, down_sum)
    up_sum.send()
    down_sum.send()
    tok = take_before(tok, early, late, small)
    early.send()
    late.send()
    tok = take_before(tok, early, late)
    early.send()
    late.send()
    tok = take_before(tok, dx_rows, down_sum)
    tok = take_before(tok, late)
    tok = take_before(tok, up_sum)
    tok = take_before(tok, early)
    for rest in (late, early, up_sum, down_sum, small, y_rows, dx_rows):
        rest.finish()
    summed, dx, small = y_rows.out, dx_rows.out, small.out
    out_sum, early = early.out[: w_out.shape[0]], early.out[w_out.shape[0] :]
    qkv_sum = jnp.concatenate([late.out, early], axis=0).T
    up_sum, down_sum = up_sum.out, down_sum.out

    inputs = tokens.astype(f32)
    block_out = (inputs + out_bias.astype(f32) + summed).astype(bf16)
    xhat, inv = normalize(inputs)
    grad_input = grad_rows + inv * (
        dx
        - jnp.mean(dx, axis=-1, keepdims=True)
        - xhat * jnp.mean(dx * xhat, axis=-1, keepdims=True)
    )
    nq, nu = bias.shape[0], b_up.shape[0]
    return (
        block_out,
        grad_input,
        qkv_sum.astype(f32),
        small[:nq],
        out_sum.astype(f32),
        up_sum.astype(f32),
        small[nq : nq + nu],
        down_sum.astype(f32),
        small[nq + nu :].reshape(5, share),
    )


def solution(mesh):
    placed = (
        P(("dp", "tensor"), None),
        P("dp", None),
        P(None, "tensor"),
        P("tensor"),
        P("tensor", None),
        P(None, "tensor"),
        P("tensor"),
        P("tensor", None),
        P(),
        P(),
        P(),
        P(),
        P(),
        P(("dp", "tensor"), None),
    )
    return jax.shard_map(
        body,
        mesh=mesh,
        in_specs=placed,
        out_specs=(
            P(("dp", "tensor"), None),
            P(("dp", "tensor"), None),
            P(None, "tensor"),
            P("tensor"),
            P("tensor", None),
            P(None, "tensor"),
            P("tensor"),
            P("tensor", None),
            P(None, "tensor"),
        ),
        check_vma=False,
    )
```

```python
import functools

import jax
import jax.numpy as jnp
from jax import lax
from jax.experimental import pallas as pl
from jax.experimental.pallas import tpu as pltpu
from jax.sharding import PartitionSpec as P

HDIM = 64
ROT = 16
PADB = 128
LANES = 128
QB = 256
VMEM = 56 * 2**20
COST = 1.0

norm_eps = 1e-05
masked_fill = -1e30
rotary_base = 10000.0
f32 = jnp.float32
bf16 = jnp.bfloat16


def swap(values, axis, bit):
    n = lax.axis_size(axis)
    return lax.ppermute(values, axis, [(i, i ^ bit) for i in range(n)])


def gather_far(values, axis):
    return swap(values, axis, lax.axis_size(axis) // 2)


def gather_near(values, axis):
    blocks = {0: values}
    bit = lax.axis_size(axis) // 4
    while bit:
        for at in list(blocks):
            blocks[at | bit] = swap(blocks[at], axis, bit)
        bit //= 2
    return [blocks[j] for j in range(len(blocks))]


class ScatterSum:
    def __init__(self, blocks, axis):
        self.blocks, self.axis, self.got = blocks, axis, None
        self.bit = 1

    def send(self):
        bit = self.bit
        self.got = {
            j ^ bit: swap(b.astype(bf16), self.axis, bit)
            for j, b in self.blocks.items()
            if j & bit
        }

    def take(self):
        got = self.got
        self.blocks = {j: self.blocks[j].astype(f32) + got[j].astype(f32) for j in got}
        self.bit *= 2

    def finish(self, bits):
        while self.bit < bits:
            self.send()
            self.take()


class Exchange:
    def __init__(self, value, axis, bit):
        self.got = swap(value, axis, bit)

    def take(self):
        self.out = self.got


def axis_bits(axis, first):
    n = lax.axis_size(axis)
    bits = [1 << k for k in range(n.bit_length() - 1)]
    return bits[first:] + bits[:first]


def tie(first, *others):
    return lax.optimization_barrier((first,) + others)


def boundary(values, *sums):
    values, got = lax.optimization_barrier((values, [a.got for a in sums]))
    for a, g in zip(sums, got):
        a.got = g
        a.take()
    return values


class StagedSum:
    def __init__(self, values, axis, first):
        self.held, self.axis, self.got = [values.astype(bf16)], axis, None
        bits = axis_bits(axis, first)
        self.steps = [(b, True) for b in bits] + [(b, False) for b in reversed(bits)]

    def part(self, side):
        def cut(a):
            a = a.reshape((2, a.shape[0] // 2) + a.shape[1:])
            return lax.dynamic_index_in_dim(a, side, 0, keepdims=False)

        parts = self.held if side is None else [cut(a) for a in self.held]
        if len(parts) == 1:
            return parts[0]
        return (parts[0].astype(f32) + parts[1].astype(f32)).astype(bf16)

    def send(self):
        bit, halving = self.steps[0]
        side = (lax.axis_index(self.axis) // bit) % 2
        self.got = swap(self.part(1 - side if halving else None), self.axis, bit)

    def take(self):
        bit, halving = self.steps.pop(0)
        side = (lax.axis_index(self.axis) // bit) % 2
        if halving:
            self.held = [self.part(side), self.got]
        else:
            mine = self.part(None)
            if not self.steps:
                self.last = (mine, self.got, side)
                return
            low = jnp.where(side == 0, mine, self.got)
            high = jnp.where(side == 0, self.got, mine)
            self.held = [jnp.concatenate([low, high], axis=0)]

    def finish(self):
        while self.steps:
            self.send()
            self.take()

class SmallSum:
    def __init__(self, values, axis):
        self.out, self.axis, self.bits, self.got = values, axis, axis_bits(axis, 0), None

    def send(self):
        self.got = swap(self.out, self.axis, self.bits.pop(0))

    def take(self):
        self.out = self.out + self.got

    def finish(self):
        while self.bits:
            self.send()
            self.take()


def token_layout(lengths, total, pad_block):
    padded = (lengths + pad_block - 1) // pad_block * pad_block
    starts = jnp.cumsum(padded) - padded
    row_ids = jnp.arange(total, dtype=jnp.int32)
    inside = (row_ids[None, :] >= starts[:, None]) & (
        row_ids[None, :] < (starts + lengths)[:, None]
    )
    slot_ids = jnp.arange(lengths.shape[0], dtype=jnp.int32)
    documents = jnp.sum(jnp.where(inside, slot_ids[:, None] + 1, 0), axis=0) - 1
    offsets = jnp.sum(jnp.where(inside, starts[:, None], 0), axis=0)
    return (documents, row_ids - offsets)


def aux_rows(documents, positions):
    half = ROT // 2
    inverse = rotary_base ** (-(jnp.arange(half, dtype=f32) * 2.0 / ROT))
    angles = inverse[:, None] * positions.astype(f32)[None, :]
    docs = (documents + 1).astype(f32)[None, :]
    return jnp.concatenate(
        [jnp.cos(angles), jnp.sin(angles), docs, jnp.zeros((7, docs.shape[1]), f32)], axis=0
    )


def cost(flops, bytes_accessed, transcendentals):
    return pl.CostEstimate(
        flops=int(COST * flops),
        bytes_accessed=int(COST * bytes_accessed),
        transcendentals=transcendentals,
    )


def dot(left, right):
    return lax.dot_general(left, right, (((1,), (0,)), ((), ())), preferred_element_type=f32)


def dot_nt(left, right):
    return lax.dot_general(left, right, (((1,), (1,)), ((), ())), preferred_element_type=f32)


def normalize(x):
    center = jnp.mean(x, axis=-1, keepdims=True)
    off = x - center
    inv = lax.rsqrt(jnp.mean(off * off, axis=-1, keepdims=True) + norm_eps)
    return off * inv, inv


def pick_block(refs, step):
    out = refs[0][...]
    for j in range(1, len(refs)):
        out = jnp.where(step == j, refs[j][...], out)
    return out


def head_window(a, at):
    if at % LANES == 0:
        return a[:, at : at + LANES]
    return pltpu.roll(a[:, at - HDIM : at + HDIM], HDIM, 1)


def pad_lanes(a):
    extra = -a.shape[1] % LANES
    if extra == 0:
        return a
    return jnp.concatenate([a, jnp.zeros((a.shape[0], extra), a.dtype)], axis=1)


def lane_tables(aux):
    rows = aux.shape[1]
    half = ROT // 2
    t = jnp.concatenate([aux, jnp.zeros((LANES - aux.shape[0], rows), f32)], axis=0).T
    lane = lax.broadcasted_iota(jnp.int32, (rows, LANES), 1)
    cosine = jnp.where(lane < half, t, jnp.where(lane < ROT, pltpu.roll(t, half, 1), 1.0))
    up = jnp.where(lane < half, pltpu.roll(t, LANES - half, 1), 0.0)
    down = jnp.where((lane >= half) & (lane < ROT), t, 0.0)
    return cosine, up, down, t[:, ROT : ROT + 1], lane


def front_kernel(heads, slots, count, me_ref, *refs):
    w_ref, b_ref, vec_ref, aux_ref = refs[count : count + 4]
    qkv_ref, normed_ref = refs[-2:]
    half = ROT // 2
    x = pick_block(refs[:count], pl.program_id(0))
    xhat, _ = normalize(x.astype(f32))
    normed = (xhat * vec_ref[0:1, :] + vec_ref[1:2, :]).astype(bf16)
    normed_ref[...] = normed
    cosine, up, down, doc, lane = lane_tables(aux_ref[...])
    used = (lane >= HDIM) & (lane <= HDIM + slots)
    hit = (lane - HDIM).astype(f32) == doc
    key_side = jnp.where(used & hit, 1.0, 0.0)
    query_side = jnp.where(used & ~hit, masked_fill, 0.0)
    value_side = jnp.where((lane >= HDIM) & (lane < HDIM + 2), 1.0, 0.0)
    own = lane < HDIM
    proj = pad_lanes(dot(normed, w_ref[...]) + b_ref[...])
    for h in range(heads):
        for part in range(3):
            a = head_window(proj, (h * 3 + part) * HDIM)
            if part < 2:
                a = a * cosine - pltpu.roll(a, LANES - half, 1) * up + pltpu.roll(a, half, 1) * down
            if part == 0:
                a = jnp.where(own, a * HDIM**-0.5, query_side)
            else:
                a = jnp.where(own, a, key_side if part == 1 else value_side)
            qkv_ref[:, pl.ds((h * 3 + part) * LANES, LANES)] = a.astype(bf16)


def front(me, offset, blocks, w_qkv, b_qkv, vectors, aux, slots, heads, kept):
    tile, width = blocks[0].shape
    wide = heads * 3 * LANES
    whole = lambda a: pl.BlockSpec(a.shape, lambda r, me: (0, 0))
    args = blocks + [w_qkv, b_qkv, vectors, aux]
    specs = [whole(a) for a in args[:-1]]
    specs.append(pl.BlockSpec((aux.shape[0], tile), lambda r, me: (0, (r + offset) ^ me[0])))
    alias = {}
    if kept is not None:
        args += kept
        specs += [pl.BlockSpec(memory_space=pl.ANY)] * 2
        alias = {len(args) - 1: 0, len(args): 1}
    return pl.pallas_call(
        functools.partial(front_kernel, heads, slots, len(blocks)),
        grid_spec=pltpu.PrefetchScalarGridSpec(
            num_scalar_prefetch=1,
            grid=(len(blocks),),
            in_specs=specs,
            out_specs=[
                pl.BlockSpec((tile, wide), lambda r, me: ((r + offset) ^ me[0], 0)),
                pl.BlockSpec((tile, width), lambda r, me: ((r + offset) ^ me[0], 0)),
            ],
        ),
        out_shape=[
            pltpu.HBM((aux.shape[1], wide), bf16),
            pltpu.HBM((aux.shape[1], width), bf16),
        ],
        input_output_aliases=alias,
        compiler_params=pltpu.CompilerParams(vmem_limit_bytes=24 * 2**20),
        cost_estimate=cost(
            flops=4 * len(blocks) * tile * width * wide,
            bytes_accessed=len(blocks) * tile * 4000,
            transcendentals=0,
        ),
        name="front",
    )(me, *args)


def mlp_kernel(
    first, count, me_ref, *refs
):
    wu_ref, wd_ref, wo_ref, vec_ref, bu_ref = refs[2 * count : 2 * count + 5]
    rest = refs[2 * count + 5 :]
    y_ref, dx_ref, g_ref, c_out, gu_ref, gd_ref, sums_ref, up_acc, down_acc = rest[-9:]
    step = pl.program_id(0)

    @pl.when(step == 0)
    def _():
        if first:
            up_acc[...] = jnp.zeros_like(up_acc)
            down_acc[...] = jnp.zeros_like(down_acc)
            sums_ref[...] = jnp.zeros_like(sums_ref)
        else:
            up_acc[...] = rest[2][...].astype(f32)
            down_acc[...] = rest[3][...].astype(f32)
            sums_ref[...] = rest[4][...]

    xhat, _ = normalize(pick_block(refs[:count], step).astype(f32))
    normed = (xhat * vec_ref[2:3, :] + vec_ref[3:4, :]).astype(bf16)
    normed_t = normed.T
    c = pick_block(refs[count : 2 * count], step)
    c_out[...] = c
    g = pad_lanes(dot_nt(c, wo_ref[...]))
    own = lax.broadcasted_iota(jnp.int32, (c.shape[0], LANES), 1) < HDIM
    for h in range(g_ref.shape[1] // LANES):
        part = jnp.where(own, head_window(g, h * HDIM), 0.0)
        g_ref[:, pl.ds(h * LANES, LANES)] = part.astype(bf16)
    y = None
    hidden_width = wu_ref.shape[1]
    for at in range(0, hidden_width, QB):
        cols = pl.ds(at, QB)
        h = dot(normed, wu_ref[:, cols]) + bu_ref[:, cols]
        cdf = 0.5 + 0.5 * lax.erf(h * 0.5**0.5)
        pdf = jnp.exp(-0.5 * h * h) * (2.0 * jnp.pi) ** -0.5
        act = (h * cdf).astype(bf16)
        gh = dot_nt(c, wd_ref[cols, :]) * (cdf + h * pdf)
        sums_ref[0:1, cols] += jnp.sum(gh, axis=0, keepdims=True)
        gh = gh.astype(bf16)
        y_part = dot(act, wd_ref[cols, :])
        dn_part = dot_nt(gh, wu_ref[:, cols])
        y = y_part if y is None else y + y_part
        dn = dn_part if at == 0 else dn + dn_part
        down_acc[cols, :] += dot(act.T, c)
        up_acc[:, cols] += dot(normed_t, gh)
    y_ref[...] = y.astype(bf16)
    dx_ref[...] = (dn * vec_ref[2:3, :]).astype(bf16)
    sums_ref[1:2, :] += jnp.sum(dn * xhat, axis=0, keepdims=True)
    sums_ref[2:3, :] += jnp.sum(dn, axis=0, keepdims=True)

    @pl.when(step == pl.num_programs(0) - 1)
    def _():
        gu_ref[...] = up_acc[...].astype(gu_ref.dtype)
        gd_ref[...] = down_acc[...].astype(gd_ref.dtype)


def mlp(me, offset, total, x, c, w_up, w_down, w_out, vectors, b_up, kept):
    count = len(x)
    tile, width = x[0].shape
    rows = count * tile
    units = w_up.shape[1]
    wide = w_out.shape[0] // HDIM * LANES
    whole = lambda a: pl.BlockSpec(a.shape, lambda r, me: (0, 0))
    shaped = lambda *s: pl.BlockSpec(s, lambda r, me: (0, 0))
    row_block = pl.BlockSpec((tile, width), lambda r, me: (r, 0))
    args = x + c + [w_up, w_down, w_out, vectors, b_up]
    specs = [whole(a) for a in args]
    alias = {}
    first = kept is None
    if not first:
        args += kept
        specs += [pl.BlockSpec(memory_space=pl.ANY)] * 2 + [whole(a) for a in kept[2:]]
        alias = {2 * count + 6: 2, 2 * count + 7: 3}
    return pl.pallas_call(
        functools.partial(mlp_kernel, first, count),
        grid_spec=pltpu.PrefetchScalarGridSpec(
            num_scalar_prefetch=1,
            grid=(count,),
            in_specs=specs,
            out_specs=[
                row_block, row_block,
                pl.BlockSpec((tile, wide), lambda r, me: ((r + offset) ^ me[0], 0)),
                pl.BlockSpec((tile, width), lambda r, me: ((r + offset) ^ me[0], 0)),
                shaped(width, units), shaped(units, width), shaped(8, width),
            ],
            scratch_shapes=[pltpu.VMEM((width, units), f32), pltpu.VMEM((units, width), f32)],
        ),
        out_shape=[
            pltpu.HBM((rows, width), bf16),
            pltpu.HBM((rows, width), bf16),
            pltpu.HBM((total, wide), bf16),
            pltpu.HBM((total, width), bf16),
            pltpu.HBM((width, units), bf16),
            pltpu.HBM((units, width), bf16),
            pltpu.HBM((8, width), f32),
        ],
        input_output_aliases=alias,
        compiler_params=pltpu.CompilerParams(vmem_limit_bytes=40 * 2**20),
        cost_estimate=cost(
            flops=14 * rows * width * units, bytes_accessed=rows * 8000, transcendentals=0
        ),
        name="mlp",
    )(me, *args)


def block_rows_of(i):
    return i * (i + 1) // 2 * QB


def attend_kernel(me_ref, q_ref, k_ref, v_ref, ct_ref, e_ref, inv_ref, vt_ref, s_ref):
    total = q_ref.shape[0]
    vt_ref[...] = v_ref[...].T
    row_at = lax.broadcasted_iota(jnp.int32, (QB, QB), 0)
    col_at = lax.broadcasted_iota(jnp.int32, (QB, QB), 1)
    causal = row_at <= col_at
    for i in range(total // QB):
        here = pl.ds(i * QB, QB)
        reach = (i + 1) * QB
        base = block_rows_of(i)
        qt = q_ref[here, :].T
        top = None
        for j in range(i + 1):
            at = pl.ds(j * QB, QB)
            s = dot(k_ref[at, :], qt)
            if j == i:
                s = jnp.where(causal, s, masked_fill)
            s_ref[at, :] = s
            part = jnp.max(s.reshape(QB // 8, 8, QB), axis=0)
            top = part if top is None else jnp.maximum(top, part)
        top = jnp.max(top, axis=0, keepdims=True)
        for j in range(i + 1):
            e_ref[0, pl.ds(base + j * QB, QB), :] = jnp.exp(
                s_ref[pl.ds(j * QB, QB), :] - top
            ).astype(bf16)
        ct = dot(vt_ref[:, :reach], e_ref[0, base : base + reach, :])
        inv = 1.0 / ct[HDIM : HDIM + 1, :]
        ct_ref[0, :, here] = ct[:HDIM, :] * inv
        inv_ref[0, i : i + 1, :] = inv


def attend(me, qkv, start, heads):
    total = qkv.shape[0]
    pick = lambda p: pl.BlockSpec((total, LANES), lambda h, me: (0, (h + start) * 3 + p))
    deep = lambda *s: pl.BlockSpec((1,) + s, lambda h, me: (h, 0, 0))
    blocks = total // QB
    kept = block_rows_of(blocks)
    return pl.pallas_call(
        attend_kernel,
        grid_spec=pltpu.PrefetchScalarGridSpec(
            num_scalar_prefetch=1,
            grid=(heads,),
            in_specs=[pick(0), pick(1), pick(2)],
            out_specs=[deep(HDIM, total), deep(kept, QB), deep(blocks, QB)],
            scratch_shapes=[pltpu.VMEM((LANES, total), bf16), pltpu.VMEM((total, QB), f32)],
        ),
        out_shape=[
            pltpu.HBM((heads, HDIM, total), f32),
            pltpu.HBM((heads, kept, QB), bf16),
            pltpu.HBM((heads, blocks, QB), f32),
        ],
        compiler_params=pltpu.CompilerParams(vmem_limit_bytes=36 * 2**20),
        cost_estimate=cost(
            flops=heads * kept * 3 * 2 * QB**2, bytes_accessed=heads * kept * 600, transcendentals=0
        ),
        name="attend",
    )(me, qkv, qkv, qkv)


def attend_back_kernel(
    me_ref, q_ref, k_ref, v_ref, g_ref, ct_ref, inv_ref, aux_ref, e_ref, normed_hbm,
    w_ref, vec_ref, c_hbm, proj_ref, bias_ref, grad_ref, norm_ref,
    kt_ref, d_ref, dk_ref, dv_ref, normed_ref, c_ref, sems,
):
    copies = [
        pltpu.make_async_copy(normed_hbm, normed_ref, sems.at[0]),
        pltpu.make_async_copy(c_hbm, c_ref, sems.at[1]),
    ]

    @pl.when(pl.program_id(0) == 0)
    def _():
        for copy in copies:
            copy.start()

    total = q_ref.shape[0]
    half = ROT // 2
    kt_ref[...] = k_ref[...].T
    feature = lax.broadcasted_iota(jnp.int32, (LANES, QB), 0)
    bias_q = jnp.zeros((1, LANES), f32)
    for i in range(total // QB):
        here = pl.ds(i * QB, QB)
        reach = (i + 1) * QB
        base = block_rows_of(i)
        qt = q_ref[here, :].T.astype(f32)
        gt = g_ref[here, :].T.astype(f32)
        inv = inv_ref[0, i : i + 1, :]
        less = -jnp.sum(gt[:HDIM, :] * ct_ref[0, :, here], axis=0, keepdims=True)
        less_hi = less.astype(bf16).astype(f32)
        ge = jnp.where(feature == HDIM, less_hi, gt)
        ge = jnp.where(feature == HDIM + 1, less - less_hi, ge).astype(bf16)
        gl = (gt * inv).T.astype(bf16)
        ql = jnp.where(feature < HDIM, qt * inv, 0.0).T.astype(bf16)
        for j in range(i + 1):
            at = pl.ds(j * QB, QB)
            e = e_ref[0, pl.ds(base + j * QB, QB), :]
            d = (e.astype(f32) * dot(v_ref[at, :], ge)).astype(bf16)
            d_ref[at, :] = d
            dv = dot(e, gl)
            dk = dot(d, ql)
            if j == i:
                dv_ref[at, :] = dv
                dk_ref[at, :] = dk
            else:
                dv_ref[at, :] += dv
                dk_ref[at, :] += dk
        dqt = dot(kt_ref[:, :reach], d_ref[:reach, :]) * (inv * HDIM**-0.5)
        c, s = aux_ref[:half, here], aux_ref[half:ROT, here]
        low, high = dqt[:half, :], dqt[half:ROT, :]
        dqt = jnp.concatenate(
            [low * c + high * s, high * c - low * s, dqt[ROT:HDIM, :],
             jnp.zeros((LANES - HDIM, QB), f32)], axis=0
        )
        dq = dqt.T
        bias_q += jnp.sum(dq, axis=0, keepdims=True)
        proj_ref[0, here, :HDIM] = dq[:, :HDIM].astype(bf16)
    bias_k = jnp.zeros((1, LANES), f32)
    bias_v = jnp.zeros((1, LANES), f32)
    for i in range(total // QB):
        here = pl.ds(i * QB, QB)
        cosine, up, down, _, _ = lane_tables(aux_ref[:, here])
        dk = dk_ref[here, :]
        dk = dk * cosine + pltpu.roll(dk, LANES - half, 1) * up - pltpu.roll(dk, half, 1) * down
        dv = dv_ref[here, :]
        bias_k += jnp.sum(dk, axis=0, keepdims=True)
        bias_v += jnp.sum(dv, axis=0, keepdims=True)
        proj_ref[0, here, HDIM : 2 * HDIM] = dk[:, :HDIM].astype(bf16)
        proj_ref[0, here, 2 * HDIM :] = dv[:, :HDIM].astype(bf16)
    bias_ref[0] = jnp.concatenate([bias_q, bias_k, bias_v], axis=1)
    @pl.when(pl.program_id(0) == 0)
    def _():
        for copy in copies:
            copy.wait()

    proj = proj_ref[0]
    grad = lax.dot_general(
        proj, normed_ref[...], (((0,), (0,)), ((), ())), preferred_element_type=f32
    )
    grad_ref[0, :HDIM, :] = dot(ct_ref[0].astype(bf16), c_ref[...]).astype(bf16)
    grad_ref[0, HDIM:, :] = grad.astype(bf16)
    column = lax.dot_general(
        proj, jnp.ones((total, LANES), bf16), (((0,), (0,)), ((), ())),
        preferred_element_type=f32,
    )[:, :1]
    weight = w_ref[0].astype(f32)
    shift = jnp.sum(weight * column, axis=0, keepdims=True)
    gain = jnp.sum(weight * grad, axis=0, keepdims=True) - shift * vec_ref[1:2, :]
    norm_ref[0] = jnp.concatenate([gain / vec_ref[0:1, :], shift], axis=0)


def attend_back(me, qkv, grad_ctx, kept, aux, normed, w_heads, vectors, c_all, start, count):
    ct, e, inv = kept
    total, width = normed.shape
    pick = lambda p: pl.BlockSpec((total, LANES), lambda h, me: (0, (h + start) * 3 + p))
    deep = lambda a: pl.BlockSpec((1,) + a.shape[1:], lambda h, me: (h + start, 0, 0))
    whole = lambda a: pl.BlockSpec(a.shape, lambda h, me: (0, 0))
    out = lambda *s: pl.BlockSpec((1,) + s, lambda h, me: (h, 0, 0))
    return pl.pallas_call(
        attend_back_kernel,
        grid_spec=pltpu.PrefetchScalarGridSpec(
            num_scalar_prefetch=1,
            grid=(count,),
            in_specs=[
                pick(0), pick(1), pick(2),
                pl.BlockSpec((total, LANES), lambda h, me: (0, h + start)),
                deep(ct), deep(inv), whole(aux), deep(e),
                pl.BlockSpec(memory_space=pl.ANY),
                deep(w_heads), whole(vectors),
                pl.BlockSpec(memory_space=pl.ANY),
            ],
            out_specs=[
                out(total, 3 * HDIM), out(1, 3 * LANES), out(4 * HDIM, width), out(2, width),
            ],
            scratch_shapes=[
                pltpu.VMEM((LANES, total), bf16),
                pltpu.VMEM((total, QB), bf16),
                pltpu.VMEM((total, LANES), f32),
                pltpu.VMEM((total, LANES), f32),
                pltpu.VMEM((total, width), bf16),
                pltpu.VMEM((total, width), bf16),
                pltpu.SemaphoreType.DMA((2,)),
            ],
        ),
        out_shape=[
            pltpu.HBM((count, total, 3 * HDIM), bf16),
            pltpu.HBM((count, 1, 3 * LANES), f32),
            pltpu.HBM((count, 4 * HDIM, width), bf16),
            pltpu.HBM((count, 2, width), f32),
        ],
        compiler_params=pltpu.CompilerParams(vmem_limit_bytes=VMEM),
        cost_estimate=cost(
            flops=count * e.shape[1] * 6 * 2 * QB**2,
            bytes_accessed=count * e.shape[1] * 600,
            transcendentals=0,
        ),
        name="attend_back",
    )(me, qkv, qkv, qkv, grad_ctx, ct, inv, aux, e, normed, w_heads, vectors, c_all)


def mid_kernel(n, me_ref, ct_ref, y0_ref, y1_ref, wo_ref, *outs):
    step = pl.program_id(0)
    y = jnp.where(step < n // 2, y0_ref[...], y1_ref[...]).astype(f32)
    ct = ct_ref[...].reshape(wo_ref.shape[0], y.shape[0]).astype(bf16)
    y = (y + dot(ct.T, wo_ref[...])).astype(bf16)
    for j in range(n):
        @pl.when(step == j)
        def _(j=j):
            outs[j][...] = y


def near_far(n, tile, width):
    half = n // 2
    return [
        pl.BlockSpec((tile, width), lambda r, me: (jnp.minimum(r, half - 1), 0)),
        pl.BlockSpec((tile, width), lambda r, me: (jnp.maximum(r - half, 0), 0)),
    ]


def mid(me, ct, y_halves, w_out):
    n = lax.axis_size("tensor")
    heads, _, total = ct.shape
    tile = total // n
    wide, width = w_out.shape
    fixed = lambda *s: pl.BlockSpec(s, lambda r, me: (0, 0))
    return pl.pallas_call(
        functools.partial(mid_kernel, n),
        grid_spec=pltpu.PrefetchScalarGridSpec(
            num_scalar_prefetch=1,
            grid=(n,),
            in_specs=[pl.BlockSpec((heads, HDIM, tile), lambda r, me: (0, 0, r ^ me[0]))]
            + near_far(n, tile, width)
            + [fixed(wide, width)],
            out_specs=[fixed(tile, width)] * n,
        ),
        out_shape=[pltpu.HBM((tile, width), bf16)] * n,
        compiler_params=pltpu.CompilerParams(vmem_limit_bytes=VMEM),
        cost_estimate=cost(
            flops=2 * total * wide * width, bytes_accessed=total * 8000, transcendentals=0
        ),
        name="mid",
    )(me, ct, *y_halves, w_out)


def back_kernel(count, me_ref, pa_ref, pb_ref, d_ref, w_ref, vec_ref, *outs):
    step = pl.program_id(0)
    dn = None
    for h, p in enumerate([r[h] for r in (pa_ref, pb_ref) for h in range(r.shape[0])]):
        part = dot(p, w_ref[h])
        dn = part if dn is None else dn + part
    dx = (d_ref[...].astype(f32) + dn * vec_ref[0:1, :]).astype(bf16)
    for j in range(count):
        @pl.when(step == j)
        def _(j=j):
            outs[j][...] = dx


def back(me, offset, proj_a, proj_b, d, w_heads, vectors):
    tile = proj_a.shape[1] // lax.axis_size("tensor")
    rows, width = d.shape
    count = rows // tile
    fixed = lambda *s: pl.BlockSpec(s, lambda r, me: (0,) * len(s))
    rows_of = lambda a: pl.BlockSpec(
        (a.shape[0], tile, a.shape[2]), lambda r, me: (0, (r + offset) ^ me[0], 0)
    )
    return pl.pallas_call(
        functools.partial(back_kernel, count),
        grid_spec=pltpu.PrefetchScalarGridSpec(
            num_scalar_prefetch=1,
            grid=(count,),
            in_specs=[rows_of(proj_a), rows_of(proj_b)]
            + [pl.BlockSpec((tile, width), lambda r, me: (r, 0))]
            + [fixed(*w_heads.shape), fixed(*vectors.shape)],
            out_specs=[fixed(tile, width)] * count,
        ),
        out_shape=[pltpu.HBM((tile, width), bf16)] * count,
        compiler_params=pltpu.CompilerParams(vmem_limit_bytes=VMEM),
        cost_estimate=cost(
            flops=1000, bytes_accessed=1000, transcendentals=0
        ),
        name="back",
    )(me, proj_a, proj_b, d, w_heads, vectors)


def join_kernel(count, side_ref, *refs):
    step = pl.program_id(0)
    for k in range(count):
        mine, got, out = refs[2 * k], refs[2 * k + 1], refs[2 * count + k]
        out[...] = jnp.where(step == 0, mine[...], got[...]).astype(f32)


def join(sums):
    count = len(sums)
    rows, width = sums[0].last[0].shape
    sides = jnp.stack([a.last[2] for a in sums]).astype(jnp.int32)
    whole = pl.BlockSpec((rows, width), lambda r, side: (0, 0))
    return pl.pallas_call(
        functools.partial(join_kernel, count),
        grid_spec=pltpu.PrefetchScalarGridSpec(
            num_scalar_prefetch=1,
            grid=(2,),
            in_specs=[whole] * (2 * count),
            out_specs=[
                pl.BlockSpec((rows, width), lambda r, side, k=k: (r ^ side[k], 0))
                for k in range(count)
            ],
        ),
        out_shape=[jax.ShapeDtypeStruct((2 * rows, width), f32)] * count,
        compiler_params=pltpu.CompilerParams(vmem_limit_bytes=24 * 2**20),
        name="join",
    )(sides, *[a for b in sums for a in b.last[:2]])


def assemble_kernel(heads, side_ref, mine_ref, got_ref, out_ref, qkv_ref, all_ref):
    rows = mine_ref.shape[0]
    all_ref[pl.ds(pl.multiple_of(side_ref[0] * rows, 8), rows), :] = mine_ref[...].astype(f32)
    all_ref[pl.ds(pl.multiple_of((1 - side_ref[0]) * rows, 8), rows), :] = got_ref[...].astype(f32)
    tall = 4 * HDIM
    for h in range(heads):
        out_ref[h * HDIM : (h + 1) * HDIM, :] = all_ref[h * tall : h * tall + HDIM, :]
    parts = [all_ref[h * tall + HDIM : (h + 1) * tall, :] for h in range(heads)]
    qkv_ref[...] = jnp.concatenate(parts, axis=0).T


def assemble(total, heads):
    mine, got, side = total.last
    rows, width = mine.shape
    whole = lambda *s: pl.BlockSpec(s, lambda r, side: (0, 0))
    return pl.pallas_call(
        functools.partial(assemble_kernel, heads),
        grid_spec=pltpu.PrefetchScalarGridSpec(
            num_scalar_prefetch=1,
            grid=(1,),
            in_specs=[whole(rows, width)] * 2,
            out_specs=[whole(heads * HDIM, width), whole(width, heads * 3 * HDIM)],
            scratch_shapes=[pltpu.VMEM((2 * rows, width), f32)],
        ),
        out_shape=[
            jax.ShapeDtypeStruct((heads * HDIM, width), f32),
            jax.ShapeDtypeStruct((width, heads * 3 * HDIM), f32),
        ],
        compiler_params=pltpu.CompilerParams(vmem_limit_bytes=24 * 2**20),
        name="assemble",
    )(side.astype(jnp.int32).reshape(1), mine, got)


def body(
    tokens,
    doc_lengths,
    w_qkv,
    b_qkv,
    w_out,
    w_up,
    b_up,
    w_down,
    out_bias,
    norm1_gain,
    norm1_shift,
    norm2_gain,
    norm2_shift,
    cotangent,
):
    row_count, width = tokens.shape
    n_tensor = lax.axis_size("tensor")
    total = row_count * n_tensor
    index = lax.axis_index("tensor")
    me = index.astype(jnp.int32).reshape(1)
    heads = w_out.shape[0] // HDIM
    slots = doc_lengths.shape[1]
    x_far = gather_far(tokens, "tensor")
    x_near = gather_near(tokens, "tensor")
    documents, positions = token_layout(doc_lengths[0], total, PADB)
    local_docs = lax.dynamic_slice_in_dim(documents, index * row_count, row_count)
    grad_send = jnp.where(local_docs[:, None] >= 0, cotangent, 0)
    c_near = gather_near(grad_send, "tensor")
    half = n_tensor // 2

    aux = aux_rows(documents, positions)
    gains = [norm1_gain, norm1_shift, norm2_gain, norm2_shift]
    vectors = jnp.stack(gains).astype(f32)
    b_up_row = b_up.astype(f32)[None]
    w_heads = w_qkv.T.reshape(heads, 3 * HDIM, width)
    b_qkv_row = b_qkv.astype(f32)[None]

    mlp_args = (w_up, w_down, w_out, vectors, b_up_row)
    front_args = (w_qkv, b_qkv_row, vectors, aux, slots, heads)
    qkv, normed = front(me, 0, x_near, *front_args, None)
    me, grad_far, qkv, normed = tie(me, grad_send, qkv, normed)
    c_far = gather_far(grad_far, "tensor")
    y0, d0, g, c_all, gu, gd, sums = mlp(me, 0, total, x_near, c_near, *mlp_args, None)
    x_far, me, y0, d0, g, c_all, gu, gd, sums = tie(x_far, me, y0, d0, g, c_all, gu, gd, sums)
    x_far = gather_near(x_far, "tensor")
    qkv, normed = front(me, half, x_far, *front_args, [qkv, normed])
    me, qkv, normed = tie(me, qkv, normed)
    kept = attend(me, qkv, 0, heads)
    c_far, me, kept = tie(c_far, me, kept)
    c_far = gather_near(c_far, "tensor")
    y1, d1, g, c_all, gu, gd, sums = mlp(
        me, half, total, x_far, c_far, *mlp_args, [g, c_all, gu, gd, sums]
    )
    me, y1, d1, g, c_all, gu, gd, sums = tie(me, y1, d1, g, c_all, gu, gd, sums)
    up, down = StagedSum(gu, "dp", 0), StagedSum(gd, "dp", 1)
    up.send()
    down.send()
    ab_args = (qkv, g, kept, aux, normed, w_heads, vectors, c_all)
    pa, ba, qa, na = attend_back(me, *ab_args, 0, 1)
    me, pa, ba, qa, na = boundary((me, pa, ba, qa, na), up, down)
    up.send()
    down.send()
    pb, bb, qb, nb = attend_back(me, *ab_args, 1, heads - 1)
    me, pb, bb, qb, nb, grad_rows = boundary((me, pb, bb, qb, nb, grad_send), up, down)
    up.send()
    down.send()
    rows = jnp.concatenate([qa, qb], axis=0).reshape(heads * 4 * HDIM, width)
    attn = StagedSum(rows, "dp", 0)
    attn.send()
    grad_rows = grad_rows.astype(f32)
    vec = jnp.concatenate(
        [
            jnp.sum(grad_rows, axis=0)[None],
            jnp.sum(na, axis=0) + jnp.sum(nb, axis=0),
            sums[1:3],
        ],
        axis=0,
    )
    vec = SmallSum(vec, "tensor")
    vec.send()
    far_blocks = back(me, half, pa, pb, d1, w_heads, vectors)
    me, far_blocks = boundary((me, far_blocks), vec)
    far_rows = ScatterSum(dict(enumerate(far_blocks)), "tensor")
    far_rows.send()
    vec.send()
    me = boundary(me, far_rows)
    far_rows.finish(half)
    cross = Exchange(far_rows.blocks[0].astype(bf16), "tensor", half)
    near_blocks = back(me, 0, pa, pb, d0, w_heads, vectors)
    me, near_blocks = boundary((me, near_blocks), up, down, attn)
    near_rows = ScatterSum(dict(enumerate(near_blocks)), "tensor")
    near_rows.send()
    attn.send()
    up.send()
    down.send()
    y_blocks = mid(me, kept[0], [y0, y1], w_out)
    tok, y_blocks = boundary((me, y_blocks), attn, up, down, near_rows, vec, cross)
    near_rows.finish(half)
    vec.finish()
    y_rows = ScatterSum(dict(enumerate(y_blocks)), "tensor")
    y_rows.send()
    attn.send()
    up.send()
    down.send()
    share = width // n_tensor
    vec = lax.dynamic_slice_in_dim(vec.out, index * share, share, 1)
    bias = jnp.concatenate([ba, bb]).reshape(heads, 3, LANES)[:, :, :HDIM].reshape(-1)
    small = SmallSum(jnp.concatenate([bias, sums[0], vec.reshape(-1)]), "dp")
    small.send()
    tok = boundary(tok, attn, small, y_rows)
    attn.send()
    small.send()
    y_rows.send()
    dx = near_rows.blocks[0].astype(f32) + cross.out.astype(f32)
    inputs = tokens.astype(f32)
    xhat, inv = normalize(inputs)
    grad_input = grad_rows + inv * (
        dx
        - jnp.mean(dx, axis=-1, keepdims=True)
        - xhat * jnp.mean(dx * xhat, axis=-1, keepdims=True)
    )
    tok, grad_input = boundary((tok, grad_input), attn, small, up, down)
    attn.send()
    up.send()
    down.send()
    small.send()
    tok = boundary(tok, attn, small)
    attn.send()
    tok = boundary(tok, up, down)
    up.finish()
    down.finish()
    up_sum, down_sum = join([up, down])
    tok, up_sum, down_sum = boundary((tok, up_sum, down_sum), y_rows)
    block_out = inputs + out_bias.astype(f32) + y_rows.blocks[0].astype(f32)
    block_out = block_out.astype(bf16)
    tok, block_out = boundary((tok, block_out), attn)
    attn.finish()
    small.finish()
    small = small.out
    out_sum, qkv_sum = assemble(attn, heads)
    nq, nu = bias.shape[0], b_up.shape[0]
    return (
        block_out,
        grad_input,
        qkv_sum,
        small[:nq],
        out_sum,
        up_sum,
        small[nq : nq + nu],
        down_sum,
        small[nq + nu :].reshape(5, share),
    )


def solution(mesh):
    placed = (
        P(("dp", "tensor"), None),
        P("dp", None),
        P(None, "tensor"),
        P("tensor"),
        P("tensor", None),
        P(None, "tensor"),
        P("tensor"),
        P("tensor", None),
        P(),
        P(),
        P(),
        P(),
        P(),
        P(("dp", "tensor"), None),
    )
    return jax.shard_map(
        body,
        mesh=mesh,
        in_specs=placed,
        out_specs=(
            P(("dp", "tensor"), None),
            P(("dp", "tensor"), None),
            P(None, "tensor"),
            P("tensor"),
            P("tensor", None),
            P(None, "tensor"),
            P("tensor"),
            P("tensor", None),
            P(None, "tensor"),
        ),
        check_vma=False,
    )
```

```python
import functools

import jax
import jax.numpy as jnp
from jax import lax
from jax.experimental import pallas as pl
from jax.experimental.pallas import tpu as pltpu
from jax.sharding import PartitionSpec as P

HDIM = 64
ROT = 16
PADB = 128
LANES = 128
QB = 256
VMEM = 56 * 2**20
COST = 1.0

norm_eps = 1e-05
masked_fill = -1e30
rotary_base = 10000.0
f32 = jnp.float32
bf16 = jnp.bfloat16


def swap(values, axis, bit):
    n = lax.axis_size(axis)
    return lax.ppermute(values, axis, [(i, i ^ bit) for i in range(n)])


def gather_far(values, axis):
    return swap(values, axis, lax.axis_size(axis) // 2)


def gather_near(values, axis):
    blocks = {0: values}
    bit = lax.axis_size(axis) // 4
    while bit:
        for at in list(blocks):
            blocks[at | bit] = swap(blocks[at], axis, bit)
        bit //= 2
    return [blocks[j] for j in range(len(blocks))]


class ScatterSum:
    def __init__(self, blocks, axis):
        self.blocks, self.axis, self.got = blocks, axis, None
        self.bit = 1

    def send(self):
        bit = self.bit
        self.got = {
            j ^ bit: swap(b.astype(bf16), self.axis, bit)
            for j, b in self.blocks.items()
            if j & bit
        }

    def take(self):
        got = self.got
        self.blocks = {j: self.blocks[j].astype(f32) + got[j].astype(f32) for j in got}
        self.bit *= 2

    def finish(self, bits):
        while self.bit < bits:
            self.send()
            self.take()


class Exchange:
    def __init__(self, value, axis, bit):
        self.got = swap(value, axis, bit)

    def take(self):
        self.out = self.got


def axis_bits(axis, first):
    n = lax.axis_size(axis)
    bits = [1 << k for k in range(n.bit_length() - 1)]
    return bits[first:] + bits[:first]


def tie(first, *others):
    return lax.optimization_barrier((first,) + others)


def boundary(values, *sums):
    values, got = lax.optimization_barrier((values, [a.got for a in sums]))
    for a, g in zip(sums, got):
        a.got = g
        a.take()
    return values


class StagedSum:
    def __init__(self, values, axis, first):
        self.held, self.axis, self.got = [values.astype(bf16)], axis, None
        bits = axis_bits(axis, first)
        self.steps = [(b, True) for b in bits] + [(b, False) for b in reversed(bits)]

    def part(self, side):
        def cut(a):
            a = a.reshape((2, a.shape[0] // 2) + a.shape[1:])
            return lax.dynamic_index_in_dim(a, side, 0, keepdims=False)

        parts = self.held if side is None else [cut(a) for a in self.held]
        if len(parts) == 1:
            return parts[0]
        return (parts[0].astype(f32) + parts[1].astype(f32)).astype(bf16)

    def send(self):
        bit, halving = self.steps[0]
        side = (lax.axis_index(self.axis) // bit) % 2
        self.got = swap(self.part(1 - side if halving else None), self.axis, bit)

    def take(self):
        bit, halving = self.steps.pop(0)
        side = (lax.axis_index(self.axis) // bit) % 2
        if halving:
            self.held = [self.part(side), self.got]
        else:
            mine = self.part(None)
            if not self.steps:
                self.last = (mine, self.got, side)
                return
            low = jnp.where(side == 0, mine, self.got)
            high = jnp.where(side == 0, self.got, mine)
            self.held = [jnp.concatenate([low, high], axis=0)]

    def finish(self):
        while self.steps:
            self.send()
            self.take()

class SmallSum:
    def __init__(self, values, axis):
        self.out, self.axis, self.bits, self.got = values, axis, axis_bits(axis, 0), None

    def send(self):
        self.got = swap(self.out, self.axis, self.bits.pop(0))

    def take(self):
        self.out = self.out + self.got

    def finish(self):
        while self.bits:
            self.send()
            self.take()


def token_layout(lengths, total, pad_block):
    padded = (lengths + pad_block - 1) // pad_block * pad_block
    starts = jnp.cumsum(padded) - padded
    row_ids = jnp.arange(total, dtype=jnp.int32)
    inside = (row_ids[None, :] >= starts[:, None]) & (
        row_ids[None, :] < (starts + lengths)[:, None]
    )
    slot_ids = jnp.arange(lengths.shape[0], dtype=jnp.int32)
    documents = jnp.sum(jnp.where(inside, slot_ids[:, None] + 1, 0), axis=0) - 1
    offsets = jnp.sum(jnp.where(inside, starts[:, None], 0), axis=0)
    return (documents, row_ids - offsets)


def aux_rows(documents, positions):
    half = ROT // 2
    inverse = rotary_base ** (-(jnp.arange(half, dtype=f32) * 2.0 / ROT))
    angles = inverse[:, None] * positions.astype(f32)[None, :]
    docs = (documents + 1).astype(f32)[None, :]
    return jnp.concatenate(
        [jnp.cos(angles), jnp.sin(angles), docs, jnp.zeros((7, docs.shape[1]), f32)], axis=0
    )


def cost(flops, bytes_accessed, transcendentals):
    return pl.CostEstimate(
        flops=int(COST * flops),
        bytes_accessed=int(COST * bytes_accessed),
        transcendentals=transcendentals,
    )


def dot(left, right):
    return lax.dot_general(left, right, (((1,), (0,)), ((), ())), preferred_element_type=f32)


def dot_nt(left, right):
    return lax.dot_general(left, right, (((1,), (1,)), ((), ())), preferred_element_type=f32)


def normalize(x):
    center = jnp.mean(x, axis=-1, keepdims=True)
    off = x - center
    inv = lax.rsqrt(jnp.mean(off * off, axis=-1, keepdims=True) + norm_eps)
    return off * inv, inv


def pick_block(refs, step):
    out = refs[0][...]
    for j in range(1, len(refs)):
        out = jnp.where(step == j, refs[j][...], out)
    return out


def head_window(a, at):
    if at % LANES == 0:
        return a[:, at : at + LANES]
    return pltpu.roll(a[:, at - HDIM : at + HDIM], HDIM, 1)


def pad_lanes(a):
    extra = -a.shape[1] % LANES
    if extra == 0:
        return a
    return jnp.concatenate([a, jnp.zeros((a.shape[0], extra), a.dtype)], axis=1)


def lane_tables(aux):
    rows = aux.shape[1]
    half = ROT // 2
    t = jnp.concatenate([aux, jnp.zeros((LANES - aux.shape[0], rows), f32)], axis=0).T
    lane = lax.broadcasted_iota(jnp.int32, (rows, LANES), 1)
    cosine = jnp.where(lane < half, t, jnp.where(lane < ROT, pltpu.roll(t, half, 1), 1.0))
    up = jnp.where(lane < half, pltpu.roll(t, LANES - half, 1), 0.0)
    down = jnp.where((lane >= half) & (lane < ROT), t, 0.0)
    return cosine, up, down, t[:, ROT : ROT + 1], lane


def front_kernel(heads, slots, count, me_ref, *refs):
    w_ref, b_ref, vec_ref, aux_ref = refs[count : count + 4]
    qkv_ref, normed_ref = refs[-2:]
    half = ROT // 2
    x = pick_block(refs[:count], pl.program_id(0))
    xhat, _ = normalize(x.astype(f32))
    normed = (xhat * vec_ref[0:1, :] + vec_ref[1:2, :]).astype(bf16)
    normed_ref[...] = normed
    cosine, up, down, doc, lane = lane_tables(aux_ref[...])
    used = (lane >= HDIM) & (lane <= HDIM + slots)
    hit = (lane - HDIM).astype(f32) == doc
    key_side = jnp.where(used & hit, 1.0, 0.0)
    query_side = jnp.where(used & ~hit, masked_fill, 0.0)
    value_side = jnp.where((lane >= HDIM) & (lane < HDIM + 2), 1.0, 0.0)
    own = lane < HDIM
    proj = pad_lanes(dot_nt(normed, w_ref[...]) + b_ref[...])
    for h in range(heads):
        for part in range(3):
            a = head_window(proj, (h * 3 + part) * HDIM)
            if part < 2:
                a = a * cosine - pltpu.roll(a, LANES - half, 1) * up + pltpu.roll(a, half, 1) * down
            if part == 0:
                a = jnp.where(own, a * HDIM**-0.5, query_side)
            else:
                a = jnp.where(own, a, key_side if part == 1 else value_side)
            qkv_ref[:, pl.ds((h * 3 + part) * LANES, LANES)] = a.astype(bf16)


def front(me, offset, blocks, w_turned, b_qkv, vectors, aux, slots, heads, kept):
    tile, width = blocks[0].shape
    wide = heads * 3 * LANES
    whole = lambda a: pl.BlockSpec(a.shape, lambda r, me: (0, 0))
    args = blocks + [w_turned, b_qkv, vectors, aux]
    specs = [whole(a) for a in args[:-1]]
    specs.append(pl.BlockSpec((aux.shape[0], tile), lambda r, me: (0, (r + offset) ^ me[0])))
    alias = {}
    if kept is not None:
        args += kept
        specs += [pl.BlockSpec(memory_space=pl.ANY)] * 2
        alias = {len(args) - 1: 0, len(args): 1}
    return pl.pallas_call(
        functools.partial(front_kernel, heads, slots, len(blocks)),
        grid_spec=pltpu.PrefetchScalarGridSpec(
            num_scalar_prefetch=1,
            grid=(len(blocks),),
            in_specs=specs,
            out_specs=[
                pl.BlockSpec((tile, wide), lambda r, me: ((r + offset) ^ me[0], 0)),
                pl.BlockSpec((tile, width), lambda r, me: ((r + offset) ^ me[0], 0)),
            ],
        ),
        out_shape=[
            pltpu.HBM((aux.shape[1], wide), bf16),
            pltpu.HBM((aux.shape[1], width), bf16),
        ],
        input_output_aliases=alias,
        compiler_params=pltpu.CompilerParams(vmem_limit_bytes=24 * 2**20),
        cost_estimate=cost(
            flops=4 * len(blocks) * tile * width * wide,
            bytes_accessed=len(blocks) * tile * 4000,
            transcendentals=0,
        ),
        name="front",
    )(me, *args)


def mlp_kernel(
    first, count, me_ref, *refs
):
    wu_ref, wd_ref, wo_ref, vec_ref, bu_ref = refs[2 * count : 2 * count + 5]
    rest = refs[2 * count + 5 :]
    y_ref, dx_ref, g_ref, c_out, gu_ref, gd_ref, sums_ref, up_acc, down_acc = rest[-9:]
    step = pl.program_id(0)

    @pl.when(step == 0)
    def _():
        if first:
            up_acc[...] = jnp.zeros_like(up_acc)
            down_acc[...] = jnp.zeros_like(down_acc)
            sums_ref[...] = jnp.zeros_like(sums_ref)
        else:
            up_acc[...] = rest[2][...].astype(f32)
            down_acc[...] = rest[3][...].astype(f32)
            sums_ref[...] = rest[4][...]

    xhat, _ = normalize(pick_block(refs[:count], step).astype(f32))
    normed = (xhat * vec_ref[2:3, :] + vec_ref[3:4, :]).astype(bf16)
    normed_t = normed.T
    c = pick_block(refs[count : 2 * count], step)
    c_out[...] = c
    g = pad_lanes(dot_nt(c, wo_ref[...]))
    own = lax.broadcasted_iota(jnp.int32, (c.shape[0], LANES), 1) < HDIM
    for h in range(g_ref.shape[1] // LANES):
        part = jnp.where(own, head_window(g, h * HDIM), 0.0)
        g_ref[:, pl.ds(h * LANES, LANES)] = part.astype(bf16)
    y = None
    hidden_width = wu_ref.shape[1]
    for at in range(0, hidden_width, QB):
        cols = pl.ds(at, QB)
        h = dot(normed, wu_ref[:, cols]) + bu_ref[:, cols]
        cdf = 0.5 + 0.5 * lax.erf(h * 0.5**0.5)
        pdf = jnp.exp(-0.5 * h * h) * (2.0 * jnp.pi) ** -0.5
        act = (h * cdf).astype(bf16)
        gh = dot_nt(c, wd_ref[cols, :]) * (cdf + h * pdf)
        sums_ref[0:1, cols] += jnp.sum(gh, axis=0, keepdims=True)
        gh = gh.astype(bf16)
        y_part = dot(act, wd_ref[cols, :])
        dn_part = dot_nt(gh, wu_ref[:, cols])
        y = y_part if y is None else y + y_part
        dn = dn_part if at == 0 else dn + dn_part
        down_acc[cols, :] += dot(act.T, c)
        up_acc[:, cols] += dot(normed_t, gh)
    y_ref[...] = y.astype(bf16)
    dx_ref[...] = (dn * vec_ref[2:3, :]).astype(bf16)
    sums_ref[1:2, :] += jnp.sum(dn * xhat, axis=0, keepdims=True)
    sums_ref[2:3, :] += jnp.sum(dn, axis=0, keepdims=True)

    @pl.when(step == pl.num_programs(0) - 1)
    def _():
        gu_ref[...] = up_acc[...].astype(gu_ref.dtype)
        gd_ref[...] = down_acc[...].astype(gd_ref.dtype)


def mlp(me, offset, total, x, c, w_up, w_down, w_out, vectors, b_up, kept):
    count = len(x)
    tile, width = x[0].shape
    rows = count * tile
    units = w_up.shape[1]
    wide = w_out.shape[0] // HDIM * LANES
    whole = lambda a: pl.BlockSpec(a.shape, lambda r, me: (0, 0))
    shaped = lambda *s: pl.BlockSpec(s, lambda r, me: (0, 0))
    row_block = pl.BlockSpec((tile, width), lambda r, me: (r, 0))
    args = x + c + [w_up, w_down, w_out, vectors, b_up]
    specs = [whole(a) for a in args]
    alias = {}
    first = kept is None
    if not first:
        args += kept
        specs += [pl.BlockSpec(memory_space=pl.ANY)] * 2 + [whole(a) for a in kept[2:]]
        alias = {2 * count + 6: 2, 2 * count + 7: 3}
    return pl.pallas_call(
        functools.partial(mlp_kernel, first, count),
        grid_spec=pltpu.PrefetchScalarGridSpec(
            num_scalar_prefetch=1,
            grid=(count,),
            in_specs=specs,
            out_specs=[
                row_block, row_block,
                pl.BlockSpec((tile, wide), lambda r, me: ((r + offset) ^ me[0], 0)),
                pl.BlockSpec((tile, width), lambda r, me: ((r + offset) ^ me[0], 0)),
                shaped(width, units), shaped(units, width), shaped(8, width),
            ],
            scratch_shapes=[pltpu.VMEM((width, units), f32), pltpu.VMEM((units, width), f32)],
        ),
        out_shape=[
            pltpu.HBM((rows, width), bf16),
            pltpu.HBM((rows, width), bf16),
            pltpu.HBM((total, wide), bf16),
            pltpu.HBM((total, width), bf16),
            pltpu.HBM((width, units), bf16),
            pltpu.HBM((units, width), bf16),
            pltpu.HBM((8, width), f32),
        ],
        input_output_aliases=alias,
        compiler_params=pltpu.CompilerParams(vmem_limit_bytes=40 * 2**20),
        cost_estimate=cost(
            flops=14 * rows * width * units, bytes_accessed=rows * 8000, transcendentals=0
        ),
        name="mlp",
    )(me, *args)


def block_rows_of(i):
    return i * (i + 1) // 2 * QB


def attend_kernel(me_ref, q_ref, k_ref, v_ref, ct_ref, e_ref, inv_ref, vt_ref, s_ref):
    total = q_ref.shape[0]
    vt_ref[...] = v_ref[...].T
    row_at = lax.broadcasted_iota(jnp.int32, (QB, QB), 0)
    col_at = lax.broadcasted_iota(jnp.int32, (QB, QB), 1)
    causal = row_at <= col_at
    for i in range(total // QB):
        here = pl.ds(i * QB, QB)
        reach = (i + 1) * QB
        base = block_rows_of(i)
        qt = q_ref[here, :].T
        top = None
        for j in range(i + 1):
            at = pl.ds(j * QB, QB)
            s = dot(k_ref[at, :], qt)
            if j == i:
                s = jnp.where(causal, s, masked_fill)
            s_ref[at, :] = s
            part = jnp.max(s.reshape(QB // 8, 8, QB), axis=0)
            top = part if top is None else jnp.maximum(top, part)
        top = jnp.max(top, axis=0, keepdims=True)
        for j in range(i + 1):
            e_ref[0, pl.ds(base + j * QB, QB), :] = jnp.exp(
                s_ref[pl.ds(j * QB, QB), :] - top
            ).astype(bf16)
        ct = dot(vt_ref[:, :reach], e_ref[0, base : base + reach, :])
        inv = 1.0 / ct[HDIM : HDIM + 1, :]
        ct_ref[0, :, here] = ct[:HDIM, :] * inv
        inv_ref[0, i : i + 1, :] = inv


def attend(me, qkv, start, heads):
    total = qkv.shape[0]
    pick = lambda p: pl.BlockSpec((total, LANES), lambda h, me: (0, (h + start) * 3 + p))
    deep = lambda *s: pl.BlockSpec((1,) + s, lambda h, me: (h, 0, 0))
    blocks = total // QB
    kept = block_rows_of(blocks)
    return pl.pallas_call(
        attend_kernel,
        grid_spec=pltpu.PrefetchScalarGridSpec(
            num_scalar_prefetch=1,
            grid=(heads,),
            in_specs=[pick(0), pick(1), pick(2)],
            out_specs=[deep(HDIM, total), deep(kept, QB), deep(blocks, QB)],
            scratch_shapes=[pltpu.VMEM((LANES, total), bf16), pltpu.VMEM((total, QB), f32)],
        ),
        out_shape=[
            pltpu.HBM((heads, HDIM, total), f32),
            pltpu.HBM((heads, kept, QB), bf16),
            pltpu.HBM((heads, blocks, QB), f32),
        ],
        compiler_params=pltpu.CompilerParams(vmem_limit_bytes=36 * 2**20),
        cost_estimate=cost(
            flops=heads * kept * 3 * 2 * QB**2, bytes_accessed=heads * kept * 600, transcendentals=0
        ),
        name="attend",
    )(me, qkv, qkv, qkv)


def attend_back_kernel(
    me_ref, q_ref, k_ref, v_ref, g_ref, ct_ref, inv_ref, aux_ref, e_ref, normed_hbm,
    w_ref, vec_ref, c_hbm, proj_ref, bias_ref, grad_ref, norm_ref,
    kt_ref, d_ref, dk_ref, dv_ref, normed_ref, c_ref, sems,
):
    copies = [
        pltpu.make_async_copy(normed_hbm, normed_ref, sems.at[0]),
        pltpu.make_async_copy(c_hbm, c_ref, sems.at[1]),
    ]

    @pl.when(pl.program_id(0) == 0)
    def _():
        for copy in copies:
            copy.start()

    total = q_ref.shape[0]
    half = ROT // 2
    kt_ref[...] = k_ref[...].T
    feature = lax.broadcasted_iota(jnp.int32, (LANES, QB), 0)
    bias_q = jnp.zeros((1, LANES), f32)
    for i in range(total // QB):
        here = pl.ds(i * QB, QB)
        reach = (i + 1) * QB
        base = block_rows_of(i)
        qt = q_ref[here, :].T.astype(f32)
        gt = g_ref[here, :].T.astype(f32)
        inv = inv_ref[0, i : i + 1, :]
        less = -jnp.sum(gt[:HDIM, :] * ct_ref[0, :, here], axis=0, keepdims=True)
        less_hi = less.astype(bf16).astype(f32)
        ge = jnp.where(feature == HDIM, less_hi, gt)
        ge = jnp.where(feature == HDIM + 1, less - less_hi, ge).astype(bf16)
        gl = (gt * inv).T.astype(bf16)
        ql = jnp.where(feature < HDIM, qt * inv, 0.0).T.astype(bf16)
        for j in range(i + 1):
            at = pl.ds(j * QB, QB)
            e = e_ref[0, pl.ds(base + j * QB, QB), :]
            d = (e.astype(f32) * dot(v_ref[at, :], ge)).astype(bf16)
            d_ref[at, :] = d
            dv = dot(e, gl)
            dk = dot(d, ql)
            if j == i:
                dv_ref[at, :] = dv
                dk_ref[at, :] = dk
            else:
                dv_ref[at, :] += dv
                dk_ref[at, :] += dk
        dqt = dot(kt_ref[:, :reach], d_ref[:reach, :]) * (inv * HDIM**-0.5)
        c, s = aux_ref[:half, here], aux_ref[half:ROT, here]
        low, high = dqt[:half, :], dqt[half:ROT, :]
        dqt = jnp.concatenate(
            [low * c + high * s, high * c - low * s, dqt[ROT:HDIM, :],
             jnp.zeros((LANES - HDIM, QB), f32)], axis=0
        )
        dq = dqt.T
        bias_q += jnp.sum(dq, axis=0, keepdims=True)
        proj_ref[0, here, :HDIM] = dq[:, :HDIM].astype(bf16)
    bias_k = jnp.zeros((1, LANES), f32)
    bias_v = jnp.zeros((1, LANES), f32)
    for i in range(total // QB):
        here = pl.ds(i * QB, QB)
        cosine, up, down, _, _ = lane_tables(aux_ref[:, here])
        dk = dk_ref[here, :]
        dk = dk * cosine + pltpu.roll(dk, LANES - half, 1) * up - pltpu.roll(dk, half, 1) * down
        dv = dv_ref[here, :]
        bias_k += jnp.sum(dk, axis=0, keepdims=True)
        bias_v += jnp.sum(dv, axis=0, keepdims=True)
        proj_ref[0, here, HDIM : 2 * HDIM] = dk[:, :HDIM].astype(bf16)
        proj_ref[0, here, 2 * HDIM :] = dv[:, :HDIM].astype(bf16)
    bias_ref[0] = jnp.concatenate([bias_q, bias_k, bias_v], axis=1)
    @pl.when(pl.program_id(0) == 0)
    def _():
        for copy in copies:
            copy.wait()

    proj = proj_ref[0]
    grad = lax.dot_general(
        proj, normed_ref[...], (((0,), (0,)), ((), ())), preferred_element_type=f32
    )
    grad_ref[0, :HDIM, :] = dot(ct_ref[0].astype(bf16), c_ref[...]).astype(bf16)
    grad_ref[0, HDIM:, :] = grad.astype(bf16)
    column = lax.dot_general(
        proj, jnp.ones((total, LANES), bf16), (((0,), (0,)), ((), ())),
        preferred_element_type=f32,
    )[:, :1]
    weight = w_ref[0].astype(f32)
    shift = jnp.sum(weight * column, axis=0, keepdims=True)
    gain = jnp.sum(weight * grad, axis=0, keepdims=True) - shift * vec_ref[1:2, :]
    norm_ref[0] = jnp.concatenate([gain / vec_ref[0:1, :], shift], axis=0)


def attend_back(me, qkv, grad_ctx, kept, aux, normed, w_heads, vectors, c_all, start, at, count):
    ct, e, inv = kept
    total, width = normed.shape
    pick = lambda p: pl.BlockSpec((total, LANES), lambda h, me: (0, (h + start) * 3 + p))
    deep = lambda a: pl.BlockSpec((1,) + a.shape[1:], lambda h, me: (h + at, 0, 0))
    whole = lambda a: pl.BlockSpec(a.shape, lambda h, me: (0, 0))
    out = lambda *s: pl.BlockSpec((1,) + s, lambda h, me: (h, 0, 0))
    return pl.pallas_call(
        attend_back_kernel,
        grid_spec=pltpu.PrefetchScalarGridSpec(
            num_scalar_prefetch=1,
            grid=(count,),
            in_specs=[
                pick(0), pick(1), pick(2),
                pl.BlockSpec((total, LANES), lambda h, me: (0, h + start)),
                deep(ct), deep(inv), whole(aux), deep(e),
                pl.BlockSpec(memory_space=pl.ANY),
                pl.BlockSpec((1,) + w_heads.shape[1:], lambda h, me: (h + start, 0, 0)),
                whole(vectors),
                pl.BlockSpec(memory_space=pl.ANY),
            ],
            out_specs=[
                out(total, 3 * HDIM), out(1, 3 * LANES), out(4 * HDIM, width), out(2, width),
            ],
            scratch_shapes=[
                pltpu.VMEM((LANES, total), bf16),
                pltpu.VMEM((total, QB), bf16),
                pltpu.VMEM((total, LANES), f32),
                pltpu.VMEM((total, LANES), f32),
                pltpu.VMEM((total, width), bf16),
                pltpu.VMEM((total, width), bf16),
                pltpu.SemaphoreType.DMA((2,)),
            ],
        ),
        out_shape=[
            pltpu.HBM((count, total, 3 * HDIM), bf16),
            pltpu.HBM((count, 1, 3 * LANES), f32),
            pltpu.HBM((count, 4 * HDIM, width), bf16),
            pltpu.HBM((count, 2, width), f32),
        ],
        compiler_params=pltpu.CompilerParams(vmem_limit_bytes=VMEM),
        cost_estimate=cost(
            flops=count * e.shape[1] * 6 * 2 * QB**2,
            bytes_accessed=count * e.shape[1] * 600,
            transcendentals=0,
        ),
        name="attend_back",
    )(me, qkv, qkv, qkv, grad_ctx, ct, inv, aux, e, normed, w_heads, vectors, c_all)


def mid_kernel(n, me_ref, cta_ref, ctb_ref, y0_ref, y1_ref, wo_ref, *outs):
    step = pl.program_id(0)
    y = jnp.where(step < n // 2, y0_ref[...], y1_ref[...]).astype(f32)
    ct = jnp.concatenate([cta_ref[...], ctb_ref[...]], axis=0)
    ct = ct.reshape(wo_ref.shape[0], y.shape[0]).astype(bf16)
    y = (y + dot(ct.T, wo_ref[...])).astype(bf16)
    for j in range(n):
        @pl.when(step == j)
        def _(j=j):
            outs[j][...] = y


def near_far(n, tile, width):
    half = n // 2
    return [
        pl.BlockSpec((tile, width), lambda r, me: (jnp.minimum(r, half - 1), 0)),
        pl.BlockSpec((tile, width), lambda r, me: (jnp.maximum(r - half, 0), 0)),
    ]


def mid(me, cta, ctb, y_halves, w_out):
    n = lax.axis_size("tensor")
    total = cta.shape[2]
    tile = total // n
    wide, width = w_out.shape
    fixed = lambda *s: pl.BlockSpec(s, lambda r, me: (0, 0))
    return pl.pallas_call(
        functools.partial(mid_kernel, n),
        grid_spec=pltpu.PrefetchScalarGridSpec(
            num_scalar_prefetch=1,
            grid=(n,),
            in_specs=[
                pl.BlockSpec((a.shape[0], HDIM, tile), lambda r, me: (0, 0, r ^ me[0]))
                for a in (cta, ctb)
            ]
            + near_far(n, tile, width)
            + [fixed(wide, width)],
            out_specs=[fixed(tile, width)] * n,
        ),
        out_shape=[pltpu.HBM((tile, width), bf16)] * n,
        compiler_params=pltpu.CompilerParams(vmem_limit_bytes=VMEM),
        cost_estimate=cost(
            flops=2 * total * wide * width, bytes_accessed=total * 8000, transcendentals=0
        ),
        name="mid",
    )(me, cta, ctb, *y_halves, w_out)


def back_kernel(count, me_ref, pa_ref, pb_ref, d_ref, w_ref, vec_ref, *outs):
    step = pl.program_id(0)
    dn = None
    for h, p in enumerate([r[h] for r in (pa_ref, pb_ref) for h in range(r.shape[0])]):
        part = dot(p, w_ref[h])
        dn = part if dn is None else dn + part
    dx = (d_ref[...].astype(f32) + dn * vec_ref[0:1, :]).astype(bf16)
    for j in range(count):
        @pl.when(step == j)
        def _(j=j):
            outs[j][...] = dx


def back(me, offset, proj_a, proj_b, d, w_heads, vectors):
    tile = proj_a.shape[1] // lax.axis_size("tensor")
    rows, width = d.shape
    count = rows // tile
    fixed = lambda *s: pl.BlockSpec(s, lambda r, me: (0,) * len(s))
    rows_of = lambda a: pl.BlockSpec(
        (a.shape[0], tile, a.shape[2]), lambda r, me: (0, (r + offset) ^ me[0], 0)
    )
    return pl.pallas_call(
        functools.partial(back_kernel, count),
        grid_spec=pltpu.PrefetchScalarGridSpec(
            num_scalar_prefetch=1,
            grid=(count,),
            in_specs=[rows_of(proj_a), rows_of(proj_b)]
            + [pl.BlockSpec((tile, width), lambda r, me: (r, 0))]
            + [fixed(*w_heads.shape), fixed(*vectors.shape)],
            out_specs=[fixed(tile, width)] * count,
        ),
        out_shape=[pltpu.HBM((tile, width), bf16)] * count,
        compiler_params=pltpu.CompilerParams(vmem_limit_bytes=VMEM),
        cost_estimate=cost(
            flops=1000, bytes_accessed=1000, transcendentals=0
        ),
        name="back",
    )(me, proj_a, proj_b, d, w_heads, vectors)


def join_kernel(count, side_ref, *refs):
    step = pl.program_id(0)
    for k in range(count):
        mine, got, out = refs[2 * k], refs[2 * k + 1], refs[2 * count + k]
        out[...] = jnp.where(step == 0, mine[...], got[...]).astype(f32)


def join(sums):
    count = len(sums)
    rows, width = sums[0].last[0].shape
    sides = jnp.stack([a.last[2] for a in sums]).astype(jnp.int32)
    whole = pl.BlockSpec((rows, width), lambda r, side: (0, 0))
    return pl.pallas_call(
        functools.partial(join_kernel, count),
        grid_spec=pltpu.PrefetchScalarGridSpec(
            num_scalar_prefetch=1,
            grid=(2,),
            in_specs=[whole] * (2 * count),
            out_specs=[
                pl.BlockSpec((rows, width), lambda r, side, k=k: (r ^ side[k], 0))
                for k in range(count)
            ],
        ),
        out_shape=[jax.ShapeDtypeStruct((2 * rows, width), f32)] * count,
        compiler_params=pltpu.CompilerParams(vmem_limit_bytes=24 * 2**20),
        name="join",
    )(sides, *[a for b in sums for a in b.last[:2]])


def assemble_kernel(heads, side_ref, mine_ref, got_ref, out_ref, qkv_ref, all_ref):
    rows = mine_ref.shape[0]
    all_ref[pl.ds(pl.multiple_of(side_ref[0] * rows, 8), rows), :] = mine_ref[...].astype(f32)
    all_ref[pl.ds(pl.multiple_of((1 - side_ref[0]) * rows, 8), rows), :] = got_ref[...].astype(f32)
    tall = 4 * HDIM
    for h in range(heads):
        out_ref[h * HDIM : (h + 1) * HDIM, :] = all_ref[h * tall : h * tall + HDIM, :]
    parts = [all_ref[h * tall + HDIM : (h + 1) * tall, :] for h in range(heads)]
    qkv_ref[...] = jnp.concatenate(parts, axis=0)


def assemble(total, heads):
    mine, got, side = total.last
    rows, width = mine.shape
    whole = lambda *s: pl.BlockSpec(s, lambda r, side: (0, 0))
    return pl.pallas_call(
        functools.partial(assemble_kernel, heads),
        grid_spec=pltpu.PrefetchScalarGridSpec(
            num_scalar_prefetch=1,
            grid=(1,),
            in_specs=[whole(rows, width)] * 2,
            out_specs=[whole(heads * HDIM, width), whole(heads * 3 * HDIM, width)],
            scratch_shapes=[pltpu.VMEM((2 * rows, width), f32)],
        ),
        out_shape=[
            jax.ShapeDtypeStruct((heads * HDIM, width), f32),
            jax.ShapeDtypeStruct((heads * 3 * HDIM, width), f32),
        ],
        compiler_params=pltpu.CompilerParams(vmem_limit_bytes=24 * 2**20),
        name="assemble",
    )(side.astype(jnp.int32).reshape(1), mine, got)


def body(
    tokens,
    doc_lengths,
    w_qkv,
    b_qkv,
    w_out,
    w_up,
    b_up,
    w_down,
    out_bias,
    norm1_gain,
    norm1_shift,
    norm2_gain,
    norm2_shift,
    cotangent,
):
    row_count, width = tokens.shape
    n_tensor = lax.axis_size("tensor")
    total = row_count * n_tensor
    index = lax.axis_index("tensor")
    me = index.astype(jnp.int32).reshape(1)
    heads = w_out.shape[0] // HDIM
    slots = doc_lengths.shape[1]
    x_far = gather_far(tokens, "tensor")
    x_near = gather_near(tokens, "tensor")
    documents, positions = token_layout(doc_lengths[0], total, PADB)
    local_docs = lax.dynamic_slice_in_dim(documents, index * row_count, row_count)
    grad_send = jnp.where(local_docs[:, None] >= 0, cotangent, 0)
    c_near = gather_near(grad_send, "tensor")
    half = n_tensor // 2

    aux = aux_rows(documents, positions)
    gains = [norm1_gain, norm1_shift, norm2_gain, norm2_shift]
    vectors = jnp.stack(gains).astype(f32)
    b_up_row = b_up.astype(f32)[None]
    w_heads = w_qkv.T.reshape(heads, 3 * HDIM, width)
    b_qkv_row = b_qkv.astype(f32)[None]

    mlp_args = (w_up, w_down, w_out, vectors, b_up_row)
    w_turned = w_qkv.T
    front_args = (w_turned, b_qkv_row, vectors, aux, slots, heads)
    qkv, normed = front(me, 0, x_near, *front_args, None)
    me, grad_far, qkv, normed = tie(me, grad_send, qkv, normed)
    c_far = gather_far(grad_far, "tensor")
    y0, d0, g, c_all, gu, gd, sums = mlp(me, 0, total, x_near, c_near, *mlp_args, None)
    x_far, me, y0, d0, g, c_all, gu, gd, sums = tie(x_far, me, y0, d0, g, c_all, gu, gd, sums)
    x_far = gather_near(x_far, "tensor")
    qkv, normed = front(me, half, x_far, *front_args, [qkv, normed])
    me, qkv, normed = tie(me, qkv, normed)
    kept_a = attend(me, qkv, 0, 1)
    c_far, me, kept_a = tie(c_far, me, kept_a)
    c_far = gather_near(c_far, "tensor")
    y1, d1, g, c_all, gu, gd, sums = mlp(
        me, half, total, x_far, c_far, *mlp_args, [g, c_all, gu, gd, sums]
    )
    me, y1, d1, g, c_all, gu, gd, sums = tie(me, y1, d1, g, c_all, gu, gd, sums)
    up, down = StagedSum(gu, "dp", 0), StagedSum(gd, "dp", 1)
    up.send()
    down.send()
    kept_b = attend(me, qkv, 1, heads - 1)
    me, kept_b = boundary((me, kept_b), up, down)
    up.send()
    down.send()
    ab_args = (aux, normed, w_heads, vectors, c_all)
    pa, ba, qa, na = attend_back(me, qkv, g, kept_a, *ab_args, 0, 0, 1)
    me, pa, ba, qa, na = boundary((me, pa, ba, qa, na), up, down)
    up.send()
    down.send()
    pb, bb, qb, nb = attend_back(me, qkv, g, kept_b, *ab_args, 1, 0, heads - 1)
    me, pb, bb, qb, nb, grad_rows = boundary((me, pb, bb, qb, nb, grad_send), up, down)
    up.send()
    down.send()
    rows = jnp.concatenate([qa, qb], axis=0).reshape(heads * 4 * HDIM, width)
    attn = StagedSum(rows, "dp", 0)
    attn.send()
    grad_rows = grad_rows.astype(f32)
    vec = jnp.concatenate(
        [
            jnp.sum(grad_rows, axis=0)[None],
            jnp.sum(na, axis=0) + jnp.sum(nb, axis=0),
            sums[1:3],
        ],
        axis=0,
    )
    vec = SmallSum(vec, "tensor")
    vec.send()
    far_blocks = back(me, half, pa, pb, d1, w_heads, vectors)
    me, far_blocks = boundary((me, far_blocks), vec)
    far_rows = ScatterSum(dict(enumerate(far_blocks)), "tensor")
    far_rows.send()
    vec.send()
    me = boundary(me, far_rows)
    far_rows.finish(half)
    cross = Exchange(far_rows.blocks[0].astype(bf16), "tensor", half)
    near_blocks = back(me, 0, pa, pb, d0, w_heads, vectors)
    me, near_blocks = boundary((me, near_blocks), up, down, attn, vec)
    near_rows = ScatterSum(dict(enumerate(near_blocks)), "tensor")
    near_rows.send()
    attn.send()
    up.send()
    down.send()
    vec.finish()
    share = width // n_tensor
    vec = lax.dynamic_slice_in_dim(vec.out, index * share, share, 1)
    bias = jnp.concatenate([ba, bb]).reshape(heads, 3, LANES)[:, :, :HDIM].reshape(-1)
    small = SmallSum(jnp.concatenate([bias, sums[0], vec.reshape(-1)]), "dp")
    small.send()
    y_blocks = mid(me, kept_a[0], kept_b[0], [y0, y1], w_out)
    tok, y_blocks = boundary((me, y_blocks), attn, up, small, near_rows, cross)
    near_rows.finish(half)
    attn.send()
    y_rows = ScatterSum(dict(enumerate(y_blocks)), "tensor")
    y_rows.send()
    up.send()
    small.send()
    dx = near_rows.blocks[0].astype(f32) + cross.out.astype(f32)
    inputs = tokens.astype(f32)
    xhat, inv = normalize(inputs)
    grad_input = grad_rows + inv * (
        dx
        - jnp.mean(dx, axis=-1, keepdims=True)
        - xhat * jnp.mean(dx * xhat, axis=-1, keepdims=True)
    )
    tok, grad_input = boundary((tok, grad_input), attn, small, y_rows)
    attn.send()
    y_rows.send()
    small.send()
    tok = boundary(tok, attn, down, small)
    attn.send()
    tok = boundary(tok, attn, up, y_rows)
    attn.send()
    down.send()
    block_out = inputs + out_bias.astype(f32) + y_rows.blocks[0].astype(f32)
    block_out = block_out.astype(bf16)
    tok, block_out = boundary((tok, block_out), down)
    up.finish()
    down.finish()
    up_sum, down_sum = join([up, down])
    tok, up_sum, down_sum = boundary((tok, up_sum, down_sum), attn)
    attn.finish()
    small.finish()
    small = small.out
    out_sum, qkv_sum = assemble(attn, heads)
    nq, nu = bias.shape[0], b_up.shape[0]
    return (
        block_out,
        grad_input,
        qkv_sum.T,
        small[:nq],
        out_sum,
        up_sum,
        small[nq : nq + nu],
        down_sum,
        small[nq + nu :].reshape(5, share),
    )


def solution(mesh):
    placed = (
        P(("dp", "tensor"), None),
        P("dp", None),
        P(None, "tensor"),
        P("tensor"),
        P("tensor", None),
        P(None, "tensor"),
        P("tensor"),
        P("tensor", None),
        P(),
        P(),
        P(),
        P(),
        P(),
        P(("dp", "tensor"), None),
    )
    return jax.shard_map(
        body,
        mesh=mesh,
        in_specs=placed,
        out_specs=(
            P(("dp", "tensor"), None),
            P(("dp", "tensor"), None),
            P(None, "tensor"),
            P("tensor"),
            P("tensor", None),
            P(None, "tensor"),
            P("tensor"),
            P("tensor", None),
            P(None, "tensor"),
        ),
        check_vma=False,
    )
```

```python
import functools

import jax
import jax.numpy as jnp
from jax import lax
from jax.experimental import pallas as pl
from jax.experimental.pallas import tpu as pltpu
from jax.sharding import PartitionSpec as P

HDIM = 64
ROT = 16
PADB = 128
LANES = 128
QB = 256
VMEM = 56 * 2**20
COST = 1.0

norm_eps = 1e-05
masked_fill = -1e30
rotary_base = 10000.0
f32 = jnp.float32
bf16 = jnp.bfloat16


def swap(values, axis, bit):
    n = lax.axis_size(axis)
    return lax.ppermute(values, axis, [(i, i ^ bit) for i in range(n)])


def gather_far(values, axis):
    return swap(values, axis, lax.axis_size(axis) // 2)


def gather_near(values, axis):
    blocks = {0: values}
    bit = lax.axis_size(axis) // 4
    while bit:
        for at in list(blocks):
            blocks[at | bit] = swap(blocks[at], axis, bit)
        bit //= 2
    return [blocks[j] for j in range(len(blocks))]


class ScatterSum:
    def __init__(self, blocks, axis):
        self.blocks, self.axis, self.got = blocks, axis, None
        self.bit = 1

    def send(self):
        bit = self.bit
        self.got = {
            j ^ bit: swap(b.astype(bf16), self.axis, bit)
            for j, b in self.blocks.items()
            if j & bit
        }

    def take(self):
        got = self.got
        self.blocks = {j: self.blocks[j].astype(f32) + got[j].astype(f32) for j in got}
        self.bit *= 2

    def finish(self, bits):
        while self.bit < bits:
            self.send()
            self.take()


class Exchange:
    def __init__(self, value, axis, bit):
        self.got = swap(value, axis, bit)

    def take(self):
        self.out = self.got


def axis_bits(axis, first):
    n = lax.axis_size(axis)
    bits = [1 << k for k in range(n.bit_length() - 1)]
    return bits[first:] + bits[:first]


def tie(first, *others):
    return lax.optimization_barrier((first,) + others)


def boundary(values, *sums):
    values, got = lax.optimization_barrier((values, [a.got for a in sums]))
    for a, g in zip(sums, got):
        a.got = g
        a.take()
    return values


class StagedSum:
    def __init__(self, values, axis, first):
        self.held, self.axis, self.got = [values.astype(bf16)], axis, None
        bits = axis_bits(axis, first)
        self.steps = [(b, True) for b in bits] + [(b, False) for b in reversed(bits)]

    def part(self, side):
        def cut(a):
            a = a.reshape((2, a.shape[0] // 2) + a.shape[1:])
            return lax.dynamic_index_in_dim(a, side, 0, keepdims=False)

        parts = self.held if side is None else [cut(a) for a in self.held]
        if len(parts) == 1:
            return parts[0]
        return (parts[0].astype(f32) + parts[1].astype(f32)).astype(bf16)

    def send(self):
        bit, halving = self.steps[0]
        side = (lax.axis_index(self.axis) // bit) % 2
        self.got = swap(self.part(1 - side if halving else None), self.axis, bit)

    def take(self):
        bit, halving = self.steps.pop(0)
        side = (lax.axis_index(self.axis) // bit) % 2
        if halving:
            self.held = [self.part(side), self.got]
        else:
            mine = self.part(None)
            if not self.steps:
                self.last = (mine, self.got, side)
                return
            low = jnp.where(side == 0, mine, self.got)
            high = jnp.where(side == 0, self.got, mine)
            self.held = [jnp.concatenate([low, high], axis=0)]

    def finish(self):
        while self.steps:
            self.send()
            self.take()

class SmallSum:
    def __init__(self, values, axis):
        self.out, self.axis, self.bits, self.got = values, axis, axis_bits(axis, 0), None

    def send(self):
        self.got = swap(self.out, self.axis, self.bits.pop(0))

    def take(self):
        self.out = self.out + self.got

    def finish(self):
        while self.bits:
            self.send()
            self.take()


def token_layout(lengths, total, pad_block):
    padded = (lengths + pad_block - 1) // pad_block * pad_block
    starts = jnp.cumsum(padded) - padded
    row_ids = jnp.arange(total, dtype=jnp.int32)
    inside = (row_ids[None, :] >= starts[:, None]) & (
        row_ids[None, :] < (starts + lengths)[:, None]
    )
    slot_ids = jnp.arange(lengths.shape[0], dtype=jnp.int32)
    documents = jnp.sum(jnp.where(inside, slot_ids[:, None] + 1, 0), axis=0) - 1
    offsets = jnp.sum(jnp.where(inside, starts[:, None], 0), axis=0)
    return (documents, row_ids - offsets)


def aux_rows(documents, positions):
    half = ROT // 2
    inverse = rotary_base ** (-(jnp.arange(half, dtype=f32) * 2.0 / ROT))
    angles = inverse[:, None] * positions.astype(f32)[None, :]
    docs = (documents + 1).astype(f32)[None, :]
    return jnp.concatenate(
        [jnp.cos(angles), jnp.sin(angles), docs, jnp.zeros((7, docs.shape[1]), f32)], axis=0
    )


def cost(flops, bytes_accessed, transcendentals):
    return pl.CostEstimate(
        flops=int(COST * flops),
        bytes_accessed=int(COST * bytes_accessed),
        transcendentals=transcendentals,
    )


def dot(left, right):
    return lax.dot_general(left, right, (((1,), (0,)), ((), ())), preferred_element_type=f32)


def dot_nt(left, right):
    return lax.dot_general(left, right, (((1,), (1,)), ((), ())), preferred_element_type=f32)


def normalize(x):
    center = jnp.mean(x, axis=-1, keepdims=True)
    off = x - center
    inv = lax.rsqrt(jnp.mean(off * off, axis=-1, keepdims=True) + norm_eps)
    return off * inv, inv


def pick_block(refs, step):
    out = refs[0][...]
    for j in range(1, len(refs)):
        out = jnp.where(step == j, refs[j][...], out)
    return out


def head_window(a, at):
    if at % LANES == 0:
        return a[:, at : at + LANES]
    return pltpu.roll(a[:, at - HDIM : at + HDIM], HDIM, 1)


def pad_lanes(a):
    extra = -a.shape[1] % LANES
    if extra == 0:
        return a
    return jnp.concatenate([a, jnp.zeros((a.shape[0], extra), a.dtype)], axis=1)


def lane_tables(aux):
    rows = aux.shape[1]
    half = ROT // 2
    t = jnp.concatenate([aux, jnp.zeros((LANES - aux.shape[0], rows), f32)], axis=0).T
    lane = lax.broadcasted_iota(jnp.int32, (rows, LANES), 1)
    cosine = jnp.where(lane < half, t, jnp.where(lane < ROT, pltpu.roll(t, half, 1), 1.0))
    up = jnp.where(lane < half, pltpu.roll(t, LANES - half, 1), 0.0)
    down = jnp.where((lane >= half) & (lane < ROT), t, 0.0)
    return cosine, up, down, t[:, ROT : ROT + 1], lane


def front_kernel(heads, slots, count, me_ref, *refs):
    w_ref, b_ref, vec_ref, aux_ref = refs[count : count + 4]
    qkv_ref, normed_ref = refs[-2:]
    half = ROT // 2
    x = pick_block(refs[:count], pl.program_id(0))
    xhat, _ = normalize(x.astype(f32))
    normed = (xhat * vec_ref[0:1, :] + vec_ref[1:2, :]).astype(bf16)
    normed_ref[...] = normed
    cosine, up, down, doc, lane = lane_tables(aux_ref[...])
    used = (lane >= HDIM) & (lane <= HDIM + slots)
    hit = (lane - HDIM).astype(f32) == doc
    key_side = jnp.where(used & hit, 1.0, 0.0)
    query_side = jnp.where(used & ~hit, masked_fill, 0.0)
    value_side = jnp.where((lane >= HDIM) & (lane < HDIM + 2), 1.0, 0.0)
    own = lane < HDIM
    proj = pad_lanes(dot_nt(normed, w_ref[...]) + b_ref[...])
    for h in range(heads):
        for part in range(3):
            a = head_window(proj, (h * 3 + part) * HDIM)
            if part < 2:
                a = a * cosine - pltpu.roll(a, LANES - half, 1) * up + pltpu.roll(a, half, 1) * down
            if part == 0:
                a = jnp.where(own, a * HDIM**-0.5, query_side)
            else:
                a = jnp.where(own, a, key_side if part == 1 else value_side)
            qkv_ref[:, pl.ds((h * 3 + part) * LANES, LANES)] = a.astype(bf16)


def front(me, offset, blocks, w_turned, b_qkv, vectors, aux, slots, heads, kept):
    tile, width = blocks[0].shape
    wide = heads * 3 * LANES
    whole = lambda a: pl.BlockSpec(a.shape, lambda r, me: (0, 0))
    args = blocks + [w_turned, b_qkv, vectors, aux]
    specs = [whole(a) for a in args[:-1]]
    specs.append(pl.BlockSpec((aux.shape[0], tile), lambda r, me: (0, (r + offset) ^ me[0])))
    alias = {}
    if kept is not None:
        args += kept
        specs += [pl.BlockSpec(memory_space=pl.ANY)] * 2
        alias = {len(args) - 1: 0, len(args): 1}
    return pl.pallas_call(
        functools.partial(front_kernel, heads, slots, len(blocks)),
        grid_spec=pltpu.PrefetchScalarGridSpec(
            num_scalar_prefetch=1,
            grid=(len(blocks),),
            in_specs=specs,
            out_specs=[
                pl.BlockSpec((tile, wide), lambda r, me: ((r + offset) ^ me[0], 0)),
                pl.BlockSpec((tile, width), lambda r, me: ((r + offset) ^ me[0], 0)),
            ],
        ),
        out_shape=[
            pltpu.HBM((aux.shape[1], wide), bf16),
            pltpu.HBM((aux.shape[1], width), bf16),
        ],
        input_output_aliases=alias,
        compiler_params=pltpu.CompilerParams(vmem_limit_bytes=24 * 2**20),
        cost_estimate=cost(
            flops=4 * len(blocks) * tile * width * wide,
            bytes_accessed=len(blocks) * tile * 4000,
            transcendentals=0,
        ),
        name="front",
    )(me, *args)


def mlp_kernel(
    first, count, me_ref, *refs
):
    wu_ref, wd_ref, wo_ref, vec_ref, bu_ref = refs[2 * count : 2 * count + 5]
    rest = refs[2 * count + 5 :]
    y_ref, dx_ref, g_ref, c_out, gu_ref, gd_ref, sums_ref, up_acc, down_acc = rest[-9:]
    step = pl.program_id(0)

    @pl.when(step == 0)
    def _():
        if first:
            up_acc[...] = jnp.zeros_like(up_acc)
            down_acc[...] = jnp.zeros_like(down_acc)
            sums_ref[...] = jnp.zeros_like(sums_ref)
        else:
            up_acc[...] = rest[2][...].astype(f32)
            down_acc[...] = rest[3][...].astype(f32)
            sums_ref[...] = rest[4][...]

    xhat, _ = normalize(pick_block(refs[:count], step).astype(f32))
    normed = (xhat * vec_ref[2:3, :] + vec_ref[3:4, :]).astype(bf16)
    normed_t = normed.T
    c = pick_block(refs[count : 2 * count], step)
    c_out[...] = c
    g = pad_lanes(dot_nt(c, wo_ref[...]))
    own = lax.broadcasted_iota(jnp.int32, (c.shape[0], LANES), 1) < HDIM
    for h in range(g_ref.shape[1] // LANES):
        part = jnp.where(own, head_window(g, h * HDIM), 0.0)
        g_ref[:, pl.ds(h * LANES, LANES)] = part.astype(bf16)
    y = None
    hidden_width = wu_ref.shape[1]
    for at in range(0, hidden_width, QB):
        cols = pl.ds(at, QB)
        h = dot(normed, wu_ref[:, cols]) + bu_ref[:, cols]
        cdf = 0.5 + 0.5 * lax.erf(h * 0.5**0.5)
        pdf = jnp.exp(-0.5 * h * h) * (2.0 * jnp.pi) ** -0.5
        act = (h * cdf).astype(bf16)
        gh = dot_nt(c, wd_ref[cols, :]) * (cdf + h * pdf)
        sums_ref[0:1, cols] += jnp.sum(gh, axis=0, keepdims=True)
        gh = gh.astype(bf16)
        y_part = dot(act, wd_ref[cols, :])
        dn_part = dot_nt(gh, wu_ref[:, cols])
        y = y_part if y is None else y + y_part
        dn = dn_part if at == 0 else dn + dn_part
        down_acc[cols, :] += dot(act.T, c)
        up_acc[:, cols] += dot(normed_t, gh)
    y_ref[...] = y.astype(bf16)
    dx_ref[...] = (dn * vec_ref[2:3, :]).astype(bf16)
    sums_ref[1:2, :] += jnp.sum(dn * xhat, axis=0, keepdims=True)
    sums_ref[2:3, :] += jnp.sum(dn, axis=0, keepdims=True)

    @pl.when(step == pl.num_programs(0) - 1)
    def _():
        gu_ref[...] = up_acc[...].astype(gu_ref.dtype)
        gd_ref[...] = down_acc[...].astype(gd_ref.dtype)


def mlp(me, offset, total, x, c, w_up, w_down, w_out, vectors, b_up, kept):
    count = len(x)
    tile, width = x[0].shape
    rows = count * tile
    units = w_up.shape[1]
    wide = w_out.shape[0] // HDIM * LANES
    whole = lambda a: pl.BlockSpec(a.shape, lambda r, me: (0, 0))
    shaped = lambda *s: pl.BlockSpec(s, lambda r, me: (0, 0))
    row_block = pl.BlockSpec((tile, width), lambda r, me: (r, 0))
    args = x + c + [w_up, w_down, w_out, vectors, b_up]
    specs = [whole(a) for a in args]
    alias = {}
    first = kept is None
    if not first:
        args += kept
        specs += [pl.BlockSpec(memory_space=pl.ANY)] * 2 + [whole(a) for a in kept[2:]]
        alias = {2 * count + 6: 2, 2 * count + 7: 3}
    return pl.pallas_call(
        functools.partial(mlp_kernel, first, count),
        grid_spec=pltpu.PrefetchScalarGridSpec(
            num_scalar_prefetch=1,
            grid=(count,),
            in_specs=specs,
            out_specs=[
                row_block, row_block,
                pl.BlockSpec((tile, wide), lambda r, me: ((r + offset) ^ me[0], 0)),
                pl.BlockSpec((tile, width), lambda r, me: ((r + offset) ^ me[0], 0)),
                shaped(width, units), shaped(units, width), shaped(8, width),
            ],
            scratch_shapes=[pltpu.VMEM((width, units), f32), pltpu.VMEM((units, width), f32)],
        ),
        out_shape=[
            pltpu.HBM((rows, width), bf16),
            pltpu.HBM((rows, width), bf16),
            pltpu.HBM((total, wide), bf16),
            pltpu.HBM((total, width), bf16),
            pltpu.HBM((width, units), bf16),
            pltpu.HBM((units, width), bf16),
            pltpu.HBM((8, width), f32),
        ],
        input_output_aliases=alias,
        compiler_params=pltpu.CompilerParams(vmem_limit_bytes=40 * 2**20 if first else VMEM),
        cost_estimate=cost(
            flops=14 * rows * width * units, bytes_accessed=rows * 8000, transcendentals=0
        ),
        name="mlp",
    )(me, *args)


def block_rows_of(i):
    return i * (i + 1) // 2 * QB


def attend_kernel(me_ref, q_ref, k_ref, v_ref, ct_ref, e_ref, inv_ref, vt_ref, s_ref):
    total = q_ref.shape[0]
    vt_ref[...] = v_ref[...].T
    row_at = lax.broadcasted_iota(jnp.int32, (QB, QB), 0)
    col_at = lax.broadcasted_iota(jnp.int32, (QB, QB), 1)
    causal = row_at <= col_at
    for i in range(total // QB):
        here = pl.ds(i * QB, QB)
        reach = (i + 1) * QB
        base = block_rows_of(i)
        qt = q_ref[here, :].T
        top = None
        for j in range(i + 1):
            at = pl.ds(j * QB, QB)
            s = dot(k_ref[at, :], qt)
            if j == i:
                s = jnp.where(causal, s, masked_fill)
            s_ref[at, :] = s
            part = jnp.max(s.reshape(QB // 8, 8, QB), axis=0)
            top = part if top is None else jnp.maximum(top, part)
        top = jnp.max(top, axis=0, keepdims=True)
        for j in range(i + 1):
            e_ref[0, pl.ds(base + j * QB, QB), :] = jnp.exp(
                s_ref[pl.ds(j * QB, QB), :] - top
            ).astype(bf16)
        ct = dot(vt_ref[:, :reach], e_ref[0, base : base + reach, :])
        inv = 1.0 / ct[HDIM : HDIM + 1, :]
        ct_ref[0, :, here] = ct[:HDIM, :] * inv
        inv_ref[0, i : i + 1, :] = inv


def attend(me, qkv, start, heads):
    total = qkv.shape[0]
    pick = lambda p: pl.BlockSpec((total, LANES), lambda h, me: (0, (h + start) * 3 + p))
    deep = lambda *s: pl.BlockSpec((1,) + s, lambda h, me: (h, 0, 0))
    blocks = total // QB
    kept = block_rows_of(blocks)
    return pl.pallas_call(
        attend_kernel,
        grid_spec=pltpu.PrefetchScalarGridSpec(
            num_scalar_prefetch=1,
            grid=(heads,),
            in_specs=[pick(0), pick(1), pick(2)],
            out_specs=[deep(HDIM, total), deep(kept, QB), deep(blocks, QB)],
            scratch_shapes=[pltpu.VMEM((LANES, total), bf16), pltpu.VMEM((total, QB), f32)],
        ),
        out_shape=[
            pltpu.HBM((heads, HDIM, total), f32),
            pltpu.HBM((heads, kept, QB), bf16),
            pltpu.HBM((heads, blocks, QB), f32),
        ],
        compiler_params=pltpu.CompilerParams(vmem_limit_bytes=VMEM if heads == 1 else 36 * 2**20),
        cost_estimate=cost(
            flops=heads * kept * 3 * 2 * QB**2, bytes_accessed=heads * kept * 600, transcendentals=0
        ),
        name="attend",
    )(me, qkv, qkv, qkv)


def attend_back_kernel(
    me_ref, q_ref, k_ref, v_ref, g_ref, ct_ref, inv_ref, aux_ref, e_ref, normed_hbm,
    w_ref, vec_ref, c_hbm, proj_ref, bias_ref, grad_ref, norm_ref,
    kt_ref, d_ref, dk_ref, dv_ref, normed_ref, c_ref, sems,
):
    copies = [
        pltpu.make_async_copy(normed_hbm, normed_ref, sems.at[0]),
        pltpu.make_async_copy(c_hbm, c_ref, sems.at[1]),
    ]

    @pl.when(pl.program_id(0) == 0)
    def _():
        for copy in copies:
            copy.start()

    total = q_ref.shape[0]
    half = ROT // 2
    kt_ref[...] = k_ref[...].T
    feature = lax.broadcasted_iota(jnp.int32, (LANES, QB), 0)
    bias_q = jnp.zeros((1, LANES), f32)
    for i in range(total // QB):
        here = pl.ds(i * QB, QB)
        reach = (i + 1) * QB
        base = block_rows_of(i)
        qt = q_ref[here, :].T.astype(f32)
        gt = g_ref[here, :].T.astype(f32)
        inv = inv_ref[0, i : i + 1, :]
        less = -jnp.sum(gt[:HDIM, :] * ct_ref[0, :, here], axis=0, keepdims=True)
        less_hi = less.astype(bf16).astype(f32)
        ge = jnp.where(feature == HDIM, less_hi, gt)
        ge = jnp.where(feature == HDIM + 1, less - less_hi, ge).astype(bf16)
        gl = (gt * inv).T.astype(bf16)
        ql = jnp.where(feature < HDIM, qt * inv, 0.0).T.astype(bf16)
        for j in range(i + 1):
            at = pl.ds(j * QB, QB)
            e = e_ref[0, pl.ds(base + j * QB, QB), :]
            d = (e.astype(f32) * dot(v_ref[at, :], ge)).astype(bf16)
            d_ref[at, :] = d
            dv = dot(e, gl)
            dk = dot(d, ql)
            if j == i:
                dv_ref[at, :] = dv
                dk_ref[at, :] = dk
            else:
                dv_ref[at, :] += dv
                dk_ref[at, :] += dk
        dqt = dot(kt_ref[:, :reach], d_ref[:reach, :]) * (inv * HDIM**-0.5)
        c, s = aux_ref[:half, here], aux_ref[half:ROT, here]
        low, high = dqt[:half, :], dqt[half:ROT, :]
        dqt = jnp.concatenate(
            [low * c + high * s, high * c - low * s, dqt[ROT:HDIM, :],
             jnp.zeros((LANES - HDIM, QB), f32)], axis=0
        )
        dq = dqt.T
        bias_q += jnp.sum(dq, axis=0, keepdims=True)
        proj_ref[0, here, :HDIM] = dq[:, :HDIM].astype(bf16)
    bias_k = jnp.zeros((1, LANES), f32)
    bias_v = jnp.zeros((1, LANES), f32)
    for i in range(total // QB):
        here = pl.ds(i * QB, QB)
        cosine, up, down, _, _ = lane_tables(aux_ref[:, here])
        dk = dk_ref[here, :]
        dk = dk * cosine + pltpu.roll(dk, LANES - half, 1) * up - pltpu.roll(dk, half, 1) * down
        dv = dv_ref[here, :]
        bias_k += jnp.sum(dk, axis=0, keepdims=True)
        bias_v += jnp.sum(dv, axis=0, keepdims=True)
        proj_ref[0, here, HDIM : 2 * HDIM] = dk[:, :HDIM].astype(bf16)
        proj_ref[0, here, 2 * HDIM :] = dv[:, :HDIM].astype(bf16)
    bias_ref[0] = jnp.concatenate([bias_q, bias_k, bias_v], axis=1)
    @pl.when(pl.program_id(0) == 0)
    def _():
        for copy in copies:
            copy.wait()

    proj = proj_ref[0]
    grad = lax.dot_general(
        proj, normed_ref[...], (((0,), (0,)), ((), ())), preferred_element_type=f32
    )
    grad_ref[0, :HDIM, :] = dot(ct_ref[0].astype(bf16), c_ref[...]).astype(bf16)
    grad_ref[0, HDIM:, :] = grad.astype(bf16)
    column = lax.dot_general(
        proj, jnp.ones((total, LANES), bf16), (((0,), (0,)), ((), ())),
        preferred_element_type=f32,
    )[:, :1]
    weight = w_ref[0].astype(f32)
    shift = jnp.sum(weight * column, axis=0, keepdims=True)
    gain = jnp.sum(weight * grad, axis=0, keepdims=True) - shift * vec_ref[1:2, :]
    norm_ref[0] = jnp.concatenate([gain / vec_ref[0:1, :], shift], axis=0)


def attend_back(me, qkv, grad_ctx, kept, aux, normed, w_heads, vectors, c_all, start, at, count):
    ct, e, inv = kept
    total, width = normed.shape
    pick = lambda p: pl.BlockSpec((total, LANES), lambda h, me: (0, (h + start) * 3 + p))
    deep = lambda a: pl.BlockSpec((1,) + a.shape[1:], lambda h, me: (h + at, 0, 0))
    whole = lambda a: pl.BlockSpec(a.shape, lambda h, me: (0, 0))
    out = lambda *s: pl.BlockSpec((1,) + s, lambda h, me: (h, 0, 0))
    return pl.pallas_call(
        attend_back_kernel,
        grid_spec=pltpu.PrefetchScalarGridSpec(
            num_scalar_prefetch=1,
            grid=(count,),
            in_specs=[
                pick(0), pick(1), pick(2),
                pl.BlockSpec((total, LANES), lambda h, me: (0, h + start)),
                deep(ct), deep(inv), whole(aux), deep(e),
                pl.BlockSpec(memory_space=pl.ANY),
                pl.BlockSpec((1,) + w_heads.shape[1:], lambda h, me: (h + start, 0, 0)),
                whole(vectors),
                pl.BlockSpec(memory_space=pl.ANY),
            ],
            out_specs=[
                out(total, 3 * HDIM), out(1, 3 * LANES), out(4 * HDIM, width), out(2, width),
            ],
            scratch_shapes=[
                pltpu.VMEM((LANES, total), bf16),
                pltpu.VMEM((total, QB), bf16),
                pltpu.VMEM((total, LANES), f32),
                pltpu.VMEM((total, LANES), f32),
                pltpu.VMEM((total, width), bf16),
                pltpu.VMEM((total, width), bf16),
                pltpu.SemaphoreType.DMA((2,)),
            ],
        ),
        out_shape=[
            pltpu.HBM((count, total, 3 * HDIM), bf16),
            pltpu.HBM((count, 1, 3 * LANES), f32),
            pltpu.HBM((count, 4 * HDIM, width), bf16),
            pltpu.HBM((count, 2, width), f32),
        ],
        compiler_params=pltpu.CompilerParams(vmem_limit_bytes=VMEM),
        cost_estimate=cost(
            flops=count * e.shape[1] * 6 * 2 * QB**2,
            bytes_accessed=count * e.shape[1] * 600,
            transcendentals=0,
        ),
        name="attend_back",
    )(me, qkv, qkv, qkv, grad_ctx, ct, inv, aux, e, normed, w_heads, vectors, c_all)


def mid_kernel(n, me_ref, cta_ref, ctb_ref, y0_ref, y1_ref, wo_ref, *outs):
    step = pl.program_id(0)
    y = jnp.where(step < n // 2, y0_ref[...], y1_ref[...]).astype(f32)
    ct = jnp.concatenate([cta_ref[...], ctb_ref[...]], axis=0)
    ct = ct.reshape(wo_ref.shape[0], y.shape[0]).astype(bf16)
    y = (y + dot(ct.T, wo_ref[...])).astype(bf16)
    for j in range(n):
        @pl.when(step == j)
        def _(j=j):
            outs[j][...] = y


def near_far(n, tile, width):
    half = n // 2
    return [
        pl.BlockSpec((tile, width), lambda r, me: (jnp.minimum(r, half - 1), 0)),
        pl.BlockSpec((tile, width), lambda r, me: (jnp.maximum(r - half, 0), 0)),
    ]


def mid(me, cta, ctb, y_halves, w_out):
    n = lax.axis_size("tensor")
    total = cta.shape[2]
    tile = total // n
    wide, width = w_out.shape
    fixed = lambda *s: pl.BlockSpec(s, lambda r, me: (0, 0))
    return pl.pallas_call(
        functools.partial(mid_kernel, n),
        grid_spec=pltpu.PrefetchScalarGridSpec(
            num_scalar_prefetch=1,
            grid=(n,),
            in_specs=[
                pl.BlockSpec((a.shape[0], HDIM, tile), lambda r, me: (0, 0, r ^ me[0]))
                for a in (cta, ctb)
            ]
            + near_far(n, tile, width)
            + [fixed(wide, width)],
            out_specs=[fixed(tile, width)] * n,
        ),
        out_shape=[pltpu.HBM((tile, width), bf16)] * n,
        compiler_params=pltpu.CompilerParams(vmem_limit_bytes=VMEM),
        cost_estimate=cost(
            flops=2 * total * wide * width, bytes_accessed=total * 8000, transcendentals=0
        ),
        name="mid",
    )(me, cta, ctb, *y_halves, w_out)


def back_kernel(count, me_ref, pa_ref, pb_ref, d_ref, w_ref, vec_ref, *outs):
    step = pl.program_id(0)
    dn = None
    for h, p in enumerate([r[h] for r in (pa_ref, pb_ref) for h in range(r.shape[0])]):
        part = dot(p, w_ref[h])
        dn = part if dn is None else dn + part
    dx = (d_ref[...].astype(f32) + dn * vec_ref[0:1, :]).astype(bf16)
    for j in range(count):
        @pl.when(step == j)
        def _(j=j):
            outs[j][...] = dx


def back(me, offset, proj_a, proj_b, d, w_heads, vectors):
    tile = proj_a.shape[1] // lax.axis_size("tensor")
    rows, width = d.shape
    count = rows // tile
    fixed = lambda *s: pl.BlockSpec(s, lambda r, me: (0,) * len(s))
    rows_of = lambda a: pl.BlockSpec(
        (a.shape[0], tile, a.shape[2]), lambda r, me: (0, (r + offset) ^ me[0], 0)
    )
    return pl.pallas_call(
        functools.partial(back_kernel, count),
        grid_spec=pltpu.PrefetchScalarGridSpec(
            num_scalar_prefetch=1,
            grid=(count,),
            in_specs=[rows_of(proj_a), rows_of(proj_b)]
            + [pl.BlockSpec((tile, width), lambda r, me: (r, 0))]
            + [fixed(*w_heads.shape), fixed(*vectors.shape)],
            out_specs=[fixed(tile, width)] * count,
        ),
        out_shape=[pltpu.HBM((tile, width), bf16)] * count,
        compiler_params=pltpu.CompilerParams(vmem_limit_bytes=VMEM),
        cost_estimate=cost(
            flops=1000, bytes_accessed=1000, transcendentals=0
        ),
        name="back",
    )(me, proj_a, proj_b, d, w_heads, vectors)


def join_kernel(count, side_ref, *refs):
    step = pl.program_id(0)
    for k in range(count):
        mine, got, out = refs[2 * k], refs[2 * k + 1], refs[2 * count + k]
        out[...] = jnp.where(step == 0, mine[...], got[...]).astype(f32)


def join(sums):
    count = len(sums)
    rows, width = sums[0].last[0].shape
    sides = jnp.stack([a.last[2] for a in sums]).astype(jnp.int32)
    whole = pl.BlockSpec((rows, width), lambda r, side: (0, 0))
    return pl.pallas_call(
        functools.partial(join_kernel, count),
        grid_spec=pltpu.PrefetchScalarGridSpec(
            num_scalar_prefetch=1,
            grid=(2,),
            in_specs=[whole] * (2 * count),
            out_specs=[
                pl.BlockSpec((rows, width), lambda r, side, k=k: (r ^ side[k], 0))
                for k in range(count)
            ],
        ),
        out_shape=[jax.ShapeDtypeStruct((2 * rows, width), f32)] * count,
        compiler_params=pltpu.CompilerParams(vmem_limit_bytes=24 * 2**20),
        name="join",
    )(sides, *[a for b in sums for a in b.last[:2]])


def assemble_kernel(heads, side_ref, mine_ref, got_ref, out_ref, qkv_ref, all_ref):
    rows = mine_ref.shape[0]
    all_ref[pl.ds(pl.multiple_of(side_ref[0] * rows, 8), rows), :] = mine_ref[...].astype(f32)
    all_ref[pl.ds(pl.multiple_of((1 - side_ref[0]) * rows, 8), rows), :] = got_ref[...].astype(f32)
    tall = 4 * HDIM
    for h in range(heads):
        out_ref[h * HDIM : (h + 1) * HDIM, :] = all_ref[h * tall : h * tall + HDIM, :]
    parts = [all_ref[h * tall + HDIM : (h + 1) * tall, :] for h in range(heads)]
    qkv_ref[...] = jnp.concatenate(parts, axis=0)


def assemble(total, heads):
    mine, got, side = total.last
    rows, width = mine.shape
    whole = lambda *s: pl.BlockSpec(s, lambda r, side: (0, 0))
    return pl.pallas_call(
        functools.partial(assemble_kernel, heads),
        grid_spec=pltpu.PrefetchScalarGridSpec(
            num_scalar_prefetch=1,
            grid=(1,),
            in_specs=[whole(rows, width)] * 2,
            out_specs=[whole(heads * HDIM, width), whole(heads * 3 * HDIM, width)],
            scratch_shapes=[pltpu.VMEM((2 * rows, width), f32)],
        ),
        out_shape=[
            jax.ShapeDtypeStruct((heads * HDIM, width), f32),
            jax.ShapeDtypeStruct((heads * 3 * HDIM, width), f32),
        ],
        compiler_params=pltpu.CompilerParams(vmem_limit_bytes=24 * 2**20),
        name="assemble",
    )(side.astype(jnp.int32).reshape(1), mine, got)


def body(
    tokens,
    doc_lengths,
    w_qkv,
    b_qkv,
    w_out,
    w_up,
    b_up,
    w_down,
    out_bias,
    norm1_gain,
    norm1_shift,
    norm2_gain,
    norm2_shift,
    cotangent,
):
    row_count, width = tokens.shape
    n_tensor = lax.axis_size("tensor")
    total = row_count * n_tensor
    index = lax.axis_index("tensor")
    me = index.astype(jnp.int32).reshape(1)
    heads = w_out.shape[0] // HDIM
    slots = doc_lengths.shape[1]
    x_far = gather_far(tokens, "tensor")
    x_near = gather_near(tokens, "tensor")
    documents, positions = token_layout(doc_lengths[0], total, PADB)
    local_docs = lax.dynamic_slice_in_dim(documents, index * row_count, row_count)
    grad_send = jnp.where(local_docs[:, None] >= 0, cotangent, 0)
    c_near = gather_near(grad_send, "tensor")
    half = n_tensor // 2

    aux = aux_rows(documents, positions)
    gains = [norm1_gain, norm1_shift, norm2_gain, norm2_shift]
    vectors = jnp.stack(gains).astype(f32)
    b_up_row = b_up.astype(f32)[None]
    w_heads = w_qkv.T.reshape(heads, 3 * HDIM, width)
    b_qkv_row = b_qkv.astype(f32)[None]

    mlp_args = (w_up, w_down, w_out, vectors, b_up_row)
    w_turned = w_qkv.T
    front_args = (w_turned, b_qkv_row, vectors, aux, slots, heads)
    qkv, normed = front(me, 0, x_near, *front_args, None)
    me, grad_far, qkv, normed = tie(me, grad_send, qkv, normed)
    c_far = gather_far(grad_far, "tensor")
    y0, d0, g, c_all, gu, gd, sums = mlp(me, 0, total, x_near, c_near, *mlp_args, None)
    x_far, me, y0, d0, g, c_all, gu, gd, sums = tie(x_far, me, y0, d0, g, c_all, gu, gd, sums)
    x_far = gather_near(x_far, "tensor")
    qkv, normed = front(me, half, x_far, *front_args, [qkv, normed])
    me, qkv, normed = tie(me, qkv, normed)
    kept_a = attend(me, qkv, 0, 1)
    c_far, me, kept_a = tie(c_far, me, kept_a)
    c_far = gather_near(c_far, "tensor")
    y1, d1, g, c_all, gu, gd, sums = mlp(
        me, half, total, x_far, c_far, *mlp_args, [g, c_all, gu, gd, sums]
    )
    me, y1, d1, g, c_all, gu, gd, sums = tie(me, y1, d1, g, c_all, gu, gd, sums)
    up, down = StagedSum(gu, "dp", 0), StagedSum(gd, "dp", 1)
    up.send()
    down.send()
    kept_b = attend(me, qkv, 1, heads - 1)
    me, kept_b = boundary((me, kept_b), up, down)
    up.send()
    down.send()
    ab_args = (aux, normed, w_heads, vectors, c_all)
    pa, ba, qa, na = attend_back(me, qkv, g, kept_a, *ab_args, 0, 0, 1)
    me, pa, ba, qa, na = boundary((me, pa, ba, qa, na), up, down)
    up.send()
    down.send()
    pb, bb, qb, nb = attend_back(me, qkv, g, kept_b, *ab_args, 1, 0, heads - 1)
    me, pb, bb, qb, nb, grad_rows = boundary((me, pb, bb, qb, nb, grad_send), up, down)
    up.send()
    down.send()
    rows = jnp.concatenate([qa, qb], axis=0).reshape(heads * 4 * HDIM, width)
    attn = StagedSum(rows, "dp", 0)
    attn.send()
    grad_rows = grad_rows.astype(f32)
    vec = jnp.concatenate(
        [
            jnp.sum(grad_rows, axis=0)[None],
            jnp.sum(na, axis=0) + jnp.sum(nb, axis=0),
            sums[1:3],
        ],
        axis=0,
    )
    vec = SmallSum(vec, "tensor")
    vec.send()
    y_blocks = mid(me, kept_a[0], kept_b[0], [y0, y1], w_out)
    me, y_blocks = tie(me, y_blocks)
    y_rows = ScatterSum(dict(enumerate(y_blocks)), "tensor")
    y_rows.send()
    far_blocks = back(me, half, pa, pb, d1, w_heads, vectors)
    me, far_blocks = boundary((me, far_blocks), up, down, attn, vec, y_rows)
    far_rows = ScatterSum(dict(enumerate(far_blocks)), "tensor")
    far_rows.send()
    vec.send()
    attn.send()
    down.send()
    me = boundary(me, far_rows)
    far_rows.finish(half)
    cross = Exchange(far_rows.blocks[0].astype(bf16), "tensor", half)
    near_blocks = back(me, 0, pa, pb, d0, w_heads, vectors)
    tok, near_blocks = boundary((me, near_blocks), attn, vec)
    near_rows = ScatterSum(dict(enumerate(near_blocks)), "tensor")
    near_rows.send()
    attn.send()
    up.send()
    vec.finish()
    share = width // n_tensor
    vec = lax.dynamic_slice_in_dim(vec.out, index * share, share, 1)
    bias = jnp.concatenate([ba, bb]).reshape(heads, 3, LANES)[:, :, :HDIM].reshape(-1)
    small = SmallSum(jnp.concatenate([bias, sums[0], vec.reshape(-1)]), "dp")
    small.send()
    tok = boundary(tok, attn, up, small, near_rows)
    near_rows.finish(half)
    attn.send()
    up.send()
    small.send()
    tok = boundary(tok, attn, down, small)
    attn.send()
    small.send()
    tok, cross_in = boundary((tok, near_rows.blocks[0]), cross)
    y_rows.send()
    dx = cross_in.astype(f32) + cross.out.astype(f32)
    inputs = tokens.astype(f32)
    xhat, inv = normalize(inputs)
    grad_input = grad_rows + inv * (
        dx
        - jnp.mean(dx, axis=-1, keepdims=True)
        - xhat * jnp.mean(dx * xhat, axis=-1, keepdims=True)
    )
    tok, grad_input = boundary((tok, grad_input), attn, up, small)
    attn.send()
    down.send()
    tok = boundary(tok, y_rows)
    block_out = inputs + out_bias.astype(f32) + y_rows.blocks[0].astype(f32)
    block_out = block_out.astype(bf16)
    tok, block_out = boundary((tok, block_out), down)
    up.finish()
    down.finish()
    up_sum, down_sum = join([up, down])
    tok, up_sum, down_sum = boundary((tok, up_sum, down_sum), attn)
    attn.finish()
    small.finish()
    small = small.out
    out_sum, qkv_sum = assemble(attn, heads)
    nq, nu = bias.shape[0], b_up.shape[0]
    return (
        block_out,
        grad_input,
        qkv_sum.T,
        small[:nq],
        out_sum,
        up_sum,
        small[nq : nq + nu],
        down_sum,
        small[nq + nu :].reshape(5, share),
    )


def solution(mesh):
    placed = (
        P(("dp", "tensor"), None),
        P("dp", None),
        P(None, "tensor"),
        P("tensor"),
        P("tensor", None),
        P(None, "tensor"),
        P("tensor"),
        P("tensor", None),
        P(),
        P(),
        P(),
        P(),
        P(),
        P(("dp", "tensor"), None),
    )
    return jax.shard_map(
        body,
        mesh=mesh,
        in_specs=placed,
        out_specs=(
            P(("dp", "tensor"), None),
            P(("dp", "tensor"), None),
            P(None, "tensor"),
            P("tensor"),
            P("tensor", None),
            P(None, "tensor"),
            P("tensor"),
            P("tensor", None),
            P(None, "tensor"),
        ),
        check_vma=False,
    )
```
